32 devices in a mesh: section: 2 (over core), tensor: 4 (over y, x), seq: 4 (over z).
Axes of the slice: x: 2, y: 2, z: 4, core: 2. Of those that a mesh axis runs over, the one named last changes fastest.
Arguments:
- byte_ids: int32 [2, 2048], P(None, 'seq'), may hold values from 0 to 255
- byte_lengths: int32 [2], replicated, may hold values from 1024 to 2048, as said below
- embedding: bfloat16 [256, 768], replicated, may hold values from -6 to 6
- conv_weight: bfloat16 [5, 768], replicated, may hold values from -2.5 to 2.5
- conv_bias: bfloat16 [768], replicated, may hold values from -2.5 to 2.5
- score_weight: bfloat16 [768], replicated, may hold values from -0.4375 to 0.4375
- norm_first: bfloat16 [768], replicated, may hold values from 0.5 to 1.5
- query_weight: bfloat16 [768, 768], P(None, 'tensor'), may hold values from -0.109375 to 0.109375
- key_weight: bfloat16 [768, 768], P(None, 'tensor'), may hold values from -0.109375 to 0.109375
- value_weight: bfloat16 [768, 768], P(None, 'tensor'), may hold values from -0.21875 to 0.21875
- out_weight: bfloat16 [768, 768], P('tensor'), may hold values from -0.875 to 0.875
- rel_bias: bfloat16 [32, 12], P(None, 'tensor'), may hold values from -4 to 4
- norm_second: bfloat16 [768], replicated, may hold values from 0.5 to 1.5
- gate_weight: bfloat16 [768, 2048], P(None, 'tensor'), may hold values from -0.21875 to 0.21875
- up_weight: bfloat16 [768, 2048], P(None, 'tensor'), may hold values from -0.21875 to 0.21875
- down_weight: bfloat16 [2048, 768], P('tensor'), may hold values from -0.1875 to 0.1875
- out_grad: bfloat16 [2, 1024, 768], P(None, 'seq'), may hold values from -6 to 6
Outputs:
- encoded: bfloat16 [2, 1024, 768], P('section', 'seq')
- grad_embedding: float32 [256, 768], replicated
- grad_conv_weight: float32 [5, 768], replicated
- grad_conv_bias: float32 [768], replicated
- grad_score_weight: float32 [768], replicated
- grad_norm_first: float32 [768], replicated
- grad_query_weight: float32 [768, 768], P(None, 'tensor')
- grad_key_weight: float32 [768, 768], P(None, 'tensor')
- grad_value_weight: float32 [768, 768], P(None, 'tensor')
- grad_out_weight: float32 [768, 768], P('tensor')
- grad_rel_bias: float32 [32, 12], P(None, 'tensor')
- grad_norm_second: float32 [768], replicated
- grad_gate_weight: float32 [768, 2048], P(None, 'tensor')
- grad_up_weight: float32 [768, 2048], P(None, 'tensor')
- grad_down_weight: float32 [2048, 768], P('tensor')
The draws below stay inside these ranges and needn't reach their ends.
Inputs may be any that keep to these rules, and one draw needn't show every extreme that they name: `byte_lengths`: one micro-batch's sequence, drawn from the seed, has all 2048 bytes in use; the others use at least half.
All inputs are finite; a program needn't handle non-finite values.
Results may differ from the reference program's by a relative error of at most 0.022.
Values may be sent and summed in bfloat16 or wider, within the bound.
No kernel may reach another device: no remote copies, remote signals or barrier semaphores. Data moves between devices by JAX's collectives and lax.ppermute only.
A program may use at most 192 MiB of HBM per device.

```python
import math
import jax
import jax.numpy as jnp
from jax import lax

D = 768
HEADS = 12
HEAD = 64
FF = 2048
BYTE_VALUES = 256
BUCKETS = 32
WIDTH = 5
MICRO = 2
SEQ_BYTES = 2048
SEQ_TOK = 1024


def draw_byte_lengths(key, part):
    key = jax.random.fold_in(key, 11)
    length_key, pick_key = jax.random.split(key)
    lengths = jax.random.randint(length_key, (MICRO,), SEQ_BYTES // 2, SEQ_BYTES + 1)
    chosen = jax.random.randint(pick_key, (), 0, MICRO)
    return jnp.where(jnp.arange(MICRO) == chosen, SEQ_BYTES, lengths).astype(jnp.int32)


def with_ends(result, rng, smallest, high):
    longest = result.shape.index(max(result.shape))
    spots = []
    for shift in (0, 1):
        where = [jax.random.randint(jax.random.fold_in(rng, axis), (), 0, length) for axis, length in enumerate(result.shape)]
        where[longest] = (where[longest] + shift) % result.shape[longest]
        spots.append(tuple(where))
    return result.at[spots[0]].set(smallest).at[spots[1]].set(high)


def steps_of(stream_key, dims, pieces, low, largest):
    def one(axis_at, blocks):
        draws = jax.random.uniform(jax.random.fold_in(jax.random.fold_in(stream_key, 6), axis_at), (blocks,), jnp.float32, low / len(pieces), largest / len(pieces))
        return jnp.repeat(jnp.exp(draws), dims[axis_at] // blocks).reshape((-1,) + (1,) * (len(dims) - axis_at - 1))

    factor_of = one(*pieces[0])
    for cut in pieces[1:]:
        factor_of = factor_of * one(*cut)
    return factor_of


def scatter_about(stream_key, shape, width, bound, shards=(), kind=jnp.bfloat16):
    gain = steps_of(stream_key, shape, shards, -0.22, 0.18) if shards else 1.0
    array = jax.random.normal(stream_key, shape, jnp.float32) * width * gain
    return jnp.minimum(jnp.maximum(array, -bound), bound).astype(kind)


def setup_inputs(seed: int = 0) -> dict:
    splits = jax.random.split(jax.random.key(seed), 18)
    return {
        "byte_ids": with_ends(jax.random.randint(splits[0], (MICRO, SEQ_BYTES), 0, BYTE_VALUES), jax.random.fold_in(splits[0], 1), 0, BYTE_VALUES - 1).astype(jnp.int32),
        "byte_lengths": draw_byte_lengths(jax.random.fold_in(splits[17], 71), 0),
        "embedding": scatter_about(splits[2], (BYTE_VALUES, D), 1.0, 6.0),
        "conv_weight": scatter_about(splits[3], (WIDTH, D), WIDTH ** -0.5, 2.5),
        "conv_bias": scatter_about(splits[4], (D,), 0.3, 2.5),
        "score_weight": scatter_about(splits[5], (D,), (D // 4) ** -0.5, 0.4375),
        "norm_first": jnp.clip(1.0 + 0.1 * jax.random.normal(splits[6], (D,), jnp.float32), 0.5, 1.5).astype(jnp.bfloat16),
        "query_weight": scatter_about(splits[7], (D, HEADS * HEAD), (4 * D) ** -0.5, 0.109375, ((1, 4),)),
        "key_weight": scatter_about(splits[8], (D, HEADS * HEAD), (4 * D) ** -0.5, 0.109375, ((1, 4),)),
        "value_weight": scatter_about(splits[9], (D, HEADS * HEAD), D ** -0.5, 0.21875, ((1, 4),)),
        "out_weight": scatter_about(splits[10], (HEADS * HEAD, D), (HEADS * HEAD // 16) ** -0.5, 0.875, ((0, 4),)),
        "rel_bias": scatter_about(splits[11], (BUCKETS, HEADS), 1.0, 4.0, ((1, 4),)),
        "norm_second": jnp.clip(1.0 + 0.1 * jax.random.normal(splits[12], (D,), jnp.float32), 0.5, 1.5).astype(jnp.bfloat16),
        "gate_weight": scatter_about(splits[13], (D, FF), D ** -0.5, 0.21875, ((1, 4),)),
        "up_weight": scatter_about(splits[14], (D, FF), D ** -0.5, 0.21875, ((1, 4),)),
        "down_weight": scatter_about(splits[15], (FF, D), (FF // 2) ** -0.5, 0.1875, ((0, 4),)),
        "out_grad": scatter_about(splits[16], (MICRO, SEQ_TOK, D), 1.0, 6.0, ((1, 4),)),
    }


epsilon = 1e-06
masked_score = -1e+30
highest = lax.Precision.HIGHEST
far_thresholds = (12, 16, 23, 32, 46, 64, 91)

@jax.custom_vjp
def low(v):
    return lax.optimization_barrier(v.astype(jnp.bfloat16)).astype(jnp.float32)

@jax.custom_vjp
def low_back(v):
    return v

def low_keep(v):
    return (low(v), None)

def low_pass(kept, grad):
    return (grad,)

def back_keep(v):
    return (v, None)

def back_low(kept, grad):
    return (low(grad),)
low.defvjp(low_keep, low_pass)
low_back.defvjp(back_keep, back_low)

def bucket_of(relative):
    distance = jnp.abs(relative)
    far_bucket = 8 + sum(((distance >= threshold).astype(jnp.int32) for threshold in far_thresholds))
    return jnp.where(distance < 8, distance, far_bucket) + 16 * (relative > 0).astype(jnp.int32)

def normalize(values):
    return values * lax.rsqrt(lax.optimization_barrier(jnp.mean(values * values, axis=-1, keepdims=True)) + epsilon)

def gbst_sequence(weights, byte_row, length):
    embedding, conv_weight, conv_bias, score_weight = weights
    count = byte_row.shape[0]
    positions = jnp.arange(count, dtype=jnp.int32)
    present = (positions < length).astype(jnp.float32)
    embedded = embedding[byte_row] * present[:, None]
    padded = jnp.pad(embedded, ((2, 2), (0, 0)))
    conv = conv_bias + sum((conv_weight[tap] * padded[tap:tap + count] for tap in range(conv_weight.shape[0])))
    extra = -count % 12
    conv_pad = jnp.pad(conv, ((0, extra), (0, 0)))
    pooled = []
    for size in range(1, 5):
        means = conv_pad.reshape(-1, size, conv.shape[1]).mean(axis=1)
        pooled.append(jnp.repeat(means, size, axis=0)[:count])
    stacked = jnp.stack(pooled)
    scores = jnp.einsum('bnd,d->bn', stacked, score_weight, precision=highest)
    size_weights = jax.nn.softmax(scores, axis=0)
    mixed = lax.optimization_barrier(jnp.sum(size_weights[:, :, None] * stacked, axis=0))
    return mixed.reshape(count // 2, 2, -1).mean(axis=1)

def t5_sequence(weights, hidden, length):
    norm_first, query_weight, key_weight, value_weight, out_weight, rel_bias, norm_second, gate_weight, up_weight, down_weight = weights
    seq_tokens = hidden.shape[0]
    heads = rel_bias.shape[1]
    head_dim = query_weight.shape[1] // heads
    normed = low(normalize(hidden) * norm_first)
    queries = low(low_back(jnp.dot(normed, query_weight, precision=highest)))
    keys = low(low_back(jnp.dot(normed, key_weight, precision=highest)))
    values = low(low_back(jnp.dot(normed, value_weight, precision=highest)))
    query_heads = queries.reshape(seq_tokens, heads, head_dim)
    key_heads = keys.reshape(seq_tokens, heads, head_dim)
    value_heads = values.reshape(seq_tokens, heads, head_dim)
    key_positions = jnp.arange(seq_tokens, dtype=jnp.int32)
    key_live = 2 * key_positions < length
    block = math.gcd(seq_tokens, 512)

    def attend(start):
        query_block = lax.dynamic_slice_in_dim(query_heads, start, block, 0)
        query_positions = start + jnp.arange(block, dtype=jnp.int32)
        scores = jnp.einsum('qhd,khd->hqk', query_block, key_heads, precision=highest)
        buckets = bucket_of(key_positions[None, :] - query_positions[:, None])
        scores = scores + jnp.transpose(rel_bias[buckets], (2, 0, 1))
        scores = low_back(scores)
        scores = jnp.where(key_live[None, None, :], scores, masked_score)
        probs = jnp.exp(scores - jax.nn.logsumexp(scores, axis=-1, keepdims=True))
        return jnp.einsum('hqk,khd->qhd', low(probs), value_heads, precision=highest)
    starts = jnp.arange(0, seq_tokens, block, dtype=jnp.int32)
    attended = lax.map(jax.checkpoint(attend), starts).reshape(seq_tokens, heads * head_dim)
    attended = low(low_back(attended))
    middle = hidden + low_back(jnp.dot(attended, out_weight, precision=highest))
    normed_two = low(normalize(middle) * norm_second)
    gate = low_back(jnp.dot(normed_two, gate_weight, precision=highest))
    upward = low_back(jnp.dot(normed_two, up_weight, precision=highest))
    inner = low(jax.nn.gelu(gate, approximate=True) * upward)
    return middle + low_back(jnp.dot(inner, down_weight, precision=highest))

def forward(weights, byte_ids, byte_lengths):
    gbst_weights = weights[:4]
    t5_weights = weights[4:]
    outputs = []
    for micro in range(byte_ids.shape[0]):
        tokens = low(low_back(gbst_sequence(gbst_weights, byte_ids[micro], byte_lengths[micro])))
        outputs.append(t5_sequence(t5_weights, tokens, byte_lengths[micro]))
    return jnp.stack(outputs)

def reference(byte_ids, byte_lengths, embedding, conv_weight, conv_bias, score_weight, norm_first, query_weight, key_weight, value_weight, out_weight, rel_bias, norm_second, gate_weight, up_weight, down_weight, out_grad):
    weights = tuple((item.astype(jnp.float32) for item in (embedding, conv_weight, conv_bias, score_weight, norm_first, query_weight, key_weight, value_weight, out_weight, rel_bias, norm_second, gate_weight, up_weight, down_weight)))
    encoded, pullback = jax.vjp(lambda values: forward(values, byte_ids, byte_lengths), weights)
    grads = pullback(out_grad.astype(jnp.float32))[0]
    return (encoded.astype(jnp.bfloat16), grads[0], grads[1], grads[2], grads[3], grads[4], grads[5], grads[6], grads[7], grads[8], grads[9], grads[10], grads[11], grads[12], grads[13])
```

```python
import functools

import jax
import jax.numpy as jnp
import numpy as np
from jax import lax
from jax.experimental import pallas as pl
from jax.experimental.pallas import tpu as pltpu
from jax.sharding import PartitionSpec as P

epsilon = 1e-06
masked_score = -1e30
far_thresholds = (12, 16, 23, 32, 46, 64, 91)
period = 12
pairs = period // 2
taps = 5
columns = period + taps - 1
chunk_rows = 176
vmem_limit = 56 * 2**20
f32 = jnp.float32
bf16 = jnp.bfloat16
whole = pl.BlockSpec(memory_space=pltpu.VMEM)
scalars = pl.BlockSpec(memory_space=pltpu.SMEM)


def pool_tables():
    pool = np.zeros((3, 128, 128), np.float32)
    spread = np.zeros((4, 128, 128), np.float32)
    total = np.zeros((128, 128), np.float32)
    for size in range(1, 5):
        for g in range(period):
            for r in range(period):
                if r // size == g // size:
                    if size > 1:
                        pool[size - 2, 4 + r, 4 + g] = 1.0 / size
                    spread[size - 1, 4 + g, period * (g // 2) + r] = 0.5 / size
    for j in range(pairs):
        total[period * j : period * (j + 1), j] = 1.0
    return (pool, spread, total)


def reached(j):
    found = set()
    for g in (2 * j, 2 * j + 1):
        for size in range(1, 5):
            first = size * (g // size)
            found.update(range(first, first + size))
    return sorted(found)


def exact(a, b, dims=((1,), (0,))):
    return lax.dot_general(
        a, b, (dims, ((), ())), precision=lax.Precision.HIGHEST, preferred_element_type=f32
    )


def mm(a, b, dims=((1,), (0,))):
    return lax.dot_general(a, b, (dims, ((), ())), preferred_element_type=f32)


rows_rows = ((0,), (0,))
cols_cols = ((1,), (1,))


def call(kernel, out, *args, specs=None, scratch=(), grid=None, out_specs=None, limit=vmem_limit):
    extra = {} if grid is None else {"grid": grid}
    return pl.pallas_call(
        kernel,
        out_shape=out,
        in_specs=[whole] * len(args) if specs is None else specs,
        out_specs=jax.tree.map(lambda _: whole, out) if out_specs is None else out_specs,
        scratch_shapes=list(scratch),
        compiler_params=pltpu.CompilerParams(vmem_limit_bytes=limit),
        **extra,
    )(*args)


def like(shape, kind):
    return jax.ShapeDtypeStruct(shape, kind)


def iota(shape, dim):
    return lax.broadcasted_iota(jnp.int32, shape, dim)


def bucket_of(relative):
    distance = jnp.abs(relative)
    far_bucket = 8 + sum(
        ((distance >= threshold).astype(jnp.int32) for threshold in far_thresholds)
    )
    return jnp.where(distance < 8, distance, far_bucket) + 16 * (relative > 0).astype(jnp.int32)


def bucket_hot(buckets, width, query_first, queries):
    offsets = iota((buckets, width), 1) - (queries - 1) - query_first
    return (bucket_of(offsets) == iota((buckets, width), 0)).astype(f32)


def one_hot(ids, vocab):
    return jnp.where(ids == iota((ids.shape[0], vocab), 1), 1.0, 0.0).astype(bf16)


def head_mask(width, head_dim, head):
    return iota((1, width), 1) // head_dim == head


def prepare_kernel(embedding, conv_weight, score_weight, conv_bias, table, score_table, bias_score):
    vocab = embedding.shape[0]
    emb = embedding[...].astype(f32)
    conv = conv_weight[...].astype(f32)
    score = score_weight[...].astype(f32)
    for tap in range(taps):
        table[tap * vocab : (tap + 1) * vocab, :] = (emb * conv[tap : tap + 1]).astype(bf16)
    scored = jnp.concatenate(
        [conv[tap : tap + 1] * score for tap in reversed(range(taps))]
        + [jnp.zeros((128 - taps, conv.shape[1]), f32)],
        axis=0,
    )
    by_byte = exact(emb, scored, cols_cols)
    high = by_byte.astype(bf16).astype(f32)
    middle = (by_byte - high).astype(bf16).astype(f32)
    low = by_byte - high - middle
    score_table[...] = (high + pltpu.roll(middle, 32, 1) + pltpu.roll(low, 64, 1)).astype(bf16)
    bias_score[...] = jnp.broadcast_to(
        jnp.sum(conv_bias[...].astype(f32) * score, axis=1, keepdims=True), bias_score.shape
    )


def position_inside(rows, first, total_bytes):
    lane = iota((rows, 128), 1)
    place = period * (first + iota((rows, 128), 0)) + lane - 4
    return (lane >= 4) & (lane < 4 + period) & (place < total_bytes)


def coefficient_inside(rows, first, total_bytes):
    lane = iota((rows, 128), 1)
    place = period * (first + iota((rows, 128), 0)) + lax.rem(lane, period)
    return (lane < period * pairs) & (place < total_bytes)


def gbst_kernel(
    total_bytes,
    ids,
    table,
    score_table,
    pool,
    spread,
    total,
    conv_bias,
    bias_score,
    tokens,
    mixing,
    coefficients,
    size_weights,
    hot,
    natural,
):
    rows = ids.shape[0]
    vocab = score_table.shape[0]
    width = table.shape[1]
    first = pl.program_id(0) * rows
    scores = jnp.zeros((rows, 128), f32)
    for r in range(columns):
        found = one_hot(ids[:, r : r + 1], vocab)
        hot[:, r * vocab : (r + 1) * vocab] = found
        part = mm(found, score_table[...])
        scores = scores + (pltpu.roll(part, r, 1) if r else part)
    scores = scores + pltpu.roll(scores, 96, 1) + pltpu.roll(scores, 64, 1)
    scores = jnp.where(
        position_inside(rows, first, total_bytes), scores + bias_score[0:1, :], 0.0
    )
    by_size = [scores] + [exact(scores, pool[size]) for size in range(3)]
    largest = functools.reduce(jnp.maximum, by_size)
    weights = [jnp.exp(item - largest) for item in by_size]
    scale = 1.0 / sum(weights)
    spread_sum = jnp.zeros((rows, 128), f32)
    for size in range(4):
        weight = weights[size] * scale
        size_weights[size] = weight
        spread_sum = spread_sum + exact(weight, spread[size])
    spread_sum = jnp.where(coefficient_inside(rows, first, total_bytes), spread_sum, 0.0)
    coefficients[...] = spread_sum
    row_total = exact(spread_sum, total[...])
    narrow = spread_sum.astype(bf16)
    bias = conv_bias[...].astype(f32)
    for j in range(pairs):
        for tap in range(taps):
            acc = None
            for r in reached(j):
                at = (r + tap) * vocab
                term = hot[:, at : at + vocab] * narrow[:, period * j + r : period * j + r + 1]
                acc = term if acc is None else acc + term
            mixing[j, :, tap * vocab : (tap + 1) * vocab] = acc
        rows_j = mm(mixing[j], table[...]) + row_total[:, j : j + 1] * bias
        for at in range(width // 128):
            natural[at, pl.ds(j, rows, stride=pairs), :] = rows_j[:, at * 128 : (at + 1) * 128]
    for at in range(width // 128):
        tokens[:, at * 128 : (at + 1) * 128] = natural[at].astype(bf16)


def attend_kernel(
    heads,
    info,
    tokens,
    gain,
    query_weight,
    key_weight,
    value_weight,
    rel_bias,
    normed,
    queries,
    keys,
    values,
    probs,
    attended,
):
    seq_tokens = normed.shape[0]
    count, width = queries.shape
    head_dim = width // heads
    query_first = pl.multiple_of(info[2] * count, count)
    live_tokens = info[3]
    hidden = tokens[0:seq_tokens, :].astype(f32)
    scale = lax.rsqrt(jnp.mean(hidden * hidden, axis=-1, keepdims=True) + epsilon)
    normed[...] = (hidden * scale * gain[...].astype(f32)).astype(bf16)
    keys[...] = mm(normed[...], key_weight[...]).astype(bf16)
    values[...] = mm(normed[...], value_weight[...]).astype(bf16)
    queries[...] = mm(normed[pl.ds(query_first, count), :], query_weight[...]).astype(bf16)
    span = seq_tokens + count
    hot = bucket_hot(rel_bias.shape[0], span, query_first, count)
    by_offset = mm(rel_bias[...].astype(f32), hot, rows_rows)
    live = 2 * iota((1, seq_tokens), 1) < live_tokens
    mixed = jnp.zeros((count, width), f32)
    for head in range(heads):
        mask = head_mask(width, head_dim, head)
        row = jnp.broadcast_to(by_offset[head : head + 1, :], (count, span))
        bias = pltpu.roll(row, span - (count - 1), 1, stride=1, stride_axis=0)[:, :seq_tokens]
        own = jnp.where(mask, queries[...], jnp.zeros((), bf16))
        scores = mm(own, keys[...], cols_cols) + bias
        scores = jnp.where(live, scores, masked_score)
        raised = jnp.exp(scores - jnp.max(scores, axis=-1, keepdims=True))
        part = (raised * (1.0 / jnp.sum(raised, axis=-1, keepdims=True))).astype(bf16)
        probs[head] = part
        mixed = jnp.where(mask, mm(part, values[...]), mixed)
    attended[...] = mixed.astype(bf16)


def gelu(value):
    inner = np.float32(np.sqrt(2 / np.pi)) * (value + 0.044715 * (value * value * value))
    return 0.5 * value * (1.0 + jnp.tanh(inner))


def gelu_both(value):
    root = np.float32(np.sqrt(2 / np.pi))
    square = value * value
    tanh = jnp.tanh(root * value * (1.0 + 0.044715 * square))
    half = 0.5 * (1.0 + tanh)
    slope = half + 0.5 * value * (1.0 - tanh * tanh) * root * (1.0 + 3 * 0.044715 * square)
    return (value * half, slope)


def feed_kernel(ways, info, *refs):
    attended = refs[:ways]
    out_weight = refs[ways : 2 * ways]
    tokens, gain, gate_weight, up_weight, down_weight, out_grad = refs[2 * ways : 2 * ways + 6]
    middle, normed, inner, grad_gate, grad_up = refs[2 * ways + 6 : 2 * ways + 11]
    pieces = refs[2 * ways + 11 : 3 * ways + 11]
    whole_part = refs[3 * ways + 11]
    count = middle.shape[0]
    first = pl.multiple_of(info[2] * count, count)
    branch = sum(mm(a[...], w[...]) for a, w in zip(attended, out_weight))
    total = tokens[pl.ds(first, count), :].astype(f32) + branch
    middle[...] = total
    scale = lax.rsqrt(jnp.mean(total * total, axis=-1, keepdims=True) + epsilon)
    normed[...] = (total * scale * gain[...].astype(f32)).astype(bf16)
    gate = mm(normed[...], gate_weight[...])
    upward = mm(normed[...], up_weight[...])
    grad_inner = mm(out_grad[...], down_weight[...], cols_cols)
    active, slope = gelu_both(gate)
    inner[...] = (active * upward).astype(bf16)
    grad_gate[...] = (grad_inner * upward * slope).astype(bf16)
    grad_up[...] = (grad_inner * active).astype(bf16)
    whole_part[...] = mm(grad_gate[...], gate_weight[...], cols_cols) + mm(
        grad_up[...], up_weight[...], cols_cols
    )
    piece = count // ways
    for k in range(ways):
        at = pl.multiple_of((info[1] ^ k) * piece, piece)
        pieces[k][...] = whole_part[pl.ds(at, piece), :].astype(bf16)


def feed_grad_kernel(
    inner, normed, grad_gate, grad_up, out_grad, down_weight, encoded, down, gate, up
):
    encoded[...] = mm(inner[...], down_weight[...]).astype(bf16)
    down[...] = mm(inner[...], out_grad[...], rows_rows).astype(bf16)
    gate[...] = mm(normed[...], grad_gate[...], rows_rows).astype(bf16)
    up[...] = mm(normed[...], grad_up[...], rows_rows).astype(bf16)


def middle_kernel(ways, info, *refs):
    pieces = refs[:ways]
    middle, out_grad, gain, grad_branch, grad_middle, grad_gain = refs[ways:]
    piece = pieces[0].shape[0]
    at = pl.multiple_of(info[1] * piece, piece)
    grad_normed = sum(item[...].astype(f32) for item in pieces)
    own = middle[pl.ds(at, piece), :]
    scale = lax.rsqrt(jnp.mean(own * own, axis=-1, keepdims=True) + epsilon)
    grad_gain[...] = jnp.sum(grad_normed * own * scale, axis=0, keepdims=True)
    through = grad_normed * gain[...].astype(f32)
    total = (
        out_grad[pl.ds(at, piece), :].astype(f32)
        + scale * through
        - own * (scale * scale * scale) * jnp.mean(through * own, axis=-1, keepdims=True)
    )
    grad_middle[...] = total
    grad_branch[...] = total.astype(bf16)


def attend_back_kernel(heads, ways, info, *refs):
    branches = refs[:ways]
    attended, probs, queries, keys, values, normed, out_weight, rel_bias = refs[ways : ways + 8]
    out_grad, query_grad, key_grad, value_grad, rel_grad = refs[ways + 8 : ways + 13]
    grad_queries, grad_keys, grad_values, branch = refs[ways + 13 :]
    count, width = queries.shape
    seq_tokens = keys.shape[0]
    head_dim = width // heads
    piece = branches[0].shape[0]
    for k in range(ways):
        at = pl.multiple_of((info[1] ^ k) * piece, piece)
        branch[pl.ds(at, piece), :] = branches[k][...]
    query_first = pl.multiple_of(info[2] * count, count)
    grad_attended = mm(branch[...], out_weight[...], cols_cols).astype(bf16)
    out_grad[...] = mm(attended[...], branch[...], rows_rows).astype(bf16)
    span = seq_tokens + count
    flip = (iota((count, count), 0) + iota((count, count), 1) == count - 1).astype(bf16)
    zero = jnp.zeros((), bf16)
    by_offset = []
    query_sum = jnp.zeros((count, width), f32)
    key_sum = jnp.zeros((seq_tokens, width), f32)
    value_sum = jnp.zeros((seq_tokens, width), f32)
    for head in range(heads):
        mask = head_mask(width, head_dim, head)
        own = jnp.where(mask, grad_attended, zero)
        grad_probs = mm(own, values[...], cols_cols)
        part = probs[head].astype(f32)
        inside = jnp.sum(part * grad_probs, axis=-1, keepdims=True)
        grad_scores = (part * (grad_probs - inside)).astype(bf16)
        flipped = jnp.concatenate(
            [mm(flip, grad_scores), jnp.zeros((count, count), f32)], axis=1
        )
        by_offset.append(
            jnp.sum(pltpu.roll(flipped, 0, 1, stride=1, stride_axis=0), axis=0, keepdims=True)
        )
        query_sum = jnp.where(mask, mm(grad_scores, keys[...]), query_sum)
        key_sum = key_sum + mm(
            grad_scores, jnp.where(mask, queries[...], zero), rows_rows
        )
        value_sum = value_sum + mm(probs[head], own, rows_rows)
    by_offset = jnp.concatenate(by_offset + [jnp.zeros((8 - heads, span), f32)], axis=0)
    hot = bucket_hot(rel_bias.shape[0], span, query_first, count)
    rel_grad[...] = exact(hot, by_offset, cols_cols)
    query_sum = query_sum.astype(bf16)
    query_grad[...] = mm(normed[pl.ds(query_first, count), :], query_sum, rows_rows).astype(bf16)
    grad_queries[...] = jnp.zeros(grad_queries.shape, bf16)
    grad_queries[pl.ds(query_first, count), :] = query_sum
    rest = grad_keys.shape[0] - seq_tokens
    for total, place, weight_grad in (
        (key_sum, grad_keys, key_grad),
        (value_sum, grad_values, value_grad),
    ):
        total = total.astype(bf16)
        place[0:seq_tokens, :] = total
        place[seq_tokens:, :] = jnp.zeros((rest, width), bf16)
        weight_grad[...] = mm(normed[...], total, rows_rows).astype(bf16)


def gbst_back_kernel(
    total_bytes,
    seq_tokens,
    info,
    grad_queries,
    grad_keys,
    grad_values,
    tokens,
    query_weight,
    key_weight,
    value_weight,
    gain,
    grad_middle,
    grad_gain_second,
    table,
    mixing,
    coefficients,
    size_weights,
    ids,
    pool,
    spread,
    total,
    embedding,
    conv_weight,
    conv_bias,
    score_weight,
    packed,
    natural,
    hot,
    by_byte,
    by_score,
    small,
    normed_grad,
):
    rows = ids.shape[0]
    token_rows = rows * pairs
    vocab, width = embedding.shape
    step = pl.program_id(0)
    first = step * rows
    score = score_weight[...].astype(f32)
    bias = conv_bias[...].astype(f32)

    @pl.when(step == 0)
    def _():
        by_byte[...] = jnp.zeros(by_byte.shape, f32)
        by_score[...] = jnp.zeros(by_score.shape, f32)
        small[...] = jnp.zeros(small.shape, f32)

    grad_normed = (
        mm(grad_queries[...], query_weight[...], cols_cols)
        + mm(grad_keys[...], key_weight[...], cols_cols)
        + mm(grad_values[...], value_weight[...], cols_cols)
    )
    present = token_rows * step + iota((token_rows, 1), 0) < seq_tokens
    hidden = jnp.where(present, tokens[...].astype(f32), 0.0)
    scale = lax.rsqrt(jnp.mean(hidden * hidden, axis=-1, keepdims=True) + epsilon)
    small[0:1, :] += jnp.sum(grad_normed * hidden * scale, axis=0, keepdims=True)
    through = grad_normed * gain[...].astype(f32)
    normed_grad[...] = scale * through - hidden * (scale * scale * scale) * jnp.mean(
        through * hidden, axis=-1, keepdims=True
    )
    piece = grad_middle.shape[0]
    own_first = (info[2] * lax.axis_size("tensor") + info[1]) * piece - token_rows * step
    block = int(np.gcd(piece, token_rows))
    for part in range(piece // block):
        at = own_first + part * block

        @pl.when((at >= 0) & (at < token_rows))
        def _():
            place = pl.ds(pl.multiple_of(at, block), block)
            normed_grad[place, :] += grad_middle[part * block : (part + 1) * block, :]

    for at in range(width // 128):
        natural[at] = normed_grad[:, at * 128 : (at + 1) * 128]
    for r in range(columns):
        hot[:, r * vocab : (r + 1) * vocab] = one_hot(ids[:, r : r + 1], vocab)
    row_total = exact(coefficients[...], total[...])
    lane = iota((rows, 128), 1)
    grad_coefficients = jnp.zeros((rows, 128), f32)
    bias_grad = jnp.zeros((1, width), f32)
    for j in range(pairs):
        grad_rows = jnp.concatenate(
            [natural[at, pl.ds(j, rows, stride=pairs), :] for at in range(width // 128)], axis=1
        )
        bias_grad = bias_grad + jnp.sum(row_total[:, j : j + 1] * grad_rows, axis=0, keepdims=True)
        on_bias = jnp.sum(grad_rows * bias, axis=1, keepdims=True)
        narrow = grad_rows.astype(bf16)
        by_byte[...] += mm(mixing[j], narrow, rows_rows)
        against = mm(narrow, table[...], cols_cols)
        for r in reached(j):
            picked = hot[:, r * vocab : (r + taps) * vocab].astype(f32) * against
            found = jnp.sum(picked, axis=1, keepdims=True) + on_bias
            grad_coefficients = jnp.where(lane == period * j + r, found, grad_coefficients)
    grad_coefficients = jnp.where(
        coefficient_inside(rows, first, total_bytes), grad_coefficients, 0.0
    )
    grad_sizes = [exact(grad_coefficients, spread[size], cols_cols) for size in range(4)]
    mean_grad = sum(size_weights[size] * grad_sizes[size] for size in range(4))
    grad_scores = jnp.zeros((rows, 128), f32)
    for size in range(4):
        grad_size = size_weights[size] * (grad_sizes[size] - mean_grad)
        grad_scores = grad_scores + (
            grad_size if size == 0 else exact(grad_size, pool[size - 1], cols_cols)
        )
    grad_scores = jnp.where(position_inside(rows, first, total_bytes), grad_scores, 0.0)
    score_sum = jnp.sum(jnp.sum(grad_scores, axis=1, keepdims=True), axis=0, keepdims=True)
    small[1:2, :] += bias_grad + score_sum * score
    small[2:3, :] += score_sum * bias
    for r in range(columns):
        shifted = pltpu.roll(grad_scores, 128 - r, 1) if r else grad_scores
        shifted = jnp.where(lane < taps, shifted, 0.0)
        high = shifted.astype(bf16)
        by_score[...] += mm(hot[:, r * vocab : (r + 1) * vocab], high, rows_rows)

    @pl.when(step == pl.num_programs(0) - 1)
    def _():
        emb = embedding[...].astype(f32)
        conv = conv_weight[...].astype(f32)
        grad_embedding = jnp.zeros((vocab, width), f32)
        grad_score = small[2:3, :]
        bytes_score = mm(by_score[...].astype(bf16), embedding[...], rows_rows)
        conv_rows = []
        for tap in range(taps):
            at = taps - 1 - tap
            here = by_byte[tap * vocab : (tap + 1) * vocab, :] + by_score[:, at : at + 1] * score
            grad_embedding = grad_embedding + conv[tap : tap + 1] * here
            conv_rows.append(jnp.sum(emb * here, axis=0, keepdims=True))
            grad_score = grad_score + conv[tap : tap + 1] * bytes_score[at : at + 1, :]
        rest = packed.shape[0] - vocab
        tail = conv_rows + [small[1:2, :], grad_score, small[0:1, :], grad_gain_second[...]]
        tail = jnp.concatenate(tail + [jnp.zeros((rest - len(tail), width), f32)], axis=0)
        packed[0:vocab, :] = grad_embedding.astype(bf16)
        packed[vocab:, :] = tail.astype(bf16)


def exchange(value, axis, mask):
    size = lax.axis_size(axis)
    return lax.ppermute(value, axis, [(i, i ^ mask) for i in range(size)])


def shards(
    byte_ids,
    byte_lengths,
    embedding,
    conv_weight,
    conv_bias,
    score_weight,
    norm_first,
    query_weight,
    key_weight,
    value_weight,
    out_weight,
    rel_bias,
    norm_second,
    gate_weight,
    up_weight,
    down_weight,
    out_grad,
):
    group = byte_ids.shape[1]
    ways = lax.axis_size("tensor")
    section, tensor, seq = (lax.axis_index(name) for name in ("section", "tensor", "seq"))
    total_bytes = group * lax.axis_size("seq")
    count = group // 2
    seq_tokens = total_bytes // 2
    heads = rel_bias.shape[1]
    width = query_weight.shape[1]
    vocab, model = embedding.shape
    units = gate_weight.shape[1]
    piece = count // ways
    conv_bias, score_weight, norm_first, norm_second = (
        item[None, :] for item in (conv_bias, score_weight, norm_first, norm_second)
    )
    length = byte_lengths[section]
    info = jnp.stack([section, tensor, seq, length]).astype(jnp.int32)
    steps = -(-total_bytes // (period * chunk_rows))
    rows = steps * chunk_rows
    token_rows = rows * pairs
    chunk_tokens = chunk_rows * pairs

    own_ids = lax.dynamic_index_in_dim(byte_ids, section, 0, keepdims=False)
    all_ids = lax.all_gather(own_ids, "seq", axis=0, tiled=True)
    all_ids = jnp.where(jnp.arange(total_bytes) < length, all_ids, -1)
    padded = jnp.pad(all_ids, (2, rows * period - total_bytes + 10), constant_values=-1)
    ids = jnp.concatenate(
        [
            padded[: rows * period].reshape(rows, period),
            padded[period : (rows + 1) * period].reshape(rows, period)[:, : taps - 1],
        ],
        axis=1,
    )
    out_weights = [out_weight] + [exchange(out_weight, "tensor", k) for k in range(1, ways)]
    pool, spread, total = (jnp.asarray(item) for item in pool_tables())
    table, score_table, bias_score = call(
        prepare_kernel,
        [like((taps * vocab, model), bf16), like((vocab, 128), bf16), like((8, 128), f32)],
        embedding,
        conv_weight,
        score_weight,
        conv_bias,
    )

    tokens, mixing, coefficients, size_weights = call(
        functools.partial(gbst_kernel, total_bytes),
        [
            like((token_rows, model), bf16),
            like((pairs, rows, taps * vocab), bf16),
            like((rows, 128), f32),
            like((4, rows, 128), f32),
        ],
        ids,
        table,
        score_table,
        pool,
        spread,
        total,
        conv_bias,
        bias_score,
        specs=[pl.BlockSpec((chunk_rows, columns), lambda i: (i, 0))] + [whole] * 7,
        out_specs=[
            pl.BlockSpec((chunk_tokens, model), lambda i: (i, 0)),
            pl.BlockSpec((pairs, chunk_rows, taps * vocab), lambda i: (0, i, 0)),
            pl.BlockSpec((chunk_rows, 128), lambda i: (i, 0)),
            pl.BlockSpec((4, chunk_rows, 128), lambda i: (0, i, 0)),
        ],
        scratch=[
            pltpu.VMEM((chunk_rows, columns * vocab), bf16),
            pltpu.VMEM((model // 128, chunk_tokens, 128), f32),
        ],
        grid=(steps,),
    )

    normed, queries, keys, values, probs, attended = call(
        functools.partial(attend_kernel, heads),
        [
            like((seq_tokens, model), bf16),
            like((count, width), bf16),
            like((seq_tokens, width), bf16),
            like((seq_tokens, width), bf16),
            like((heads, count, seq_tokens), bf16),
            like((count, width), bf16),
        ],
        info,
        tokens,
        norm_first,
        query_weight,
        key_weight,
        value_weight,
        rel_bias,
        specs=[scalars] + [whole] * 6,
    )
    all_attended = [attended] + [exchange(attended, "tensor", k) for k in range(1, ways)]

    def of_section(*dims):
        return pl.BlockSpec((None, *dims), lambda i, info: (info[0], *(0 for _ in dims)))

    def feed_call(kernel, out, args, specs, scratch=()):
        return pl.pallas_call(
            kernel,
            out_shape=out,
            grid_spec=pltpu.PrefetchScalarGridSpec(
                num_scalar_prefetch=1,
                grid=(1,),
                in_specs=specs,
                out_specs=[whole] * len(out),
                scratch_shapes=list(scratch),
            ),
            compiler_params=pltpu.CompilerParams(vmem_limit_bytes=vmem_limit),
        )(*args)

    middle, normed_second, inner, grad_gate, grad_up, *normed_parts = feed_call(
        functools.partial(feed_kernel, ways),
        [
            like((count, model), f32),
            like((count, model), bf16),
            like((count, units), bf16),
            like((count, units), bf16),
            like((count, units), bf16),
        ]
        + [like((piece, model), bf16)] * ways,
        [info, *all_attended, *out_weights, tokens, norm_second]
        + [gate_weight, up_weight, down_weight, out_grad],
        [whole] * (2 * ways + 5) + [of_section(count, model)],
        [pltpu.VMEM((count, model), f32)],
    )
    normed_parts = normed_parts[:1] + [
        exchange(normed_parts[k], "tensor", k) for k in range(1, ways)
    ]

    def feed_grads(info, *refs):
        feed_grad_kernel(*refs)

    encoded, grad_down, grad_gate_weight, grad_up_weight = feed_call(
        feed_grads,
        [
            like((count, model), bf16),
            like((units, model), bf16),
            like((model, units), bf16),
            like((model, units), bf16),
        ],
        [info, inner, normed_second, grad_gate, grad_up, out_grad, down_weight],
        [whole] * 4 + [of_section(count, model), whole],
    )
    output = (middle + lax.psum(encoded, "tensor").astype(f32)).astype(bf16)[None]

    grad_branch, grad_middle, grad_gain_second = feed_call(
        functools.partial(middle_kernel, ways),
        [like((piece, model), bf16), like((piece, model), f32), like((1, model), f32)],
        [info, *normed_parts, middle, out_grad, norm_second],
        [whole] * (ways + 1) + [of_section(count, model), whole],
    )
    branches = [grad_branch] + [exchange(grad_branch, "tensor", k) for k in range(1, ways)]
    (
        grad_out_weight,
        grad_query_weight,
        grad_key_weight,
        grad_value_weight,
        grad_rel,
        grad_queries,
        grad_keys,
        grad_values,
    ) = call(
        functools.partial(attend_back_kernel, heads, ways),
        [
            like((width, model), bf16),
            like((model, width), bf16),
            like((model, width), bf16),
            like((model, width), bf16),
            like((rel_bias.shape[0], 8), f32),
            like((token_rows, width), bf16),
            like((token_rows, width), bf16),
            like((token_rows, width), bf16),
        ],
        info,
        *branches,
        attended,
        probs,
        queries,
        keys,
        values,
        normed,
        out_weight,
        rel_bias,
        specs=[scalars] + [whole] * (ways + 8),
        scratch=[pltpu.VMEM((count, model), bf16)],
    )

    per_chunk = pl.BlockSpec((chunk_tokens, width), lambda i: (i, 0))
    packed_rows = 16 * ways * -(-(vocab + taps + 4) // (16 * ways))
    packed = call(
        functools.partial(gbst_back_kernel, total_bytes, seq_tokens),
        like((packed_rows, model), bf16),
        info,
        grad_queries,
        grad_keys,
        grad_values,
        tokens,
        query_weight,
        key_weight,
        value_weight,
        norm_first,
        grad_middle,
        grad_gain_second,
        table,
        mixing,
        coefficients,
        size_weights,
        ids,
        pool,
        spread,
        total,
        embedding,
        conv_weight,
        conv_bias,
        score_weight,
        specs=[scalars]
        + [per_chunk] * 3
        + [pl.BlockSpec((chunk_tokens, model), lambda i: (i, 0))]
        + [whole] * 7
        + [
            pl.BlockSpec((pairs, chunk_rows, taps * vocab), lambda i: (0, i, 0)),
            pl.BlockSpec((chunk_rows, 128), lambda i: (i, 0)),
            pl.BlockSpec((4, chunk_rows, 128), lambda i: (0, i, 0)),
            pl.BlockSpec((chunk_rows, columns), lambda i: (i, 0)),
        ]
        + [whole] * 7,
        scratch=[
            pltpu.VMEM((model // 128, chunk_tokens, 128), f32),
            pltpu.VMEM((chunk_rows, columns * vocab), bf16),
            pltpu.VMEM((taps * vocab, model), f32),
            pltpu.VMEM((vocab, 128), f32),
            pltpu.VMEM((8, model), f32),
            pltpu.VMEM((chunk_tokens, model), f32),
        ],
        grid=(steps,),
    )
    packed = lax.psum(packed, ("section", "tensor", "seq")).astype(f32)
    sums = lax.psum(
        (
            grad_query_weight,
            grad_key_weight,
            grad_value_weight,
            grad_out_weight,
            grad_rel[:, :heads].astype(bf16),
            grad_gate_weight,
            grad_up_weight,
            grad_down,
        ),
        ("section", "seq"),
    )
    sums = [item.astype(f32) for item in sums]
    tail = packed[vocab:]
    return (
        output,
        packed[:vocab],
        tail[:taps],
        tail[taps],
        tail[taps + 1],
        tail[taps + 2],
        sums[0],
        sums[1],
        sums[2],
        sums[3],
        sums[4],
        tail[taps + 3],
        sums[5],
        sums[6],
        sums[7],
    )


def solution(mesh):
    return jax.shard_map(
        shards,
        mesh=mesh,
        in_specs=(
            P(None, "seq"),
            P(),
            P(),
            P(),
            P(),
            P(),
            P(),
            P(None, "tensor"),
            P(None, "tensor"),
            P(None, "tensor"),
            P("tensor", None),
            P(None, "tensor"),
            P(),
            P(None, "tensor"),
            P(None, "tensor"),
            P("tensor", None),
            P(None, "seq", None),
        ),
        out_specs=(
            P("section", "seq", None),
            P(),
            P(),
            P(),
            P(),
            P(),
            P(None, "tensor"),
            P(None, "tensor"),
            P(None, "tensor"),
            P("tensor", None),
            P(None, "tensor"),
            P(),
            P(None, "tensor"),
            P(None, "tensor"),
            P("tensor", None),
        ),
        check_vma=False,
    )
```

```python
import functools

import jax
import jax.numpy as jnp
import numpy as np
from jax import lax
from jax.experimental import pallas as pl
from jax.experimental.pallas import tpu as pltpu
from jax.sharding import PartitionSpec as P

epsilon = 1e-06
masked_score = -1e30
far_thresholds = (12, 16, 23, 32, 46, 64, 91)
period = 12
pairs = period // 2
taps = 5
columns = period + taps - 1
chunk_rows = 176
feed_chunks = 1
f32 = jnp.float32
bf16 = jnp.bfloat16
whole = pl.BlockSpec(memory_space=pltpu.VMEM)
local = pl.BlockSpec(memory_space=pltpu.VMEM)
distant = pl.BlockSpec(memory_space=pltpu.VMEM)
scalars = pl.BlockSpec(memory_space=pltpu.SMEM)


def pool_tables():
    pool = np.zeros((128, 384), np.float32)
    spread = np.zeros((512, 128), np.float32)
    total = np.zeros((128, 128), np.float32)
    for size in range(1, 5):
        for g in range(period):
            for r in range(period):
                if r // size == g // size:
                    if size > 1:
                        pool[4 + r, 128 * (size - 2) + 4 + g] = 1.0
                    spread[128 * (size - 1) + 4 + g, period * (g // 2) + r] = 1.0
    for j in range(pairs):
        total[period * j : period * (j + 1), j] = 1.0
    return (pool, spread, total)


def split_mm(a, b, dims=((1,), (0,))):
    high = a.astype(bf16)
    low = (a - high.astype(f32)).astype(bf16)
    return mm(high, b[...], dims) + mm(low, b[...], dims)


def lanes(value, count):
    return [value[:, 128 * i : 128 * (i + 1)] for i in range(count)]


def reached(j):
    found = set()
    for g in (2 * j, 2 * j + 1):
        for size in range(1, 5):
            first = size * (g // size)
            found.update(range(first, first + size))
    return sorted(found)


def exact(a, b, dims=((1,), (0,))):
    return lax.dot_general(
        a, b, (dims, ((), ())), precision=lax.Precision.HIGHEST, preferred_element_type=f32
    )


def mm(a, b, dims=((1,), (0,))):
    return lax.dot_general(a, b, (dims, ((), ())), preferred_element_type=f32)


rows_rows = ((0,), (0,))
cols_cols = ((1,), (1,))


def call(kernel, out, *args, specs=None, scratch=(), grid=None, out_specs=None, near=False, limit=16, cost=1):
    extra = {} if grid is None else {"grid": grid}
    specs = [whole] * len(args) if specs is None else specs
    if near:
        spaces = {id(local): pltpu.VMEM, id(distant): pltpu.HBM}
        args = [
            pltpu.with_memory_space_constraint(arg, spaces[id(spec)]) if id(spec) in spaces else arg
            for arg, spec in zip(args, specs)
        ]
    return pl.pallas_call(
        kernel,
        out_shape=out,
        in_specs=specs,
        out_specs=jax.tree.map(lambda _: whole, out) if out_specs is None else out_specs,
        scratch_shapes=list(scratch),
        cost_estimate=pl.CostEstimate(
            flops=int(cost * 1e6), bytes_accessed=int(cost * 3e3), transcendentals=0
        ),
        compiler_params=pltpu.CompilerParams(
            vmem_limit_bytes=(limit if near else 56) * 2**20
        ),
        **extra,
    )(*args)


def like(shape, kind):
    return jax.ShapeDtypeStruct(shape, kind)


def iota(shape, dim):
    return lax.broadcasted_iota(jnp.int32, shape, dim)


def bucket_of(relative):
    distance = jnp.abs(relative)
    far_bucket = 8 + sum(
        ((distance >= threshold).astype(jnp.int32) for threshold in far_thresholds)
    )
    return jnp.where(distance < 8, distance, far_bucket) + 16 * (relative > 0).astype(jnp.int32)


def bucket_hot(buckets, width, query_first, queries):
    offsets = iota((buckets, width), 1) - (queries - 1) - query_first
    return (bucket_of(offsets) == iota((buckets, width), 0)).astype(f32)


def one_hot(ids, vocab):
    return jnp.where(ids == iota((ids.shape[0], vocab), 1), 1.0, 0.0).astype(bf16)


def head_mask(width, head_dim, head):
    return iota((1, width), 1) // head_dim == head


def as_row(vector):
    return vector[...].astype(f32).reshape(1, vector.shape[0])


def fill_table(embedding, conv_weight, table):
    vocab = embedding.shape[0]
    emb = embedding[...].astype(f32)
    for tap in range(taps):
        row = conv_weight[tap : tap + 1, :].astype(f32)
        table[tap * vocab : (tap + 1) * vocab, :] = (emb * row).astype(bf16)


def prepare_kernel(embedding, conv_weight, score_weight, conv_bias, table, score_table, bias_score):
    emb = embedding[...].astype(f32)
    conv = conv_weight[...].astype(f32)
    score = as_row(score_weight)
    fill_table(embedding, conv_weight, table)
    scored = jnp.concatenate(
        [conv[tap : tap + 1] * score for tap in reversed(range(taps))]
        + [jnp.zeros((128 - taps, conv.shape[1]), f32)],
        axis=0,
    )
    by_byte = exact(emb, scored, cols_cols)
    high = by_byte.astype(bf16).astype(f32)
    middle = (by_byte - high).astype(bf16).astype(f32)
    low = by_byte - high - middle
    score_table[...] = (high + pltpu.roll(middle, 32, 1) + pltpu.roll(low, 64, 1)).astype(bf16)
    bias_score[...] = jnp.broadcast_to(
        jnp.sum(as_row(conv_bias) * score, axis=1, keepdims=True), bias_score.shape
    )


def position_inside(rows, first, total_bytes):
    lane = iota((rows, 128), 1)
    place = period * (first + iota((rows, 128), 0)) + lane - 4
    return (lane >= 4) & (lane < 4 + period) & (place < total_bytes)


def coefficient_inside(rows, first, total_bytes):
    lane = iota((rows, 128), 1)
    place = period * (first + iota((rows, 128), 0)) + lax.rem(lane, period)
    return (lane < period * pairs) & (place < total_bytes)


def laid_out(pieces, lengths, line, first, rows):
    section, seq = (lax.axis_index("section"), lax.axis_index("seq"))
    count = pieces[0].shape[1] // 128
    line[...] = jnp.full(line.shape, -1.0, f32)
    for k, item in enumerate(pieces):
        for at in range(count):
            both = item[:, at * 128 : (at + 1) * 128]
            row = jnp.where(section == 1, both[1:2], both[0:1])
            line[pl.ds((seq ^ k) * count + at + 1, 1), :] = row.astype(f32)
    place = 128 * (iota(line.shape, 0) - 1) + iota(line.shape, 1)
    values = jnp.where(place < lengths[section], line[...], -1.0).astype(bf16)
    shape = (rows, line.shape[0])
    flipped = first + rows - 1 - iota(shape, 0)
    here = (period * flipped + 126) // 128
    found = [
        mm((here + step == iota(shape, 1)).astype(bf16), values) for step in range(2)
    ]
    start = lax.rem(2 - period * (first + rows - 1) + 128 * period * (rows + first), 128)
    for _ in range(period // 4):
        found = [pltpu.roll(item, 0, 1, stride=4, stride_axis=0) for item in found]
    found = [pltpu.roll(item, start, 1) for item in found]
    shape = (rows, 128)
    lane = iota(shape, 1)
    begin = lax.rem(period * (first + rows - 1 - iota(shape, 0)) + 126, 128)
    merged_rows = jnp.where(lane + begin < 128, found[0], found[1]).astype(bf16)
    flip = (iota((rows, rows), 0) + iota((rows, rows), 1) == rows - 1).astype(bf16)
    return mm(flip, merged_rows)


def fill_hot(ids, hot, vocab):
    rows = ids.shape[0]
    value = iota((rows, vocab), 1).astype(f32)
    for r in range(columns):
        found = jnp.where(ids[:, r : r + 1] == value, 1.0, 0.0).astype(bf16)
        hot[r] = found


def gbst_kernel(total_bytes, steps, count, lengths, *refs):
    pieces = refs[:count]
    table, score_table, pool, spread, total, conv_bias, bias_score = refs[count : count + 7]
    tokens, kept, mixing, coefficients, size_weights, ids = refs[count + 7 : count + 13]
    hot, natural, line, narrow = refs[count + 13 :]
    rows = ids.shape[0]
    vocab = score_table.shape[0]
    width = table.shape[1]
    first = pl.program_id(0) * rows if steps > 1 else 0
    ids[...] = laid_out(pieces, lengths, line, first, rows)
    fill_hot(ids, hot, vocab)
    parts = mm(hot[...].reshape(columns * rows, vocab), score_table[...])
    scores = parts[:rows]
    for r in range(1, columns):
        scores = scores + pltpu.roll(parts[r * rows : (r + 1) * rows], r, 1)
    scores = scores + pltpu.roll(scores, 96, 1) + pltpu.roll(scores, 64, 1)
    scores = jnp.where(
        position_inside(rows, first, total_bytes), scores + bias_score[0:1, :], 0.0
    )
    pooled = lanes(split_mm(scores, pool), 3)
    by_size = [scores] + [item * (1.0 / (size + 2)) for size, item in enumerate(pooled)]
    largest = functools.reduce(jnp.maximum, by_size)
    weights = [jnp.exp(item - largest) for item in by_size]
    scale = 1.0 / sum(weights)
    weights = [weight * scale for weight in weights]
    for size in range(4):
        size_weights[size] = weights[size]
    weights = [weight * (0.5 / (size + 1)) for size, weight in enumerate(weights)]
    spread_sum = split_mm(jnp.concatenate(weights, axis=1), spread)
    spread_sum = jnp.where(coefficient_inside(rows, first, total_bytes), spread_sum, 0.0)
    coefficients[...] = spread_sum
    narrow[...] = spread_sum.astype(bf16)
    row_total = split_mm(spread_sum, total)

    def mix(step, carry):
        own = pl.ds(pl.multiple_of(step * 16, 16), 16)
        weight = narrow[own, :]
        for j in range(pairs):
            acc = [None] * taps
            for r in reached(j):
                at = period * j + r
                column = jnp.broadcast_to(weight[:, at : at + 1], (16, vocab))
                for tap in range(taps):
                    term = hot[r + tap, own, :] * column
                    acc[tap] = term if acc[tap] is None else acc[tap] + term
            for tap in range(taps):
                mixing[j, own, tap * vocab : (tap + 1) * vocab] = acc[tap]
        return carry

    lax.fori_loop(0, rows // 16, mix, 0, unroll=True)
    bias = as_row(conv_bias)
    by_phase = mm(mixing[...].reshape(pairs * rows, taps * vocab), table[...])
    for j in range(pairs):
        rows_j = by_phase[j * rows : (j + 1) * rows] + row_total[:, j : j + 1] * bias
        for at in range(width // 128):
            natural[at, pl.ds(j, rows, stride=pairs), :] = rows_j[:, at * 128 : (at + 1) * 128]
    for at in range(width // 128):
        tokens[:, at * 128 : (at + 1) * 128] = natural[at].astype(bf16)
    kept[...] = tokens[...]


def attend_kernel(
    heads,
    lengths,
    tokens,
    gain,
    query_weight,
    key_weight,
    value_weight,
    rel_bias,
    normed,
    queries,
    keys,
    values,
    probs,
    attended,
    own_tokens,
):
    seq_tokens = normed.shape[0]
    count, width = queries.shape
    head_dim = width // heads
    query_first = pl.multiple_of(lax.axis_index("seq") * count, count)
    live_tokens = lengths[lax.axis_index("section")]
    own_tokens[...] = tokens[pl.ds(query_first, count), :]
    hidden = tokens[0:seq_tokens, :].astype(f32)
    scale = lax.rsqrt(jnp.mean(hidden * hidden, axis=-1, keepdims=True) + epsilon)
    normed[...] = (hidden * scale * as_row(gain)).astype(bf16)
    keys[...] = mm(normed[...], key_weight[...], cols_cols).astype(bf16)
    values[...] = mm(normed[...], value_weight[...], cols_cols).astype(bf16)
    queries[...] = mm(
        normed[pl.ds(query_first, count), :], query_weight[...], cols_cols
    ).astype(bf16)
    span = seq_tokens + count
    hot = bucket_hot(rel_bias.shape[1], span, query_first, count)
    by_offset = mm(rel_bias[...].astype(f32), hot)
    live = 2 * iota((1, seq_tokens), 1) < live_tokens
    mixed = jnp.zeros((count, width), f32)
    for head in range(heads):
        mask = head_mask(width, head_dim, head)
        row = jnp.broadcast_to(by_offset[head : head + 1, :], (count, span))
        bias = pltpu.roll(row, span - (count - 1), 1, stride=1, stride_axis=0)[:, :seq_tokens]
        own = jnp.where(mask, queries[...], jnp.zeros((), bf16))
        scores = mm(own, keys[...], cols_cols) + bias
        scores = jnp.where(live, scores, masked_score)
        raised = jnp.exp(scores - jnp.max(scores, axis=-1, keepdims=True))
        part = (raised * (1.0 / jnp.sum(raised, axis=-1, keepdims=True))).astype(bf16)
        probs[head] = part
        mixed = jnp.where(mask, mm(part, values[...]), mixed)
    attended[...] = mixed.astype(bf16)


def gelu(value):
    inner = np.float32(np.sqrt(2 / np.pi)) * (value + 0.044715 * (value * value * value))
    return 0.5 * value * (1.0 + jnp.tanh(inner))


def gelu_both(value):
    root = np.float32(np.sqrt(2 / np.pi))
    square = value * value
    tanh = jnp.tanh(root * value * (1.0 + 0.044715 * square))
    half = 0.5 * (1.0 + tanh)
    slope = half + 0.5 * value * (1.0 - tanh * tanh) * root * (1.0 + 3 * 0.044715 * square)
    return (value * half, slope)


def feed_kernel(ways, *refs):
    attended = refs[:ways]
    out_weight = refs[ways : 2 * ways]
    tokens, gain, gate_weight, up_weight, down_weight, out_grad = refs[2 * ways : 2 * ways + 6]
    middle, normed, inner, grad_gate, grad_up = refs[2 * ways + 6 : 2 * ways + 11]
    pieces = refs[2 * ways + 11 : 3 * ways + 11]
    whole_part = refs[3 * ways + 11]
    count = middle.shape[0]
    branch = sum(mm(a[...], w[...]) for a, w in zip(attended, out_weight))
    total = tokens[...].astype(f32) + branch
    middle[...] = total
    scale = lax.rsqrt(jnp.mean(total * total, axis=-1, keepdims=True) + epsilon)
    normed[...] = (total * scale * as_row(gain)).astype(bf16)
    gate = mm(normed[...], gate_weight[...])
    upward = mm(normed[...], up_weight[...])
    grad_inner = mm(out_grad[lax.axis_index("section")], down_weight[...], cols_cols)
    active, slope = gelu_both(gate)
    inner[...] = (active * upward).astype(bf16)
    grad_gate[...] = (grad_inner * upward * slope).astype(bf16)
    grad_up[...] = (grad_inner * active).astype(bf16)
    whole_part[...] = mm(grad_gate[...], gate_weight[...], cols_cols) + mm(
        grad_up[...], up_weight[...], cols_cols
    )
    deal(whole_part, pieces)


def deal(source, pieces):
    piece = pieces[0].shape[0]
    for k, out in enumerate(pieces):
        at = pl.multiple_of((lax.axis_index("tensor") ^ k) * piece, piece)
        out[...] = source[pl.ds(at, piece), :].astype(bf16)


def collect(pieces, target):
    piece = pieces[0].shape[0]
    for k, item in enumerate(pieces):
        at = pl.multiple_of((lax.axis_index("tensor") ^ k) * piece, piece)
        target[pl.ds(at, piece), :] = item[...].astype(target.dtype)


def feed_grad_kernel(ways, chunks, inner, normed, grad_gate, grad_up, out_grad, down_weight, *refs):
    sums, pieces = (refs[: 2 * chunks], refs[2 * chunks : 2 * chunks + ways])
    whole_part, stack = refs[2 * chunks + ways :]
    first = 0
    for left, right in (
        (normed, grad_gate[...]),
        (normed, grad_up[...]),
        (inner, out_grad[lax.axis_index("section")]),
    ):
        product = mm(left[...], right, rows_rows)
        rows, columns = product.shape
        for at in range(0, columns, 256):
            stack[first : first + rows, :] = product[:, at : at + 256].astype(bf16)
            first += rows
    section = lax.axis_index("section")
    half = first // (2 * chunks)
    for chunk in range(chunks):
        for side, out in enumerate(sums[2 * chunk : 2 * chunk + 2]):
            at = (2 * chunk + (section ^ side)) * half
            out[...] = stack[pl.ds(pl.multiple_of(at, half), half), :]
    whole_part[...] = mm(inner[...], down_weight[...])
    deal(whole_part, pieces)


def middle_kernel(ways, *refs):
    pieces = refs[:ways]
    middle, out_grad, gain, grad_branch, grad_middle, grad_gain = refs[ways:]
    piece = pieces[0].shape[0]
    at = pl.multiple_of(lax.axis_index("tensor") * piece, piece)
    grad_normed = sum(item[...].astype(f32) for item in pieces)
    own = middle[pl.ds(at, piece), :]
    scale = lax.rsqrt(jnp.mean(own * own, axis=-1, keepdims=True) + epsilon)
    grad_gain[...] = jnp.sum(grad_normed * own * scale, axis=0, keepdims=True)
    through = grad_normed * as_row(gain)
    total = (
        out_grad[lax.axis_index("section"), pl.ds(at, piece), :].astype(f32)
        + scale * through
        - own * (scale * scale * scale) * jnp.mean(through * own, axis=-1, keepdims=True)
    )
    grad_middle[...] = total
    grad_branch[...] = total.astype(bf16)


def attend_back_kernel(heads, ways, *refs):
    branches = refs[:ways]
    attended, probs, queries, keys, values, normed, out_weight = refs[ways : ways + 7]
    keep, send, rel_grad, grad_queries, grad_keys, grad_values = refs[ways + 7 : ways + 13]
    branch, stack = refs[ways + 13 :]
    count, width = queries.shape
    seq_tokens = keys.shape[0]
    head_dim = width // heads
    collect(branches, branch)
    query_first = pl.multiple_of(lax.axis_index("seq") * count, count)
    grad_attended = mm(branch[...], out_weight[...], cols_cols).astype(bf16)
    stack[3 * width :, :] = mm(attended[...], branch[...], rows_rows).astype(bf16)
    span = seq_tokens + count
    flip = (iota((count, count), 0) + iota((count, count), 1) == count - 1).astype(bf16)
    zero = jnp.zeros((), bf16)
    by_offset = []
    query_sum = jnp.zeros((count, width), f32)
    key_sum = jnp.zeros((seq_tokens, width), f32)
    value_sum = jnp.zeros((seq_tokens, width), f32)
    for head in range(heads):
        mask = head_mask(width, head_dim, head)
        own = jnp.where(mask, grad_attended, zero)
        grad_probs = mm(own, values[...], cols_cols)
        part = probs[head].astype(f32)
        inside = jnp.sum(part * grad_probs, axis=-1, keepdims=True)
        grad_scores = (part * (grad_probs - inside)).astype(bf16)
        flipped = jnp.concatenate(
            [mm(flip, grad_scores), jnp.zeros((count, count), f32)], axis=1
        )
        by_offset.append(
            jnp.sum(pltpu.roll(flipped, 0, 1, stride=1, stride_axis=0), axis=0, keepdims=True)
        )
        query_sum = jnp.where(mask, mm(grad_scores, keys[...]), query_sum)
        key_sum = key_sum + mm(
            grad_scores, jnp.where(mask, queries[...], zero), rows_rows
        )
        value_sum = value_sum + mm(probs[head], own, rows_rows)
    by_offset = jnp.concatenate(by_offset + [jnp.zeros((8 - heads, span), f32)], axis=0)
    hot = bucket_hot(128, span, query_first, count)
    rel_grad[...] = exact(by_offset, hot, cols_cols)
    query_sum = query_sum.astype(bf16)
    stack[0:width, :] = mm(
        query_sum, normed[pl.ds(query_first, count), :], rows_rows
    ).astype(bf16)
    grad_queries[...] = jnp.zeros(grad_queries.shape, bf16)
    grad_queries[pl.ds(query_first, count), :] = query_sum
    rest = grad_keys.shape[0] - seq_tokens
    for at, (total, place) in enumerate(((key_sum, grad_keys), (value_sum, grad_values))):
        total = total.astype(bf16)
        place[0:seq_tokens, :] = total
        place[seq_tokens:, :] = jnp.zeros((rest, width), bf16)
        stack[(at + 1) * width : (at + 2) * width, :] = mm(
            total, normed[...], rows_rows
        ).astype(bf16)
    half = keep.shape[0]
    section = lax.axis_index("section")
    keep[...] = stack[pl.ds(pl.multiple_of(section * half, half), half), :]
    send[...] = stack[pl.ds(pl.multiple_of((1 - section) * half, half), half), :]


def normed_back_kernel(
    steps,
    seq_tokens,
    ways,
    grad_queries,
    grad_keys,
    grad_values,
    tokens,
    query_weight,
    key_weight,
    value_weight,
    gain,
    grad_middle,
    grad_tokens,
    grad_gain,
    whole_part,
):
    token_rows, width = tokens.shape
    step = pl.program_id(0) if steps > 1 else 0
    whole_part[...] = (
        mm(grad_queries[...], query_weight[...])
        + mm(grad_keys[...], key_weight[...])
        + mm(grad_values[...], value_weight[...])
    )
    scale_row = as_row(gain)
    block = 32

    def one(part, total):
        own = pl.ds(pl.multiple_of(part * block, block), block)
        place = token_rows * step + part * block + iota((block, 1), 0)
        hidden = jnp.where(place < seq_tokens, tokens[own, :].astype(f32), 0.0)
        grad_normed = whole_part[own, :]
        scale = lax.rsqrt(jnp.mean(hidden * hidden, axis=-1, keepdims=True) + epsilon)
        against = grad_normed * hidden
        total = total + jnp.sum((against * scale).reshape(block // 8, 8, width), axis=0)
        inner = jnp.mean(against * scale_row, axis=-1, keepdims=True)
        result = scale * (grad_normed * scale_row) - hidden * (scale * scale * scale * inner)
        for at in range(width // 128):
            grad_tokens[at, own, :] = result[:, at * 128 : (at + 1) * 128]
        return total

    total = jnp.zeros((8, width), f32)
    total = lax.fori_loop(0, token_rows // block, one, total, unroll=11)
    total = jnp.sum(total, axis=0, keepdims=True)
    if steps > 1:
        total = total + jnp.where(step == 0, 0.0, grad_gain[0:1, :])
    grad_gain[0:1, :] = total
    piece = grad_middle.shape[0]
    own_first = (lax.axis_index("seq") * ways + lax.axis_index("tensor")) * piece
    own_first = own_first - token_rows * step
    for part in range(piece // block):
        begin = own_first + part * block

        @pl.when((begin >= 0) & (begin < token_rows))
        def _():
            place = pl.ds(pl.multiple_of(begin, block), block)
            rows = grad_middle[part * block : (part + 1) * block, :]
            for at in range(width // 128):
                grad_tokens[at, place, :] += rows[:, at * 128 : (at + 1) * 128]


def gbst_back_kernel(
    total_bytes,
    steps,
    grad_tokens,
    grad_gain_first,
    grad_gain_second,
    rel_grad,
    mixing,
    coefficients,
    size_weights,
    ids,
    pool,
    spread,
    total,
    embedding,
    conv_weight,
    conv_bias,
    score_weight,
    keep,
    send,
    hot,
    by_byte,
    by_score,
    small,
    packed,
    table,
    phased,
    against,
    found,
):
    rows = ids.shape[0]
    vocab, width = embedding.shape
    step = pl.program_id(0) if steps > 1 else 0
    first = step * rows
    score = as_row(score_weight)
    bias = as_row(conv_bias)

    def at_step(wanted):
        return pl.when(step == wanted) if steps > 1 else lambda run: run()

    @at_step(0)
    def _():
        by_score[...] = jnp.zeros(by_score.shape, f32)
        small[...] = jnp.zeros(small.shape, f32)
        fill_table(embedding, conv_weight, table)

    row_total = split_mm(coefficients[...], total)
    lane = iota((rows, 128), 1)
    on_bias = []
    bias_grad = jnp.zeros((1, width), f32)
    for j in range(pairs):
        grad_rows = jnp.concatenate(
            [grad_tokens[at, pl.ds(j, rows, stride=pairs), :] for at in range(width // 128)],
            axis=1,
        )
        narrow = grad_rows.astype(bf16)
        phased[j * rows : (j + 1) * rows, :] = narrow
        bias_grad = bias_grad + jnp.sum(row_total[:, j : j + 1] * grad_rows, axis=0, keepdims=True)
        on_bias.append(jnp.sum(grad_rows * bias, axis=1, keepdims=True))
    against[...] = mm(phased[...], table[...], cols_cols)
    fill_hot(ids, hot, vocab)
    product = mm(mixing[...].reshape(pairs * rows, taps * vocab), phased[...], rows_rows)
    if steps > 1:
        by_byte[...] = product + jnp.where(step == 0, 0.0, by_byte[...])
    else:
        by_byte[...] = product

    def pick(part, carry):
        own = pl.ds(pl.multiple_of(part * 16, 16), 16)
        spot = iota((16, 128), 1)
        result = jnp.zeros((16, 128), f32)
        for j in range(pairs):
            for r in reached(j):
                begin = pl.ds(pl.multiple_of(j * rows + part * 16, 16), 16)
                picked = sum(
                    hot[r + tap, own, :].astype(f32)
                    * against[begin, tap * vocab : (tap + 1) * vocab]
                    for tap in range(taps)
                )
                result = jnp.where(
                    spot == period * j + r, jnp.sum(picked, axis=1, keepdims=True), result
                )
        found[own, :] = result
        return carry

    lax.fori_loop(0, rows // 16, pick, 0, unroll=True)
    grad_coefficients = found[...]
    for j in range(pairs):
        grad_coefficients = grad_coefficients + jnp.where(lane // period == j, on_bias[j], 0.0)
    grad_coefficients = jnp.where(
        coefficient_inside(rows, first, total_bytes), grad_coefficients, 0.0
    )
    grad_sizes = lanes(split_mm(grad_coefficients, spread, cols_cols), 4)
    grad_sizes = [item * (0.5 / (size + 1)) for size, item in enumerate(grad_sizes)]
    mean_grad = sum(size_weights[size] * grad_sizes[size] for size in range(4))
    by_size = [size_weights[size] * (grad_sizes[size] - mean_grad) for size in range(4)]
    pooled = [item * (1.0 / (size + 2)) for size, item in enumerate(by_size[1:])]
    grad_scores = by_size[0] + split_mm(jnp.concatenate(pooled, axis=1), pool, cols_cols)
    grad_scores = jnp.where(position_inside(rows, first, total_bytes), grad_scores, 0.0)
    score_sum = jnp.sum(jnp.sum(grad_scores, axis=1, keepdims=True), axis=0, keepdims=True)
    small[1:2, :] += bias_grad + score_sum * score
    small[2:3, :] += score_sum * bias
    shifted = []
    for r in range(columns):
        item = pltpu.roll(grad_scores, 128 - r, 1) if r else grad_scores
        shifted.append(jnp.where(lane < taps, item, 0.0).astype(bf16))
    shifted = jnp.concatenate(shifted, axis=0)
    by_score[...] += mm(hot[...].reshape(columns * rows, vocab), shifted, rows_rows)

    @at_step(steps - 1)
    def _():
        emb = embedding[...].astype(f32)
        conv = conv_weight[...].astype(f32)
        grad_embedding = jnp.zeros((vocab, width), f32)
        grad_score = small[2:3, :]
        bytes_score = mm(by_score[...].astype(bf16), embedding[...], rows_rows)
        conv_rows = []
        for tap in range(taps):
            at = taps - 1 - tap
            here = by_byte[tap * vocab : (tap + 1) * vocab, :] + by_score[:, at : at + 1] * score
            grad_embedding = grad_embedding + conv[tap : tap + 1] * here
            conv_rows.append(jnp.sum(emb * here, axis=0, keepdims=True))
            grad_score = grad_score + conv[tap : tap + 1] * bytes_score[at : at + 1, :]
        rest = packed.shape[0] - vocab
        tail = conv_rows + [small[1:2, :], grad_score]
        tail += [grad_gain_first[0:1, :], grad_gain_second[0:1, :]]
        copies = jnp.concatenate([rel_grad[...]] * (width // 128), axis=1)
        own = iota(copies.shape, 1) // 128 == lax.axis_index("tensor")
        tail.append(jnp.where(own, copies, 0.0))
        used = sum(item.shape[0] for item in tail)
        tail = jnp.concatenate(tail + [jnp.zeros((rest - used, width), f32)], axis=0)
        packed[0:vocab, :] = grad_embedding.astype(bf16)
        packed[vocab:, :] = tail.astype(bf16)
        section = lax.axis_index("section")
        half = keep.shape[0]
        for side, out in enumerate((keep, send)):
            out[...] = packed[pl.ds(pl.multiple_of((section ^ side) * half, half), half), :]


def deal_kernel(keep, other, *refs):
    pieces, whole_part = (refs[:-1], refs[-1])
    whole_part[...] = keep[...].astype(f32) + other[...].astype(f32)
    deal(whole_part, pieces)


def copied_out(value):
    return [value] + [exchange(value, "tensor", k) for k in range(1, lax.axis_size("tensor"))]


def spread_out(pieces):
    return [pieces[0]] + [exchange(pieces[k], "tensor", k) for k in range(1, len(pieces))]


def seq_masks():
    return [1 << bit for bit in range(lax.axis_size("seq").bit_length() - 1)]


def merged(items):
    return sum(item.astype(f32) for item in items).astype(bf16)


def half_of(item, bit):
    half = item.shape[0] // 2
    return jnp.where(bit, item[half:], item[:half])


def even(rows):
    return rows % 32 == 0


def sum_over(items, axis, mask, halved):
    if not even(items[0].shape[0]):
        part = merged(items)
        return [part, exchange(part, axis, mask)]
    bit = (lax.axis_index(axis) & mask) != 0
    sent = merged([half_of(item, jnp.logical_not(bit)) for item in items])
    halved.append(mask)
    return [half_of(item, bit) for item in items] + [exchange(sent, axis, mask)]


class Staged:
    def __init__(self, keep, send):
        self.items = [keep, exchange(send, "section", 1)]
        self.masks = seq_masks()
        self.halved = []
        self.sent = None

    def add(self):
        mask = self.masks[0]
        rows = self.items[0].shape[0]
        if even(rows):
            bit = (lax.axis_index("seq") & mask) != 0
            self.sent = merged([half_of(item, jnp.logical_not(bit)) for item in self.items])
            self.items = [half_of(item, bit) for item in self.items]
            self.halved.append(mask)
        else:
            self.sent = merged(self.items)
            self.items = [self.sent]

    def swap(self):
        self.items = self.items + [exchange(self.sent, "seq", self.masks.pop(0))]

    def before(self, value):
        self.sent, value = lax.optimization_barrier((self.sent, value))
        return value

    def received_before(self, value):
        self.items[-1], value = lax.optimization_barrier((self.items[-1], value))
        return value

    def finish(self):
        while self.masks:
            self.add()
            self.swap()
        return merged(self.items)


def gather_sum(total, halved):
    pieces = {0: total}
    for mask in reversed(halved):
        for at, item in list(pieces.items()):
            pieces[at ^ mask] = exchange(item, "seq", mask)
    names = list(pieces)
    pieces = [pieces[name] for name in names]
    return (pieces + [exchange(item, "section", 1) for item in pieces], names)


def place_of(halved, at, rows, index):
    first = 0
    size = rows
    for mask in halved:
        size = size // 2
        first = first + jnp.where(((index ^ at) & mask) != 0, size, 0)
    return first


def unstack(pieces, halved, names, chunks, stack):
    count = len(names)
    section, seq = (lax.axis_index("section"), lax.axis_index("seq"))
    rows = pieces[0].shape[0] // chunks
    half = rows * count
    for i, item in enumerate(pieces):
        side, at = divmod(i, count)
        place = place_of(halved, names[at], half, seq) + (section ^ side) * half
        for chunk in range(chunks):
            first = pl.multiple_of(place + 2 * half * chunk, 8)
            stack[pl.ds(first, rows), :] = item[chunk * rows : (chunk + 1) * rows, :].astype(f32)


def weights_kernel(halved, names, *refs):
    count = 2 * len(names)
    pieces, outs, stack = (refs[:count], refs[count:-1], refs[-1])
    unstack(pieces, halved, names, 1, stack)
    rows = outs[0].shape[0]
    for i, out in enumerate(outs):
        out[...] = stack[i * rows : (i + 1) * rows, :]


def feed_weights_kernel(halved, names, chunks, *refs):
    count = 2 * len(names)
    pieces, outs, stack = (refs[:count], refs[count:-1], refs[-1])
    unstack(pieces, halved, names, chunks, stack)
    first = 0
    for out in outs:
        rows, columns = out.shape
        for at in range(0, columns, 256):
            out[:, at : at + 256] = stack[first : first + rows, :]
            first += rows


def packed_kernel(ways, heads, *refs):
    pieces = refs[: 2 * ways]
    embedding, conv, bias, score, first, second, rel, stack = refs[2 * ways :]
    rows = pieces[0].shape[0]
    vocab, width = embedding.shape
    section, tensor = (lax.axis_index("section"), lax.axis_index("tensor"))
    for i, item in enumerate(pieces):
        side, k = divmod(i, ways)
        at = ((section ^ side) * ways + (tensor ^ k)) * rows
        stack[pl.ds(pl.multiple_of(at, rows), rows), :] = item[...].astype(f32)
    embedding[...] = stack[0:vocab, :]
    conv[...] = stack[vocab : vocab + taps, :]
    for i, out in enumerate((bias, score, first, second)):
        out[...] = stack[vocab + taps + i : vocab + taps + i + 1, :].reshape(width)
    at = vocab + taps + 4
    own = stack[at : at + heads, pl.ds(pl.multiple_of(tensor * 128, 128), 128)]
    rel[...] = own[:, : rel.shape[1]]


def encoded_kernel(ways, *refs):
    pieces, middle, out = (refs[:ways], refs[ways], refs[ways + 1])
    piece = out.shape[0]
    at = pl.multiple_of(lax.axis_index("tensor") * piece, piece)
    total = sum(item[...].astype(f32) for item in pieces)
    out[...] = (middle[pl.ds(at, piece), :] + total).astype(bf16)


def assemble_kernel(ways, *refs):
    collect(refs[:ways], refs[ways])


def exchange(value, axis, mask):
    size = lax.axis_size(axis)
    return lax.ppermute(value, axis, [(i, i ^ mask) for i in range(size)])


def shards(
    byte_ids,
    byte_lengths,
    embedding,
    conv_weight,
    conv_bias,
    score_weight,
    norm_first,
    query_weight,
    key_weight,
    value_weight,
    out_weight,
    rel_bias,
    norm_second,
    gate_weight,
    up_weight,
    down_weight,
    out_grad,
):
    group = byte_ids.shape[1]
    ways = lax.axis_size("tensor")
    total_bytes = group * lax.axis_size("seq")
    count = group // 2
    seq_tokens = total_bytes // 2
    heads = rel_bias.shape[1]
    width = query_weight.shape[1]
    vocab, model = embedding.shape
    units = gate_weight.shape[1]
    piece = count // ways
    query_weight, key_weight, value_weight, rel_bias = (
        item.T for item in (query_weight, key_weight, value_weight, rel_bias)
    )
    steps = -(-total_bytes // (period * chunk_rows))
    rows = steps * chunk_rows
    token_rows = rows * pairs
    chunk_tokens = chunk_rows * pairs

    near = seq_tokens <= 1024
    held = pltpu.VMEM if near else like
    far = pltpu.HBM if near else like
    place = functools.partial(call, near=near)
    table, score_table, bias_score = place(
        prepare_kernel,
        [held((taps * vocab, model), bf16), held((vocab, 128), bf16), held((8, 128), f32)],
        embedding,
        conv_weight,
        score_weight,
        conv_bias,
        specs=[distant] * 4,
        cost=2,
    )

    all_ids = [byte_ids] + [
        exchange(byte_ids, "seq", k) for k in range(1, lax.axis_size("seq"))
    ]
    all_ids[0], score_table = lax.optimization_barrier((all_ids[0], score_table))
    out_weights = copied_out(out_weight)
    pool, spread, total = (jnp.asarray(item, bf16) for item in pool_tables())
    def chunked(item, dims):
        if steps == 1:
            return distant
        at = next(i for i, (a, b) in enumerate(zip(item.shape, dims)) if a != b)
        return pl.BlockSpec(dims, lambda i: tuple(i if d == at else 0 for d in range(len(dims))))

    def chunks(item):
        dims = tuple(
            chunk_rows if d == rows else chunk_tokens if d == token_rows else d
            for d in item.shape
        )
        return chunked(item, dims)

    grid = None if steps == 1 else (steps,)
    gbst_out = [
        held((token_rows, model), bf16),
        far((token_rows, model), bf16),
        far((pairs, rows, taps * vocab), bf16),
        far((rows, 128), f32),
        far((4, rows, 128), f32),
        far((rows, 128), f32),
    ]
    near_tokens, tokens, mixing, coefficients, size_weights, ids = place(
        functools.partial(gbst_kernel, total_bytes, steps, len(all_ids)),
        gbst_out,
        byte_lengths,
        *all_ids,
        table,
        score_table,
        pool,
        spread,
        total,
        conv_bias,
        bias_score,
        specs=[scalars, distant]
        + [local] * (len(all_ids) - 1)
        + [local] * 2
        + [distant] * 4
        + [local],
        out_specs=[chunks(item) for item in gbst_out],
        scratch=[
            pltpu.VMEM((columns, chunk_rows, vocab), bf16),
            pltpu.VMEM((model // 128, chunk_tokens, 128), f32),
            pltpu.VMEM((8 * -(-(total_bytes // 128 + 4) // 8), 128), f32),
            pltpu.VMEM((chunk_rows, 128), bf16),
        ],
        grid=grid,
        cost=6,
    )

    normed, queries, keys, values, probs, attended, own_tokens = place(
        functools.partial(attend_kernel, heads),
        [
            far((seq_tokens, model), bf16),
            far((count, width), bf16),
            far((seq_tokens, width), bf16),
            far((seq_tokens, width), bf16),
            far((heads, count, seq_tokens), bf16),
            held((count, width), bf16),
            held((count, model), bf16),
        ],
        byte_lengths,
        near_tokens,
        norm_first,
        query_weight,
        key_weight,
        value_weight,
        rel_bias,
        specs=[scalars, local] + [whole] * 5,
        cost=4,
    )
    all_attended = copied_out(attended)

    middle, normed_second, inner, grad_gate, grad_up, *normed_parts = place(
        functools.partial(feed_kernel, ways),
        [
            held((count, model), f32),
            held((count, model), bf16),
            held((count, units), bf16),
            held((count, units), bf16),
            held((count, units), bf16),
        ]
        + [held((piece, model), bf16)] * ways,
        *all_attended,
        *out_weights,
        own_tokens,
        norm_second,
        gate_weight,
        up_weight,
        down_weight,
        out_grad,
        specs=[local] * ways + [distant] * ways + [local] + [whole] * 5,
        cost=3,
        scratch=[pltpu.VMEM((count, model), f32)],
    )
    normed_parts = spread_out(normed_parts)
    feed_rows = 3 * model * units // 256
    half = feed_rows // (2 * feed_chunks)
    feed_parts = place(
        functools.partial(feed_grad_kernel, ways, feed_chunks),
        [held((half, 256), bf16)] * (2 * feed_chunks) + [held((piece, model), bf16)] * ways,
        inner,
        normed_second,
        grad_gate,
        grad_up,
        out_grad,
        down_weight,
        specs=[local] * 4 + [whole] * 2,
        cost=1.6,
        scratch=[pltpu.VMEM((count, model), f32), pltpu.VMEM((feed_rows, 256), bf16)],
    )
    feed_parts, encoded = (feed_parts[: 2 * feed_chunks], list(feed_parts[2 * feed_chunks :]))
    normed_parts[0], encoded[0] = lax.optimization_barrier((normed_parts[0], encoded[0]))
    feed_sums = [Staged(*feed_parts[2 * i : 2 * i + 2]) for i in range(feed_chunks)]

    feed_sums[0].add()
    normed_parts[0] = feed_sums[0].before(normed_parts[0])
    feed_sums[0].swap()
    grad_branch, grad_middle, grad_gain_second = place(
        functools.partial(middle_kernel, ways),
        [held((piece, model), bf16), far((piece, model), f32), far((1, model), f32)],
        *normed_parts,
        middle,
        out_grad,
        norm_second,
        specs=[local] * (ways + 1) + [whole] * 2,
    )
    branches = copied_out(grad_branch)
    stack_rows = 4 * width
    weight_keep, weight_send, grad_rel, grad_queries, grad_keys, grad_values = place(
        functools.partial(attend_back_kernel, heads, ways),
        [held((stack_rows // 2, model), bf16)] * 2
        + [far((8, 128), f32)]
        + [far((token_rows, width), bf16)] * 3,
        *branches,
        attended,
        probs,
        queries,
        keys,
        values,
        normed,
        out_weight,
        specs=[local] * ways + [whole] * 7,
        cost=5.4,
        scratch=[pltpu.VMEM((count, model), bf16), pltpu.VMEM((stack_rows, model), bf16)],
    )
    grad_tokens_out = [held((model // 128, token_rows, 128), f32), held((8, model), f32)]
    per_tile = pl.BlockSpec((model // 128, chunk_tokens, 128), lambda i: (0, i, 0))
    grad_tokens, grad_gain_first = place(
        functools.partial(normed_back_kernel, steps, seq_tokens, ways),
        grad_tokens_out,
        grad_queries,
        grad_keys,
        grad_values,
        tokens,
        query_weight,
        key_weight,
        value_weight,
        norm_first,
        grad_middle,
        specs=[chunks(item) for item in (grad_queries, grad_keys, grad_values, tokens)]
        + [distant] * 5,
        out_specs=[whole if steps == 1 else per_tile, whole],
        scratch=[pltpu.VMEM((chunk_tokens, model), f32)],
        grid=grid,
        limit=20,
        cost=4,
    )
    grad_tokens = feed_sums[0].received_before(grad_tokens)
    feed_sums[0].add()
    feed_sums[0].swap()
    packed_rows = 32 * ways * -(-(vocab + taps + 12) // (32 * ways))
    quarter = packed_rows // (2 * ways)
    keep, send = place(
        functools.partial(gbst_back_kernel, total_bytes, steps),
        [held((packed_rows // 2, model), bf16)] * 2,
        grad_tokens,
        grad_gain_first,
        grad_gain_second,
        grad_rel,
        mixing,
        coefficients,
        size_weights,
        ids,
        pool,
        spread,
        total,
        embedding,
        conv_weight,
        conv_bias,
        score_weight,
        specs=[local if steps == 1 else per_tile, local if steps == 1 else whole]
        + [distant] * 2
        + [chunks(item) for item in (mixing, coefficients, size_weights, ids)]
        + [distant] * 7,
        scratch=[
            pltpu.VMEM((columns, chunk_rows, vocab), bf16),
            pltpu.VMEM((taps * vocab, model), f32),
            pltpu.VMEM((vocab, 128), f32),
            pltpu.VMEM((8, model), f32),
            pltpu.VMEM((packed_rows, model), bf16),
            pltpu.VMEM((taps * vocab, model), bf16),
            pltpu.VMEM((chunk_tokens, model), bf16),
            pltpu.VMEM((chunk_tokens, taps * vocab), f32),
            pltpu.VMEM((chunk_rows, 128), f32),
        ],
        grid=grid,
        limit=30,
        cost=12,
    )
    keep, weight_send, *encoded = lax.optimization_barrier((keep, weight_send, *encoded))
    keep = feed_sums[0].received_before(keep)
    weight_sum = Staged(weight_keep, weight_send)
    encoded = spread_out(encoded)
    (own_encoded,) = place(
        functools.partial(encoded_kernel, ways),
        [held((piece, model), bf16)],
        *encoded,
        middle,
        specs=[local] * (ways + 1),
    )
    parts = place(
        deal_kernel,
        [held((quarter, model), bf16)] * ways,
        keep,
        exchange(send, "section", 1),
        specs=[local] * 2,
        scratch=[pltpu.VMEM((packed_rows // 2, model), f32)],
    )
    items = spread_out(parts)
    for mask in seq_masks():
        part = merged(items)
        items = [part, exchange(part, "seq", mask)]
    part = merged(items)
    gathered = copied_out(part)
    gathered = gathered + [exchange(item, "section", 1) for item in gathered]
    grads = place(
        functools.partial(packed_kernel, ways, heads),
        [like((vocab, model), f32), like((taps, model), f32)]
        + [like((model,), f32)] * 4
        + [like((heads, rel_bias.shape[1]), f32)],
        *gathered,
        specs=[local] * len(gathered),
        scratch=[pltpu.VMEM((packed_rows, model), f32)],
    )
    grad_embedding, grad_conv, grad_bias, grad_score, grad_first, grad_second, grad_rel = grads

    (output,) = place(
        functools.partial(assemble_kernel, ways),
        [like((count, model), bf16)],
        *copied_out(own_encoded),
        specs=[local] * ways,
    )

    feed_total = feed_sums[0].finish()
    pieces, names = gather_sum(feed_total, feed_sums[0].halved)
    feed_grads = place(
        functools.partial(feed_weights_kernel, feed_sums[0].halved, names, feed_chunks),
        [like((model, units), f32), like((model, units), f32), like((units, model), f32)],
        *pieces,
        specs=[local] * len(pieces),
        scratch=[pltpu.VMEM((feed_rows, 256), f32)],
    )
    pieces, names = gather_sum(weight_sum.finish(), weight_sum.halved)
    weight_grads = place(
        functools.partial(weights_kernel, weight_sum.halved, names),
        [like((width, model), f32)] * 4,
        *pieces,
        specs=[local] * len(pieces),
        scratch=[pltpu.VMEM((stack_rows, model), f32)],
    )
    return (
        output[None],
        grad_embedding,
        grad_conv,
        grad_bias,
        grad_score,
        grad_first,
        *(item.T for item in weight_grads[:3]),
        weight_grads[3],
        grad_rel.T,
        grad_second,
        *feed_grads,
    )


def solution(mesh):
    return jax.shard_map(
        shards,
        mesh=mesh,
        in_specs=(
            P(None, "seq"),
            P(),
            P(),
            P(),
            P(),
            P(),
            P(),
            P(None, "tensor"),
            P(None, "tensor"),
            P(None, "tensor"),
            P("tensor", None),
            P(None, "tensor"),
            P(),
            P(None, "tensor"),
            P(None, "tensor"),
            P("tensor", None),
            P(None, "seq", None),
        ),
        out_specs=(
            P("section", "seq", None),
            P(),
            P(),
            P(),
            P(),
            P(),
            P(None, "tensor"),
            P(None, "tensor"),
            P(None, "tensor"),
            P("tensor", None),
            P(None, "tensor"),
            P(),
            P(None, "tensor"),
            P(None, "tensor"),
            P("tensor", None),
        ),
        check_vma=False,
    )
```

```python
import functools

import jax
import jax.numpy as jnp
import numpy as np
from jax import lax
from jax.experimental import pallas as pl
from jax.experimental.pallas import tpu as pltpu
from jax.sharding import PartitionSpec as P

epsilon = 1e-06
masked_score = -1e30
far_thresholds = (12, 16, 23, 32, 46, 64, 91)
period = 12
pairs = period // 2
taps = 5
columns = period + taps - 1
chunk_rows = 176
feed_chunks = 1
f32 = jnp.float32
bf16 = jnp.bfloat16
whole = pl.BlockSpec(memory_space=pltpu.VMEM)
local = pl.BlockSpec(memory_space=pltpu.VMEM)
distant = pl.BlockSpec(memory_space=pltpu.VMEM)
scalars = pl.BlockSpec(memory_space=pltpu.SMEM)


def pool_tables():
    pool = np.zeros((128, 384), np.float32)
    spread = np.zeros((512, 128), np.float32)
    total = np.zeros((128, 128), np.float32)
    for size in range(1, 5):
        for g in range(period):
            for r in range(period):
                if r // size == g // size:
                    if size > 1:
                        pool[4 + r, 128 * (size - 2) + 4 + g] = 1.0
                    spread[128 * (size - 1) + 4 + g, period * (g // 2) + r] = 1.0
    for j in range(pairs):
        total[period * j : period * (j + 1), j] = 1.0
    return (pool, spread, total)


def split_mm(a, b, dims=((1,), (0,))):
    high = a.astype(bf16)
    low = (a - high.astype(f32)).astype(bf16)
    return mm(high, b[...], dims) + mm(low, b[...], dims)


def lanes(value, count):
    return [value[:, 128 * i : 128 * (i + 1)] for i in range(count)]


def reached(j):
    found = set()
    for g in (2 * j, 2 * j + 1):
        for size in range(1, 5):
            first = size * (g // size)
            found.update(range(first, first + size))
    return sorted(found)


def exact(a, b, dims=((1,), (0,))):
    return lax.dot_general(
        a, b, (dims, ((), ())), precision=lax.Precision.HIGHEST, preferred_element_type=f32
    )


def mm(a, b, dims=((1,), (0,))):
    return lax.dot_general(a, b, (dims, ((), ())), preferred_element_type=f32)


rows_rows = ((0,), (0,))
cols_cols = ((1,), (1,))


def call(kernel, out, *args, specs=None, scratch=(), grid=None, out_specs=None, near=False, limit=16, cost=1):
    extra = {} if grid is None else {"grid": grid}
    specs = [whole] * len(args) if specs is None else specs
    if near:
        spaces = {id(local): pltpu.VMEM, id(distant): pltpu.HBM}
        args = [
            pltpu.with_memory_space_constraint(arg, spaces[id(spec)]) if id(spec) in spaces else arg
            for arg, spec in zip(args, specs)
        ]
    return pl.pallas_call(
        kernel,
        out_shape=out,
        in_specs=specs,
        out_specs=jax.tree.map(lambda _: whole, out) if out_specs is None else out_specs,
        scratch_shapes=list(scratch),
        cost_estimate=pl.CostEstimate(
            flops=int(cost * 1e9), bytes_accessed=int(cost * 3e6), transcendentals=0
        ),
        compiler_params=pltpu.CompilerParams(
            vmem_limit_bytes=(limit if near else 56) * 2**20
        ),
        **extra,
    )(*args)


def like(shape, kind):
    return jax.ShapeDtypeStruct(shape, kind)


def iota(shape, dim):
    return lax.broadcasted_iota(jnp.int32, shape, dim)


def bucket_of(relative):
    distance = jnp.abs(relative)
    far_bucket = 8 + sum(
        ((distance >= threshold).astype(jnp.int32) for threshold in far_thresholds)
    )
    return jnp.where(distance < 8, distance, far_bucket) + 16 * (relative > 0).astype(jnp.int32)


def bucket_hot(buckets, width, query_first, queries):
    offsets = iota((buckets, width), 1) - (queries - 1) - query_first
    return (bucket_of(offsets) == iota((buckets, width), 0)).astype(f32)


def one_hot(ids, vocab):
    return jnp.where(ids == iota((ids.shape[0], vocab), 1), 1.0, 0.0).astype(bf16)


def head_mask(width, head_dim, head):
    return iota((1, width), 1) // head_dim == head


def as_row(vector):
    return vector[...].astype(f32).reshape(1, vector.shape[0])


def fill_table(embedding, conv_weight, table):
    vocab = embedding.shape[0]
    emb = embedding[...].astype(f32)
    for tap in range(taps):
        row = conv_weight[tap : tap + 1, :].astype(f32)
        table[tap * vocab : (tap + 1) * vocab, :] = (emb * row).astype(bf16)


def prepare_kernel(embedding, conv_weight, score_weight, conv_bias, table, score_table, bias_score):
    emb = embedding[...].astype(f32)
    conv = conv_weight[...].astype(f32)
    score = as_row(score_weight)
    fill_table(embedding, conv_weight, table)
    scored = jnp.concatenate(
        [conv[tap : tap + 1] * score for tap in reversed(range(taps))]
        + [jnp.zeros((128 - taps, conv.shape[1]), f32)],
        axis=0,
    )
    by_byte = exact(emb, scored, cols_cols)
    high = by_byte.astype(bf16).astype(f32)
    middle = (by_byte - high).astype(bf16).astype(f32)
    low = by_byte - high - middle
    score_table[...] = (high + pltpu.roll(middle, 32, 1) + pltpu.roll(low, 64, 1)).astype(bf16)
    bias_score[...] = jnp.broadcast_to(
        jnp.sum(as_row(conv_bias) * score, axis=1, keepdims=True), bias_score.shape
    )


def position_inside(rows, first, total_bytes):
    lane = iota((rows, 128), 1)
    place = period * (first + iota((rows, 128), 0)) + lane - 4
    return (lane >= 4) & (lane < 4 + period) & (place < total_bytes)


def coefficient_inside(rows, first, total_bytes):
    lane = iota((rows, 128), 1)
    place = period * (first + iota((rows, 128), 0)) + lax.rem(lane, period)
    return (lane < period * pairs) & (place < total_bytes)


def laid_out(found_ids, lengths, line, first, rows):
    section, seq = (lax.axis_index("section"), lax.axis_index("seq"))
    count = found_ids[0].shape[1] // 128
    line[...] = jnp.full(line.shape, -1.0, f32)
    for k, item in enumerate(found_ids):
        for at in range(count):
            both = item[:, at * 128 : (at + 1) * 128]
            row = jnp.where(section == 1, both[1:2], both[0:1])
            line[pl.ds((seq ^ k) * count + at + 1, 1), :] = row.astype(f32)
    place = 128 * (iota(line.shape, 0) - 1) + iota(line.shape, 1)
    values = jnp.where(place < lengths[section], line[...], -1.0).astype(bf16)
    shape = (rows, line.shape[0])
    flipped = first + rows - 1 - iota(shape, 0)
    here = (period * flipped + 126) // 128
    found = [
        mm((here + step == iota(shape, 1)).astype(bf16), values) for step in range(2)
    ]
    start = lax.rem(2 - period * (first + rows - 1) + 128 * period * (rows + first), 128)
    for _ in range(period // 4):
        found = [pltpu.roll(item, 0, 1, stride=4, stride_axis=0) for item in found]
    found = [pltpu.roll(item, start, 1) for item in found]
    shape = (rows, 128)
    lane = iota(shape, 1)
    begin = lax.rem(period * (first + rows - 1 - iota(shape, 0)) + 126, 128)
    merged_rows = jnp.where(lane + begin < 128, found[0], found[1]).astype(bf16)
    flip = (iota((rows, rows), 0) + iota((rows, rows), 1) == rows - 1).astype(bf16)
    return mm(flip, merged_rows)


def fill_hot(ids, hot, vocab):
    rows = ids.shape[0]
    value = iota((rows, vocab), 1).astype(f32)
    for r in range(columns):
        found = jnp.where(ids[:, r : r + 1] == value, 1.0, 0.0).astype(bf16)
        hot[r] = found


def fill_mixing(hot, narrow, mixing, vocab):
    rows = narrow.shape[0]

    def mix(step, carry):
        own = pl.ds(pl.multiple_of(step * 16, 16), 16)
        weight = narrow[own, :]
        for j in range(pairs):
            acc = [None] * taps
            for r in reached(j):
                at = period * j + r
                column = jnp.broadcast_to(weight[:, at : at + 1], (16, vocab))
                for tap in range(taps):
                    term = hot[r + tap, own, :] * column
                    acc[tap] = term if acc[tap] is None else acc[tap] + term
            for tap in range(taps):
                mixing[j, own, tap * vocab : (tap + 1) * vocab] = acc[tap]
        return carry

    lax.fori_loop(0, rows // 16, mix, 0, unroll=True)


def gbst_kernel(total_bytes, steps, parts, lengths, *refs):
    found_ids = refs[:parts]
    table, score_table, pool, spread, total, conv_bias, bias_score = refs[parts : parts + 7]
    tokens, kept, coefficients, size_weights, ids = refs[parts + 7 : parts + 12]
    mixing, hot, natural, line, narrow = refs[parts + 12 :]
    rows = ids.shape[0]
    vocab = score_table.shape[0]
    width = table.shape[1]
    first = pl.program_id(0) * rows if steps > 1 else 0
    ids[...] = laid_out(found_ids, lengths, line, first, rows)
    fill_hot(ids, hot, vocab)
    parts = mm(hot[...].reshape(columns * rows, vocab), score_table[...])
    scores = parts[:rows]
    for r in range(1, columns):
        scores = scores + pltpu.roll(parts[r * rows : (r + 1) * rows], r, 1)
    scores = scores + pltpu.roll(scores, 96, 1) + pltpu.roll(scores, 64, 1)
    scores = jnp.where(
        position_inside(rows, first, total_bytes), scores + bias_score[0:1, :], 0.0
    )
    pooled = lanes(split_mm(scores, pool), 3)
    by_size = [scores] + [item * (1.0 / (size + 2)) for size, item in enumerate(pooled)]
    largest = functools.reduce(jnp.maximum, by_size)
    weights = [jnp.exp(item - largest) for item in by_size]
    scale = 1.0 / sum(weights)
    weights = [weight * scale for weight in weights]
    for size in range(4):
        size_weights[size] = weights[size]
    weights = [weight * (0.5 / (size + 1)) for size, weight in enumerate(weights)]
    spread_sum = split_mm(jnp.concatenate(weights, axis=1), spread)
    spread_sum = jnp.where(coefficient_inside(rows, first, total_bytes), spread_sum, 0.0)
    coefficients[...] = spread_sum
    narrow[...] = spread_sum.astype(bf16)
    row_total = split_mm(spread_sum, total)

    fill_mixing(hot, narrow, mixing, vocab)
    bias = as_row(conv_bias)
    by_phase = mm(mixing[...].reshape(pairs * rows, taps * vocab), table[...])
    for j in range(pairs):
        rows_j = by_phase[j * rows : (j + 1) * rows] + row_total[:, j : j + 1] * bias
        for at in range(width // 128):
            natural[at, pl.ds(j, rows, stride=pairs), :] = rows_j[:, at * 128 : (at + 1) * 128]
    for at in range(width // 128):
        tokens[:, at * 128 : (at + 1) * 128] = natural[at].astype(bf16)
    kept[...] = tokens[...]


def attend_kernel(
    heads,
    lengths,
    tokens,
    gain,
    query_weight,
    key_weight,
    value_weight,
    rel_bias,
    normed,
    queries,
    keys,
    values,
    probs,
    attended,
    own_tokens,
):
    seq_tokens = normed.shape[0]
    count, width = queries.shape
    head_dim = width // heads
    query_first = pl.multiple_of(lax.axis_index("seq") * count, count)
    live_tokens = lengths[lax.axis_index("section")]
    own_tokens[...] = tokens[pl.ds(query_first, count), :]
    hidden = tokens[0:seq_tokens, :].astype(f32)
    scale = lax.rsqrt(jnp.mean(hidden * hidden, axis=-1, keepdims=True) + epsilon)
    normed[...] = (hidden * scale * as_row(gain)).astype(bf16)
    keys[...] = mm(normed[...], key_weight[...], cols_cols).astype(bf16)
    values[...] = mm(normed[...], value_weight[...], cols_cols).astype(bf16)
    queries[...] = mm(
        normed[pl.ds(query_first, count), :], query_weight[...], cols_cols
    ).astype(bf16)
    span = seq_tokens + count
    hot = bucket_hot(rel_bias.shape[1], span, query_first, count)
    by_offset = mm(rel_bias[...].astype(f32), hot)
    live = 2 * iota((1, seq_tokens), 1) < live_tokens
    mixed = jnp.zeros((count, width), f32)
    for head in range(heads):
        mask = head_mask(width, head_dim, head)
        row = jnp.broadcast_to(by_offset[head : head + 1, :], (count, span))
        bias = pltpu.roll(row, span - (count - 1), 1, stride=1, stride_axis=0)[:, :seq_tokens]
        own = jnp.where(mask, queries[...], jnp.zeros((), bf16))
        scores = mm(own, keys[...], cols_cols) + bias
        scores = jnp.where(live, scores, masked_score)
        raised = jnp.exp(scores - jnp.max(scores, axis=-1, keepdims=True))
        part = (raised * (1.0 / jnp.sum(raised, axis=-1, keepdims=True))).astype(bf16)
        probs[head] = part
        mixed = jnp.where(mask, mm(part, values[...]), mixed)
    attended[...] = mixed.astype(bf16)


def gelu(value):
    inner = np.float32(np.sqrt(2 / np.pi)) * (value + 0.044715 * (value * value * value))
    return 0.5 * value * (1.0 + jnp.tanh(inner))


def gelu_both(value):
    root = np.float32(np.sqrt(2 / np.pi))
    square = value * value
    tanh = jnp.tanh(root * value * (1.0 + 0.044715 * square))
    half = 0.5 * (1.0 + tanh)
    slope = half + 0.5 * value * (1.0 - tanh * tanh) * root * (1.0 + 3 * 0.044715 * square)
    return (value * half, slope)


def feed_kernel(ways, *refs):
    attended = refs[:ways]
    out_weight = refs[ways : 2 * ways]
    tokens, gain, gate_weight, up_weight, down_weight, out_grad = refs[2 * ways : 2 * ways + 6]
    middle, normed, inner, grad_gate, grad_up = refs[2 * ways + 6 : 2 * ways + 11]
    pieces = refs[2 * ways + 11 : 3 * ways + 11]
    whole_part = refs[3 * ways + 11]
    count = middle.shape[0]
    branch = sum(mm(a[...], w[...]) for a, w in zip(attended, out_weight))
    total = tokens[...].astype(f32) + branch
    middle[...] = total
    scale = lax.rsqrt(jnp.mean(total * total, axis=-1, keepdims=True) + epsilon)
    normed[...] = (total * scale * as_row(gain)).astype(bf16)
    gate = mm(normed[...], gate_weight[...])
    upward = mm(normed[...], up_weight[...])
    grad_inner = mm(out_grad[lax.axis_index("section")], down_weight[...], cols_cols)
    active, slope = gelu_both(gate)
    inner[...] = (active * upward).astype(bf16)
    grad_gate[...] = (grad_inner * upward * slope).astype(bf16)
    grad_up[...] = (grad_inner * active).astype(bf16)
    whole_part[...] = mm(grad_gate[...], gate_weight[...], cols_cols) + mm(
        grad_up[...], up_weight[...], cols_cols
    )
    deal(whole_part, pieces)


def deal(source, pieces):
    piece = pieces[0].shape[0]
    for k, out in enumerate(pieces):
        at = pl.multiple_of((lax.axis_index("tensor") ^ k) * piece, piece)
        out[...] = source[pl.ds(at, piece), :].astype(bf16)


def collect(pieces, target):
    piece = pieces[0].shape[0]
    for k, item in enumerate(pieces):
        at = pl.multiple_of((lax.axis_index("tensor") ^ k) * piece, piece)
        target[pl.ds(at, piece), :] = item[...].astype(target.dtype)


def feed_grad_kernel(chunks, inner, normed, grad_gate, grad_up, out_grad, down_weight, *refs):
    sums, encoded = (refs[: 2 * chunks], refs[2 * chunks])
    stack = refs[2 * chunks + 1]
    first = 0
    for left, right in (
        (normed, grad_gate[...]),
        (normed, grad_up[...]),
        (inner, out_grad[lax.axis_index("section")]),
    ):
        product = mm(left[...], right, rows_rows)
        rows, columns = product.shape
        for at in range(0, columns, 256):
            stack[first : first + rows, :] = product[:, at : at + 256].astype(bf16)
            first += rows
    section = lax.axis_index("section")
    half = first // (2 * chunks)
    for chunk in range(chunks):
        for side, out in enumerate(sums[2 * chunk : 2 * chunk + 2]):
            at = (2 * chunk + (section ^ side)) * half
            out[...] = stack[pl.ds(pl.multiple_of(at, half), half), :]
    encoded[...] = mm(inner[...], down_weight[...]).astype(bf16)


def middle_kernel(ways, *refs):
    pieces = refs[:ways]
    middle, out_grad, gain, grad_branch, grad_middle, grad_gain = refs[ways:]
    piece = pieces[0].shape[0]
    at = pl.multiple_of(lax.axis_index("tensor") * piece, piece)
    grad_normed = sum(item[...].astype(f32) for item in pieces)
    own = middle[pl.ds(at, piece), :]
    scale = lax.rsqrt(jnp.mean(own * own, axis=-1, keepdims=True) + epsilon)
    grad_gain[...] = jnp.sum(grad_normed * own * scale, axis=0, keepdims=True)
    through = grad_normed * as_row(gain)
    total = (
        out_grad[lax.axis_index("section"), pl.ds(at, piece), :].astype(f32)
        + scale * through
        - own * (scale * scale * scale) * jnp.mean(through * own, axis=-1, keepdims=True)
    )
    grad_middle[...] = total
    grad_branch[...] = total.astype(bf16)


def attend_back_kernel(heads, ways, *refs):
    branches = refs[:ways]
    attended, probs, queries, keys, values, normed, out_weight = refs[ways : ways + 7]
    keep, send, rel_grad, grad_queries, grad_keys, grad_values = refs[ways + 7 : ways + 13]
    branch, stack = refs[ways + 13 :]
    count, width = queries.shape
    seq_tokens = keys.shape[0]
    head_dim = width // heads
    collect(branches, branch)
    query_first = pl.multiple_of(lax.axis_index("seq") * count, count)
    grad_attended = mm(branch[...], out_weight[...], cols_cols).astype(bf16)
    stack[3 * width :, :] = mm(attended[...], branch[...], rows_rows).astype(bf16)
    span = seq_tokens + count
    flip = (iota((count, count), 0) + iota((count, count), 1) == count - 1).astype(bf16)
    zero = jnp.zeros((), bf16)
    by_offset = []
    query_sum = jnp.zeros((count, width), f32)
    key_sum = jnp.zeros((seq_tokens, width), f32)
    value_sum = jnp.zeros((seq_tokens, width), f32)
    for head in range(heads):
        mask = head_mask(width, head_dim, head)
        own = jnp.where(mask, grad_attended, zero)
        grad_probs = mm(own, values[...], cols_cols)
        part = probs[head].astype(f32)
        inside = jnp.sum(part * grad_probs, axis=-1, keepdims=True)
        grad_scores = (part * (grad_probs - inside)).astype(bf16)
        flipped = jnp.concatenate(
            [mm(flip, grad_scores), jnp.zeros((count, count), f32)], axis=1
        )
        by_offset.append(
            jnp.sum(pltpu.roll(flipped, 0, 1, stride=1, stride_axis=0), axis=0, keepdims=True)
        )
        query_sum = jnp.where(mask, mm(grad_scores, keys[...]), query_sum)
        key_sum = key_sum + mm(
            grad_scores, jnp.where(mask, queries[...], zero), rows_rows
        )
        value_sum = value_sum + mm(probs[head], own, rows_rows)
    by_offset = jnp.concatenate(by_offset + [jnp.zeros((8 - heads, span), f32)], axis=0)
    hot = bucket_hot(128, span, query_first, count)
    rel_grad[...] = exact(by_offset, hot, cols_cols)
    query_sum = query_sum.astype(bf16)
    stack[0:width, :] = mm(
        query_sum, normed[pl.ds(query_first, count), :], rows_rows
    ).astype(bf16)
    grad_queries[...] = jnp.zeros(grad_queries.shape, bf16)
    grad_queries[pl.ds(query_first, count), :] = query_sum
    rest = grad_keys.shape[0] - seq_tokens
    for at, (total, place) in enumerate(((key_sum, grad_keys), (value_sum, grad_values))):
        total = total.astype(bf16)
        place[0:seq_tokens, :] = total
        place[seq_tokens:, :] = jnp.zeros((rest, width), bf16)
        stack[(at + 1) * width : (at + 2) * width, :] = mm(
            total, normed[...], rows_rows
        ).astype(bf16)
    half = keep.shape[0]
    section = lax.axis_index("section")
    keep[...] = stack[pl.ds(pl.multiple_of(section * half, half), half), :]
    send[...] = stack[pl.ds(pl.multiple_of((1 - section) * half, half), half), :]


def normed_back_kernel(
    steps,
    seq_tokens,
    ways,
    grad_queries,
    grad_keys,
    grad_values,
    tokens,
    query_weight,
    key_weight,
    value_weight,
    gain,
    grad_middle,
    grad_tokens,
    grad_gain,
    whole_part,
):
    token_rows, width = tokens.shape
    step = pl.program_id(0) if steps > 1 else 0
    whole_part[...] = (
        mm(grad_queries[...], query_weight[...])
        + mm(grad_keys[...], key_weight[...])
        + mm(grad_values[...], value_weight[...])
    )
    scale_row = as_row(gain)
    block = 32

    def one(part, total):
        own = pl.ds(pl.multiple_of(part * block, block), block)
        place = token_rows * step + part * block + iota((block, 1), 0)
        hidden = jnp.where(place < seq_tokens, tokens[own, :].astype(f32), 0.0)
        grad_normed = whole_part[own, :]
        scale = lax.rsqrt(jnp.mean(hidden * hidden, axis=-1, keepdims=True) + epsilon)
        against = grad_normed * hidden
        total = total + jnp.sum((against * scale).reshape(block // 8, 8, width), axis=0)
        inner = jnp.mean(against * scale_row, axis=-1, keepdims=True)
        result = scale * (grad_normed * scale_row) - hidden * (scale * scale * scale * inner)
        for at in range(width // 128):
            grad_tokens[at, own, :] = result[:, at * 128 : (at + 1) * 128]
        return total

    total = jnp.zeros((8, width), f32)
    total = lax.fori_loop(0, token_rows // block, one, total, unroll=11)
    total = jnp.sum(total, axis=0, keepdims=True)
    if steps > 1:
        total = total + jnp.where(step == 0, 0.0, grad_gain[0:1, :])
    grad_gain[0:1, :] = total
    piece = grad_middle.shape[0]
    own_first = (lax.axis_index("seq") * ways + lax.axis_index("tensor")) * piece
    own_first = own_first - token_rows * step
    for part in range(piece // block):
        begin = own_first + part * block

        @pl.when((begin >= 0) & (begin < token_rows))
        def _():
            place = pl.ds(pl.multiple_of(begin, block), block)
            rows = grad_middle[part * block : (part + 1) * block, :]
            for at in range(width // 128):
                grad_tokens[at, place, :] += rows[:, at * 128 : (at + 1) * 128]


def middle_back_kernel(heads, ways, seq_tokens, *refs):
    first, second = (refs[: ways + 7], refs[ways + 7 : ways + 13])
    keep, send, rel_grad, grad_tokens, grad_gain = refs[ways + 13 : ways + 18]
    branch, stack, grad_queries, grad_keys, grad_values, whole_part = refs[ways + 18 :]
    grads = (grad_queries, grad_keys, grad_values)
    attend_back_kernel(heads, ways, *first, keep, send, rel_grad, *grads, branch, stack)
    normed_back_kernel(
        1, seq_tokens, ways, *grads, *second, grad_tokens, grad_gain, whole_part
    )


def gbst_back_kernel(
    total_bytes,
    steps,
    grad_tokens,
    grad_gain_first,
    grad_gain_second,
    rel_grad,
    coefficients,
    size_weights,
    ids,
    pool,
    spread,
    total,
    embedding,
    conv_weight,
    conv_bias,
    score_weight,
    keep,
    send,
    hot,
    by_byte,
    by_score,
    small,
    packed,
    table,
    phased,
    against,
    found,
    mixing,
    weights,
):
    rows = ids.shape[0]
    vocab, width = embedding.shape
    step = pl.program_id(0) if steps > 1 else 0
    first = step * rows
    score = as_row(score_weight)
    bias = as_row(conv_bias)

    def at_step(wanted):
        return pl.when(step == wanted) if steps > 1 else lambda run: run()

    @at_step(0)
    def _():
        by_score[...] = jnp.zeros(by_score.shape, f32)
        small[...] = jnp.zeros(small.shape, f32)
        fill_table(embedding, conv_weight, table)

    row_total = split_mm(coefficients[...], total)
    lane = iota((rows, 128), 1)
    on_bias = []
    bias_grad = jnp.zeros((1, width), f32)
    for j in range(pairs):
        grad_rows = jnp.concatenate(
            [grad_tokens[at, pl.ds(j, rows, stride=pairs), :] for at in range(width // 128)],
            axis=1,
        )
        narrow = grad_rows.astype(bf16)
        phased[j * rows : (j + 1) * rows, :] = narrow
        bias_grad = bias_grad + jnp.sum(row_total[:, j : j + 1] * grad_rows, axis=0, keepdims=True)
        on_bias.append(jnp.sum(grad_rows * bias, axis=1, keepdims=True))
    against[...] = mm(phased[...], table[...], cols_cols)
    fill_hot(ids, hot, vocab)
    weights[...] = coefficients[...].astype(bf16)
    fill_mixing(hot, weights, mixing, vocab)
    product = mm(mixing[...].reshape(pairs * rows, taps * vocab), phased[...], rows_rows)
    if steps > 1:
        by_byte[...] = product + jnp.where(step == 0, 0.0, by_byte[...])
    else:
        by_byte[...] = product

    def pick(part, carry):
        own = pl.ds(pl.multiple_of(part * 16, 16), 16)
        spot = iota((16, 128), 1)
        result = jnp.zeros((16, 128), f32)
        for j in range(pairs):
            for r in reached(j):
                begin = pl.ds(pl.multiple_of(j * rows + part * 16, 16), 16)
                picked = sum(
                    hot[r + tap, own, :].astype(f32)
                    * against[begin, tap * vocab : (tap + 1) * vocab]
                    for tap in range(taps)
                )
                result = jnp.where(
                    spot == period * j + r, jnp.sum(picked, axis=1, keepdims=True), result
                )
        found[own, :] = result
        return carry

    lax.fori_loop(0, rows // 16, pick, 0, unroll=True)
    grad_coefficients = found[...]
    for j in range(pairs):
        grad_coefficients = grad_coefficients + jnp.where(lane // period == j, on_bias[j], 0.0)
    grad_coefficients = jnp.where(
        coefficient_inside(rows, first, total_bytes), grad_coefficients, 0.0
    )
    grad_sizes = lanes(split_mm(grad_coefficients, spread, cols_cols), 4)
    grad_sizes = [item * (0.5 / (size + 1)) for size, item in enumerate(grad_sizes)]
    mean_grad = sum(size_weights[size] * grad_sizes[size] for size in range(4))
    by_size = [size_weights[size] * (grad_sizes[size] - mean_grad) for size in range(4)]
    pooled = [item * (1.0 / (size + 2)) for size, item in enumerate(by_size[1:])]
    grad_scores = by_size[0] + split_mm(jnp.concatenate(pooled, axis=1), pool, cols_cols)
    grad_scores = jnp.where(position_inside(rows, first, total_bytes), grad_scores, 0.0)
    score_sum = jnp.sum(jnp.sum(grad_scores, axis=1, keepdims=True), axis=0, keepdims=True)
    small[1:2, :] += bias_grad + score_sum * score
    small[2:3, :] += score_sum * bias
    shifted = []
    for r in range(columns):
        item = pltpu.roll(grad_scores, 128 - r, 1) if r else grad_scores
        shifted.append(jnp.where(lane < taps, item, 0.0).astype(bf16))
    shifted = jnp.concatenate(shifted, axis=0)
    by_score[...] += mm(hot[...].reshape(columns * rows, vocab), shifted, rows_rows)

    @at_step(steps - 1)
    def _():
        emb = embedding[...].astype(f32)
        conv = conv_weight[...].astype(f32)
        grad_embedding = jnp.zeros((vocab, width), f32)
        grad_score = small[2:3, :]
        bytes_score = mm(by_score[...].astype(bf16), embedding[...], rows_rows)
        conv_rows = []
        for tap in range(taps):
            at = taps - 1 - tap
            here = by_byte[tap * vocab : (tap + 1) * vocab, :] + by_score[:, at : at + 1] * score
            grad_embedding = grad_embedding + conv[tap : tap + 1] * here
            conv_rows.append(jnp.sum(emb * here, axis=0, keepdims=True))
            grad_score = grad_score + conv[tap : tap + 1] * bytes_score[at : at + 1, :]
        rest = packed.shape[0] - vocab
        tail = conv_rows + [small[1:2, :], grad_score]
        tail += [grad_gain_first[0:1, :], grad_gain_second[0:1, :]]
        copies = jnp.concatenate([rel_grad[...]] * (width // 128), axis=1)
        own = iota(copies.shape, 1) // 128 == lax.axis_index("tensor")
        tail.append(jnp.where(own, copies, 0.0))
        used = sum(item.shape[0] for item in tail)
        tail = jnp.concatenate(tail + [jnp.zeros((rest - used, width), f32)], axis=0)
        packed[0:vocab, :] = grad_embedding.astype(bf16)
        packed[vocab:, :] = tail.astype(bf16)
        section = lax.axis_index("section")
        half = keep.shape[0]
        for side, out in enumerate((keep, send)):
            out[...] = packed[pl.ds(pl.multiple_of((section ^ side) * half, half), half), :]


def deal_kernel(keep, other, *refs):
    pieces, whole_part = (refs[:-1], refs[-1])
    whole_part[...] = keep[...].astype(f32) + other[...].astype(f32)
    deal(whole_part, pieces)


def copied_out(value):
    return [value] + [exchange(value, "tensor", k) for k in range(1, lax.axis_size("tensor"))]


def spread_out(pieces):
    return [pieces[0]] + [exchange(pieces[k], "tensor", k) for k in range(1, len(pieces))]


def seq_masks():
    return [1 << bit for bit in range(lax.axis_size("seq").bit_length() - 1)]


def merged(items):
    return sum(item.astype(f32) for item in items).astype(bf16)


def half_of(item, bit):
    half = item.shape[0] // 2
    return jnp.where(bit, item[half:], item[:half])


def even(rows):
    return rows % 32 == 0


def sum_over(items, axis, mask, halved):
    if not even(items[0].shape[0]):
        part = merged(items)
        return [part, exchange(part, axis, mask)]
    bit = (lax.axis_index(axis) & mask) != 0
    sent = merged([half_of(item, jnp.logical_not(bit)) for item in items])
    halved.append(mask)
    return [half_of(item, bit) for item in items] + [exchange(sent, axis, mask)]


class Staged:
    def __init__(self, keep, send):
        self.items = [keep, exchange(send, "section", 1)]
        self.masks = seq_masks()
        self.halved = []
        self.sent = None

    def add(self):
        mask = self.masks[0]
        rows = self.items[0].shape[0]
        if even(rows):
            bit = (lax.axis_index("seq") & mask) != 0
            self.sent = merged([half_of(item, jnp.logical_not(bit)) for item in self.items])
            self.items = [half_of(item, bit) for item in self.items]
            self.halved.append(mask)
        else:
            self.sent = merged(self.items)
            self.items = [self.sent]

    def swap(self, extra=None):
        rows = self.sent.shape[0]
        sent = self.sent if extra is None else jnp.concatenate([self.sent, extra], axis=0)
        sent = exchange(sent, "seq", self.masks.pop(0))
        self.items = self.items + [sent[:rows]]
        return sent[rows:]

    def before(self, value):
        self.sent, value = lax.optimization_barrier((self.sent, value))
        return value

    def received_before(self, value):
        self.items[-1], value = lax.optimization_barrier((self.items[-1], value))
        return value

    def finish(self):
        while self.masks:
            self.add()
            self.swap()
        return merged(self.items)


class Encoded:
    def __init__(self, rows):
        self.masks = [1 << bit for bit in range(lax.axis_size("tensor").bit_length() - 1)]
        self.items = [rows]
        self.left = list(self.masks)

    def swap(self):
        mask = self.left.pop(0)
        bit = (lax.axis_index("tensor") & mask) != 0
        blocks = 2 * len(self.left) if self.left else 1
        split = [
            item.reshape(blocks, 2, item.shape[0] // (2 * blocks), item.shape[1])
            for item in self.items
        ]
        shape = (self.items[0].shape[0] // 2, self.items[0].shape[1])
        keep = [jnp.where(bit, item[:, 1], item[:, 0]).reshape(shape) for item in split]
        sent = [jnp.where(bit, item[:, 0], item[:, 1]).reshape(shape) for item in split]
        self.items = keep + [exchange(merged(sent), "tensor", mask)]

    def gather(self):
        mask = self.masks.pop(0)
        self.pieces = [*self.pieces, exchange(jnp.concatenate(self.pieces), "tensor", mask)]


class Gather:
    def __init__(self, total, halved):
        self.pieces = {0: total}
        self.ahead = {}
        self.halved = halved
        self.masks = list(reversed(halved))
        self.arrays, self.holds = ([], [])
        self.done = []

    def swap(self, extra=None):
        mask = self.masks.pop(0)
        arrived = None
        for at in list(self.pieces):
            if at ^ mask in self.ahead:
                self.pieces[at ^ mask] = self.ahead[at ^ mask]
                continue
            sent = self.pieces[at]
            if extra is not None and arrived is None:
                sent = jnp.concatenate([sent, extra], axis=0)
            sent = exchange(sent, "seq", mask)
            if extra is not None and arrived is None:
                rows = self.pieces[at].shape[0]
                arrived, sent = (sent[rows:], sent[:rows])
            self.pieces[at ^ mask] = sent
        return arrived

    def early(self):
        for mask in self.masks:
            self.ahead[mask] = exchange(self.pieces[0], "seq", mask)

    def finish(self):
        while self.masks:
            self.swap()

    def across(self):
        names = [at for at in self.pieces if at not in self.done]
        self.done += names
        array = jnp.concatenate([self.pieces[at] for at in names], axis=0)
        self.arrays += [array, exchange(array, "section", 1)]
        self.holds += [(0, names), (1, names)]
        return self.arrays[-1]


def place_of(halved, at, rows, index):
    first = 0
    size = rows
    for mask in halved:
        size = size // 2
        first = first + jnp.where(((index ^ at) & mask) != 0, size, 0)
    return first


def unstack(arrays, halved, holds, stack):
    section, seq = (lax.axis_index("section"), lax.axis_index("seq"))
    half = stack.shape[0] // 2
    for array, (side, names) in zip(arrays, holds):
        rows = array.shape[0] // len(names)
        for i, name in enumerate(names):
            first = place_of(halved, name, half, seq) + (section ^ side) * half
            part = array[i * rows : (i + 1) * rows, :].astype(f32)
            stack[pl.ds(pl.multiple_of(first, 8), rows), :] = part


def weights_kernel(halved, holds, *refs):
    count = len(holds)
    outs, stack = (refs[count:-1], refs[-1])
    unstack(refs[:count], halved, holds, stack)
    rows = outs[0].shape[0]
    for i, out in enumerate(outs):
        out[...] = stack[i * rows : (i + 1) * rows, :]


def feed_weights_kernel(halved, holds, *refs):
    count = len(holds)
    outs, stack = (refs[count:-1], refs[-1])
    unstack(refs[:count], halved, holds, stack)
    first = 0
    for out in outs:
        rows, columns = out.shape
        for at in range(0, columns, 256):
            out[:, at : at + 256] = stack[first : first + rows, :]
            first += rows


def packed_kernel(ways, heads, *refs):
    pieces, others = (refs[:ways], refs[ways])
    embedding, conv, bias, score, first, second, rel, stack = refs[ways + 1 :]
    rows = pieces[0].shape[0]
    vocab, width = embedding.shape
    section, tensor = (lax.axis_index("section"), lax.axis_index("tensor"))
    for k, item in enumerate(pieces):
        other = others[k * rows : (k + 1) * rows, :]
        for side, rows_k in enumerate((item[...], other)):
            at = ((section ^ side) * ways + (tensor ^ k)) * rows
            stack[pl.ds(pl.multiple_of(at, rows), rows), :] = rows_k.astype(f32)
    embedding[...] = stack[0:vocab, :]
    conv[...] = stack[vocab : vocab + taps, :]
    for i, out in enumerate((bias, score, first, second)):
        out[...] = stack[vocab + taps + i : vocab + taps + i + 1, :].reshape(width)
    at = vocab + taps + 4
    own = stack[at : at + heads, pl.ds(pl.multiple_of(tensor * 128, 128), 128)]
    rel[...] = own[:, : rel.shape[1]]


def encoded_kernel(*refs):
    pieces, middle, out = (refs[:-2], refs[-2], refs[-1])
    piece = out.shape[0]
    at = pl.multiple_of(lax.axis_index("tensor") * piece, piece)
    total = sum(item[...].astype(f32) for item in pieces)
    out[...] = (middle[pl.ds(at, piece), :] + total).astype(bf16)


def assemble_kernel(*refs):
    pieces, out = (refs[:-1], refs[-1])
    rows = pieces[0].shape[0]
    at = 0
    for item in pieces:
        for part in range(item.shape[0] // rows):
            first = pl.multiple_of((lax.axis_index("tensor") ^ at) * rows, rows)
            out[pl.ds(first, rows), :] = item[part * rows : (part + 1) * rows, :]
            at += 1


def exchange(value, axis, mask):
    size = lax.axis_size(axis)
    return lax.ppermute(value, axis, [(i, i ^ mask) for i in range(size)])


def shards(
    byte_ids,
    byte_lengths,
    embedding,
    conv_weight,
    conv_bias,
    score_weight,
    norm_first,
    query_weight,
    key_weight,
    value_weight,
    out_weight,
    rel_bias,
    norm_second,
    gate_weight,
    up_weight,
    down_weight,
    out_grad,
):
    group = byte_ids.shape[1]
    ways = lax.axis_size("tensor")
    total_bytes = group * lax.axis_size("seq")
    count = group // 2
    seq_tokens = total_bytes // 2
    heads = rel_bias.shape[1]
    width = query_weight.shape[1]
    vocab, model = embedding.shape
    units = gate_weight.shape[1]
    piece = count // ways
    query_weight, key_weight, value_weight, rel_bias = (
        item.T for item in (query_weight, key_weight, value_weight, rel_bias)
    )
    steps = -(-total_bytes // (period * chunk_rows))
    rows = steps * chunk_rows
    token_rows = rows * pairs
    chunk_tokens = chunk_rows * pairs

    near = seq_tokens <= 1024
    held = pltpu.VMEM if near else like
    far = pltpu.HBM if near else like
    place = functools.partial(call, near=near)
    table, score_table, bias_score = place(
        prepare_kernel,
        [held((taps * vocab, model), bf16), held((vocab, 128), bf16), held((8, 128), f32)],
        embedding,
        conv_weight,
        score_weight,
        conv_bias,
        specs=[distant] * 4,
        cost=2,
    )

    all_ids = [byte_ids] + [
        exchange(byte_ids, "seq", k) for k in range(1, lax.axis_size("seq"))
    ]
    all_ids[-1], score_table, out_weight = lax.optimization_barrier(
        (all_ids[-1], score_table, out_weight)
    )
    out_weights = copied_out(out_weight)

    pool, spread, total = (jnp.asarray(item, bf16) for item in pool_tables())
    def chunked(item, dims):
        if steps == 1:
            return distant
        at = next(i for i, (a, b) in enumerate(zip(item.shape, dims)) if a != b)
        return pl.BlockSpec(dims, lambda i: tuple(i if d == at else 0 for d in range(len(dims))))

    def chunks(item):
        dims = tuple(
            chunk_rows if d == rows else chunk_tokens if d == token_rows else d
            for d in item.shape
        )
        return chunked(item, dims)

    grid = None if steps == 1 else (steps,)
    gbst_out = [
        held((token_rows, model), bf16),
        far((token_rows, model), bf16),
        far((rows, 128), f32),
        far((4, rows, 128), f32),
        far((rows, 128), f32),
    ]
    near_tokens, tokens, coefficients, size_weights, ids = place(
        functools.partial(gbst_kernel, total_bytes, steps, len(all_ids)),
        gbst_out,
        byte_lengths,
        *all_ids,
        table,
        score_table,
        pool,
        spread,
        total,
        conv_bias,
        bias_score,
        specs=[scalars, distant]
        + [local] * (len(all_ids) + 1)
        + [distant] * 4
        + [local],
        out_specs=[chunks(item) for item in gbst_out],
        scratch=[
            pltpu.VMEM((pairs, chunk_rows, taps * vocab), bf16),
            pltpu.VMEM((columns, chunk_rows, vocab), bf16),
            pltpu.VMEM((model // 128, chunk_tokens, 128), f32),
            pltpu.VMEM((8 * -(-(total_bytes // 128 + 4) // 8), 128), f32),
            pltpu.VMEM((chunk_rows, 128), bf16),
        ],
        grid=grid,
        cost=6,
    )

    normed, queries, keys, values, probs, attended, own_tokens = place(
        functools.partial(attend_kernel, heads),
        [
            far((seq_tokens, model), bf16),
            far((count, width), bf16),
            far((seq_tokens, width), bf16),
            far((seq_tokens, width), bf16),
            far((heads, count, seq_tokens), bf16),
            held((count, width), bf16),
            held((count, model), bf16),
        ],
        byte_lengths,
        near_tokens,
        norm_first,
        query_weight,
        key_weight,
        value_weight,
        rel_bias,
        specs=[scalars, local] + [whole] * 5,
        cost=4,
    )
    attended, *out_weights = lax.optimization_barrier((attended, *out_weights))
    all_attended = copied_out(attended)

    middle, normed_second, inner, grad_gate, grad_up, *normed_parts = place(
        functools.partial(feed_kernel, ways),
        [
            held((count, model), f32),
            held((count, model), bf16),
            held((count, units), bf16),
            held((count, units), bf16),
            held((count, units), bf16),
        ]
        + [held((piece, model), bf16)] * ways,
        *all_attended,
        *out_weights,
        own_tokens,
        norm_second,
        gate_weight,
        up_weight,
        down_weight,
        out_grad,
        specs=[local] * ways + [distant] * ways + [local] + [whole] * 5,
        cost=3,
        scratch=[pltpu.VMEM((count, model), f32)],
    )
    normed_parts = spread_out(normed_parts)
    feed_rows = 3 * model * units // 256
    half = feed_rows // (2 * feed_chunks)
    feed_parts = place(
        functools.partial(feed_grad_kernel, feed_chunks),
        [held((half, 256), bf16)] * (2 * feed_chunks) + [far((count, model), bf16)],
        inner,
        normed_second,
        grad_gate,
        grad_up,
        out_grad,
        down_weight,
        specs=[local] * 4 + [whole] * 2,
        cost=2,
        scratch=[pltpu.VMEM((feed_rows, 256), bf16)],
    )
    feed_parts, encoded = (feed_parts[: 2 * feed_chunks], feed_parts[2 * feed_chunks])
    feed_sums = [Staged(*feed_parts[2 * i : 2 * i + 2]) for i in range(feed_chunks)]

    feed = feed_sums[0]
    feed.add()
    normed_parts[0] = feed.before(normed_parts[0])
    feed.swap()
    grad_branch, grad_middle, grad_gain_second = place(
        functools.partial(middle_kernel, ways),
        [held((piece, model), bf16), far((piece, model), f32), far((1, model), f32)],
        *normed_parts,
        middle,
        out_grad,
        norm_second,
        specs=[local] * (ways + 1) + [whole] * 2,
    )
    branches = copied_out(grad_branch)
    branches[0] = feed.received_before(branches[0])
    feed.add()
    branches[0] = feed.before(branches[0])
    feed.swap()
    stack_rows = 4 * width
    first = (*branches, attended, probs, queries, keys, values, normed, out_weight)
    second = (tokens, query_weight, key_weight, value_weight, norm_first, grad_middle)
    weights_out = [held((stack_rows // 2, model), bf16)] * 2 + [far((8, 128), f32)]
    grads_out = [far((token_rows, width), bf16)] * 3
    grad_tokens_out = [held((model // 128, token_rows, 128), f32), held((8, model), f32)]
    per_tile = pl.BlockSpec((model // 128, chunk_tokens, 128), lambda i: (0, i, 0))
    scratch = [pltpu.VMEM((count, model), bf16), pltpu.VMEM((stack_rows, model), bf16)]
    whole_part = pltpu.VMEM((chunk_tokens, model), f32)
    first_specs = [local] * ways + [distant] * 7
    if steps == 1:
        weight_keep, weight_send, grad_rel, grad_tokens, grad_gain_first = place(
            functools.partial(middle_back_kernel, heads, ways, seq_tokens),
            weights_out + grad_tokens_out,
            *first,
            *second,
            specs=first_specs + [distant] * 6,
            scratch=scratch + [pltpu.VMEM((token_rows, width), bf16)] * 3 + [whole_part],
            limit=30,
            cost=10,
        )
    else:
        weight_keep, weight_send, grad_rel, *grads = place(
            functools.partial(attend_back_kernel, heads, ways),
            weights_out + grads_out,
            *first,
            specs=first_specs,
            scratch=scratch,
        )
        grad_tokens, grad_gain_first = place(
            functools.partial(normed_back_kernel, steps, seq_tokens, ways),
            grad_tokens_out,
            *grads,
            *second,
            specs=[chunks(item) for item in (*grads, tokens)] + [distant] * 5,
            out_specs=[per_tile, whole],
            scratch=[whole_part],
            grid=grid,
        )
    grad_tokens, weight_send, feed.items, encoded = lax.optimization_barrier(
        (grad_tokens, weight_send, feed.items, encoded)
    )
    branch = Encoded(encoded)
    feed_gather = Gather(feed.finish(), feed.halved)
    feed_gather.pieces[0], grad_tokens = lax.optimization_barrier(
        (feed_gather.pieces[0], grad_tokens)
    )
    feed_gather.swap()
    weight_sum = Staged(weight_keep, weight_send)
    weight_sum.add()
    grad_tokens = weight_sum.before(grad_tokens)
    weight_sum.swap()
    branch.swap()
    packed_rows = 32 * ways * -(-(vocab + taps + 12) // (32 * ways))
    quarter = packed_rows // (2 * ways)
    keep, send = place(
        functools.partial(gbst_back_kernel, total_bytes, steps),
        [held((packed_rows // 2, model), bf16)] * 2,
        grad_tokens,
        grad_gain_first,
        grad_gain_second,
        grad_rel,
        coefficients,
        size_weights,
        ids,
        pool,
        spread,
        total,
        embedding,
        conv_weight,
        conv_bias,
        score_weight,
        specs=[local if steps == 1 else per_tile, local if steps == 1 else whole]
        + [distant] * 2
        + [chunks(item) for item in (coefficients, size_weights, ids)]
        + [distant] * 7,
        scratch=[
            pltpu.VMEM((columns, chunk_rows, vocab), bf16),
            pltpu.VMEM((taps * vocab, model), f32),
            pltpu.VMEM((vocab, 128), f32),
            pltpu.VMEM((8, model), f32),
            pltpu.VMEM((packed_rows, model), bf16),
            pltpu.VMEM((taps * vocab, model), bf16),
            pltpu.VMEM((chunk_tokens, model), bf16),
            pltpu.VMEM((chunk_tokens, taps * vocab), f32),
            pltpu.VMEM((chunk_rows, 128), f32),
            pltpu.VMEM((pairs, chunk_rows, taps * vocab), bf16),
            pltpu.VMEM((chunk_rows, 128), bf16),
        ],
        grid=grid,
        limit=30,
        cost=12,
    )
    together = lax.optimization_barrier
    keep, send, feed_gather.pieces, weight_sum.items, branch.items = together(
        (keep, send, feed_gather.pieces, weight_sum.items, branch.items)
    )
    other = exchange(send, "section", 1)
    branch.swap()
    feed_gather.early()
    parts = place(
        deal_kernel,
        [held((quarter, model), bf16)] * ways,
        keep,
        other,
        specs=[local] * 2,
        scratch=[pltpu.VMEM((packed_rows // 2, model), f32)],
    )
    part = merged(spread_out(parts))
    weight_sum.add()
    part, branch.items, weight_sum.sent, weight_sum.items = together(
        (part, branch.items, weight_sum.sent, weight_sum.items)
    )
    masks = seq_masks()
    items = [part, exchange(part, "seq", masks[0])]
    weight_sum.swap()
    (own_encoded,) = place(
        encoded_kernel,
        [held((piece, model), bf16)],
        *branch.items,
        middle,
        specs=[local] * (len(branch.items) + 1),
    )
    branch.pieces = [own_encoded]
    branch.gather()
    items, branch.pieces, feed_gather.pieces, feed_gather.ahead = together(
        (items, branch.pieces, feed_gather.pieces, feed_gather.ahead)
    )
    for mask in masks[1:]:
        part = merged(items)
        items = [part, exchange(part, "seq", mask)]
    feed_gather.finish()
    while branch.masks:
        branch.gather()
    items, weight_sum.items, feed_gather.pieces, branch.pieces = together(
        (items, weight_sum.items, feed_gather.pieces, branch.pieces)
    )
    weight_gather = Gather(weight_sum.finish(), weight_sum.halved)
    weight_gather.swap()
    weight_gather.early()
    part = merged(items)
    gathered = copied_out(part)
    feed_gather.across()
    gathered = [*gathered, exchange(jnp.concatenate(gathered, axis=0), "section", 1)]
    weight_gather.finish()
    weight_gather.across()
    grads = place(
        functools.partial(packed_kernel, ways, heads),
        [like((vocab, model), f32), like((taps, model), f32)]
        + [like((model,), f32)] * 4
        + [like((heads, rel_bias.shape[1]), f32)],
        *gathered,
        specs=[local] * len(gathered),
        scratch=[pltpu.VMEM((packed_rows, model), f32)],
    )

    (output,) = place(
        assemble_kernel,
        [like((count, model), bf16)],
        *branch.pieces,
        specs=[local] * len(branch.pieces),
    )
    feed_grads = place(
        functools.partial(feed_weights_kernel, feed_gather.halved, feed_gather.holds),
        [like((model, units), f32), like((model, units), f32), like((units, model), f32)],
        *feed_gather.arrays,
        specs=[local] * len(feed_gather.arrays),
        scratch=[pltpu.VMEM((feed_rows, 256), f32)],
    )
    weight_gather.arrays, grads, output, feed_grads = together(
        (weight_gather.arrays, grads, output, feed_grads)
    )
    weight_grads = place(
        functools.partial(weights_kernel, weight_gather.halved, weight_gather.holds),
        [like((width, model), f32)] * 4,
        *weight_gather.arrays,
        specs=[local] * len(weight_gather.arrays),
        scratch=[pltpu.VMEM((stack_rows, model), f32)],
    )
    grad_embedding, grad_conv, grad_bias, grad_score, grad_first, grad_second, grad_rel = grads
    return (
        output[None],
        grad_embedding,
        grad_conv,
        grad_bias,
        grad_score,
        grad_first,
        *(item.T for item in weight_grads[:3]),
        weight_grads[3],
        grad_rel.T,
        grad_second,
        *feed_grads,
    )


def solution(mesh):
    return jax.shard_map(
        shards,
        mesh=mesh,
        in_specs=(
            P(None, "seq"),
            P(),
            P(),
            P(),
            P(),
            P(),
            P(),
            P(None, "tensor"),
            P(None, "tensor"),
            P(None, "tensor"),
            P("tensor", None),
            P(None, "tensor"),
            P(),
            P(None, "tensor"),
            P(None, "tensor"),
            P("tensor", None),
            P(None, "seq", None),
        ),
        out_specs=(
            P("section", "seq", None),
            P(),
            P(),
            P(),
            P(),
            P(),
            P(None, "tensor"),
            P(None, "tensor"),
            P(None, "tensor"),
            P("tensor", None),
            P(None, "tensor"),
            P(),
            P(None, "tensor"),
            P(None, "tensor"),
            P("tensor", None),
        ),
        check_vma=False,
    )
```

```python
import functools

import jax
import jax.numpy as jnp
import numpy as np
from jax import lax
from jax.experimental import pallas as pl
from jax.experimental.pallas import tpu as pltpu
from jax.sharding import PartitionSpec as P

epsilon = 1e-06
masked_score = -1e30
far_thresholds = (12, 16, 23, 32, 46, 64, 91)
period = 12
pairs = period // 2
taps = 5
columns = period + taps - 1
chunk_rows = 176
feed_chunks = 1
f32 = jnp.float32
bf16 = jnp.bfloat16
whole = pl.BlockSpec(memory_space=pltpu.VMEM)
local = pl.BlockSpec(memory_space=pltpu.VMEM)
distant = pl.BlockSpec(memory_space=pltpu.VMEM)
scalars = pl.BlockSpec(memory_space=pltpu.SMEM)


def pool_tables():
    pool = np.zeros((128, 384), np.float32)
    spread = np.zeros((512, 128), np.float32)
    total = np.zeros((128, 128), np.float32)
    for size in range(1, 5):
        for g in range(period):
            for r in range(period):
                if r // size == g // size:
                    if size > 1:
                        pool[4 + r, 128 * (size - 2) + 4 + g] = 1.0
                    spread[128 * (size - 1) + 4 + g, period * (g // 2) + r] = 1.0
    for j in range(pairs):
        total[period * j : period * (j + 1), j] = 1.0
    return (pool, spread, total)


def split_mm(a, b, dims=((1,), (0,))):
    high = a.astype(bf16)
    low = (a - high.astype(f32)).astype(bf16)
    return mm(high, b[...], dims) + mm(low, b[...], dims)


def lanes(value, count):
    return [value[:, 128 * i : 128 * (i + 1)] for i in range(count)]


def reached(j):
    found = set()
    for g in (2 * j, 2 * j + 1):
        for size in range(1, 5):
            first = size * (g // size)
            found.update(range(first, first + size))
    return sorted(found)


def exact(a, b, dims=((1,), (0,))):
    return lax.dot_general(
        a, b, (dims, ((), ())), precision=lax.Precision.HIGHEST, preferred_element_type=f32
    )


def mm(a, b, dims=((1,), (0,))):
    return lax.dot_general(a, b, (dims, ((), ())), preferred_element_type=f32)


rows_rows = ((0,), (0,))
cols_cols = ((1,), (1,))


def call(kernel, out, *args, specs=None, scratch=(), grid=None, out_specs=None, near=False, limit=16, cost=1):
    extra = {} if grid is None else {"grid": grid}
    specs = [whole] * len(args) if specs is None else specs
    if near:
        spaces = {id(local): pltpu.VMEM, id(distant): pltpu.HBM}
        args = [
            pltpu.with_memory_space_constraint(arg, spaces[id(spec)]) if id(spec) in spaces else arg
            for arg, spec in zip(args, specs)
        ]
    return pl.pallas_call(
        kernel,
        out_shape=out,
        in_specs=specs,
        out_specs=jax.tree.map(lambda _: whole, out) if out_specs is None else out_specs,
        scratch_shapes=list(scratch),
        cost_estimate=pl.CostEstimate(
            flops=int(cost * 1e9), bytes_accessed=int(cost * 3e6), transcendentals=0
        ),
        compiler_params=pltpu.CompilerParams(
            vmem_limit_bytes=(limit if near else 56) * 2**20
        ),
        **extra,
    )(*args)


def like(shape, kind):
    return jax.ShapeDtypeStruct(shape, kind)


def iota(shape, dim):
    return lax.broadcasted_iota(jnp.int32, shape, dim)


def bucket_of(relative):
    distance = jnp.abs(relative)
    far_bucket = 8 + sum(
        ((distance >= threshold).astype(jnp.int32) for threshold in far_thresholds)
    )
    return jnp.where(distance < 8, distance, far_bucket) + 16 * (relative > 0).astype(jnp.int32)


def bucket_hot(buckets, width, query_first, queries):
    offsets = iota((buckets, width), 1) - (queries - 1) - query_first
    return (bucket_of(offsets) == iota((buckets, width), 0)).astype(f32)


def one_hot(ids, vocab):
    return jnp.where(ids == iota((ids.shape[0], vocab), 1), 1.0, 0.0).astype(bf16)


def head_mask(width, head_dim, head):
    return iota((1, width), 1) // head_dim == head


def as_row(vector):
    return vector[...].astype(f32).reshape(1, vector.shape[0])


def fill_table(embedding, conv_weight, table):
    vocab = embedding.shape[0]
    emb = embedding[...].astype(f32)
    for tap in range(taps):
        row = conv_weight[tap : tap + 1, :].astype(f32)
        table[tap * vocab : (tap + 1) * vocab, :] = (emb * row).astype(bf16)


def prepare_kernel(embedding, conv_weight, score_weight, conv_bias, table, score_table, bias_score):
    emb = embedding[...].astype(f32)
    conv = conv_weight[...].astype(f32)
    score = as_row(score_weight)
    fill_table(embedding, conv_weight, table)
    scored = jnp.concatenate(
        [conv[tap : tap + 1] * score for tap in reversed(range(taps))]
        + [jnp.zeros((128 - taps, conv.shape[1]), f32)],
        axis=0,
    )
    by_byte = exact(emb, scored, cols_cols)
    high = by_byte.astype(bf16).astype(f32)
    middle = (by_byte - high).astype(bf16).astype(f32)
    low = by_byte - high - middle
    score_table[...] = (high + pltpu.roll(middle, 32, 1) + pltpu.roll(low, 64, 1)).astype(bf16)
    bias_score[...] = jnp.broadcast_to(
        jnp.sum(as_row(conv_bias) * score, axis=1, keepdims=True), bias_score.shape
    )


def position_inside(rows, first, total_bytes):
    lane = iota((rows, 128), 1)
    place = period * (first + iota((rows, 128), 0)) + lane - 4
    return (lane >= 4) & (lane < 4 + period) & (place < total_bytes)


def coefficient_inside(rows, first, total_bytes):
    lane = iota((rows, 128), 1)
    place = period * (first + iota((rows, 128), 0)) + lax.rem(lane, period)
    return (lane < period * pairs) & (place < total_bytes)


def laid_out(found_ids, lengths, line, first, rows):
    section, seq = (lax.axis_index("section"), lax.axis_index("seq"))
    count = found_ids[0].shape[1] // 128
    line[...] = jnp.full(line.shape, -1.0, f32)
    for k, item in enumerate(found_ids):
        for at in range(count):
            both = item[:, at * 128 : (at + 1) * 128]
            row = jnp.where(section == 1, both[1:2], both[0:1])
            line[pl.ds((seq ^ k) * count + at + 1, 1), :] = row.astype(f32)
    place = 128 * (iota(line.shape, 0) - 1) + iota(line.shape, 1)
    values = jnp.where(place < lengths[section], line[...], -1.0).astype(bf16)
    shape = (rows, line.shape[0])
    flipped = first + rows - 1 - iota(shape, 0)
    here = (period * flipped + 126) // 128
    found = [
        mm((here + step == iota(shape, 1)).astype(bf16), values) for step in range(2)
    ]
    start = lax.rem(2 - period * (first + rows - 1) + 128 * period * (rows + first), 128)
    for _ in range(period // 4):
        found = [pltpu.roll(item, 0, 1, stride=4, stride_axis=0) for item in found]
    found = [pltpu.roll(item, start, 1) for item in found]
    shape = (rows, 128)
    lane = iota(shape, 1)
    begin = lax.rem(period * (first + rows - 1 - iota(shape, 0)) + 126, 128)
    merged_rows = jnp.where(lane + begin < 128, found[0], found[1]).astype(bf16)
    flip = (iota((rows, rows), 0) + iota((rows, rows), 1) == rows - 1).astype(bf16)
    return mm(flip, merged_rows)


def fill_hot(ids, hot, vocab):
    rows = ids.shape[0]
    value = iota((rows, vocab), 1).astype(f32)
    for r in range(columns):
        found = jnp.where(ids[:, r : r + 1] == value, 1.0, 0.0).astype(bf16)
        hot[r] = found


def fill_mixing(hot, narrow, mixing, vocab):
    rows = narrow.shape[0]

    def mix(step, carry):
        own = pl.ds(pl.multiple_of(step * 16, 16), 16)
        weight = narrow[own, :]
        for j in range(pairs):
            acc = [None] * taps
            for r in reached(j):
                at = period * j + r
                column = jnp.broadcast_to(weight[:, at : at + 1], (16, vocab))
                for tap in range(taps):
                    term = hot[r + tap, own, :] * column
                    acc[tap] = term if acc[tap] is None else acc[tap] + term
            for tap in range(taps):
                mixing[j, own, tap * vocab : (tap + 1) * vocab] = acc[tap]
        return carry

    lax.fori_loop(0, rows // 16, mix, 0, unroll=True)


def gbst_kernel(total_bytes, steps, parts, lengths, *refs):
    found_ids = refs[:parts]
    table, score_table, pool, spread, total, conv_bias, bias_score = refs[parts : parts + 7]
    tokens, kept, coefficients, size_weights, ids = refs[parts + 7 : parts + 12]
    mixing, hot, natural, line, narrow = refs[parts + 12 :]
    rows = ids.shape[0]
    vocab = score_table.shape[0]
    width = table.shape[1]
    first = pl.program_id(0) * rows if steps > 1 else 0
    ids[...] = laid_out(found_ids, lengths, line, first, rows)
    fill_hot(ids, hot, vocab)
    parts = mm(hot[...].reshape(columns * rows, vocab), score_table[...])
    scores = parts[:rows]
    for r in range(1, columns):
        scores = scores + pltpu.roll(parts[r * rows : (r + 1) * rows], r, 1)
    scores = scores + pltpu.roll(scores, 96, 1) + pltpu.roll(scores, 64, 1)
    scores = jnp.where(
        position_inside(rows, first, total_bytes), scores + bias_score[0:1, :], 0.0
    )
    pooled = lanes(split_mm(scores, pool), 3)
    by_size = [scores] + [item * (1.0 / (size + 2)) for size, item in enumerate(pooled)]
    largest = functools.reduce(jnp.maximum, by_size)
    weights = [jnp.exp(item - largest) for item in by_size]
    scale = 1.0 / sum(weights)
    weights = [weight * scale for weight in weights]
    for size in range(4):
        size_weights[size] = weights[size]
    weights = [weight * (0.5 / (size + 1)) for size, weight in enumerate(weights)]
    spread_sum = split_mm(jnp.concatenate(weights, axis=1), spread)
    spread_sum = jnp.where(coefficient_inside(rows, first, total_bytes), spread_sum, 0.0)
    coefficients[...] = spread_sum
    narrow[...] = spread_sum.astype(bf16)
    row_total = split_mm(spread_sum, total)

    fill_mixing(hot, narrow, mixing, vocab)
    bias = as_row(conv_bias)
    by_phase = mm(mixing[...].reshape(pairs * rows, taps * vocab), table[...])
    for j in range(pairs):
        rows_j = by_phase[j * rows : (j + 1) * rows] + row_total[:, j : j + 1] * bias
        for at in range(width // 128):
            natural[at, pl.ds(j, rows, stride=pairs), :] = rows_j[:, at * 128 : (at + 1) * 128]
    for at in range(width // 128):
        tokens[:, at * 128 : (at + 1) * 128] = natural[at].astype(bf16)
    kept[...] = tokens[...]


def attend_kernel(
    heads,
    lengths,
    tokens,
    gain,
    query_weight,
    key_weight,
    value_weight,
    rel_bias,
    normed,
    queries,
    keys,
    values,
    probs,
    attended,
    own_tokens,
):
    seq_tokens = normed.shape[0]
    count, width = queries.shape
    head_dim = width // heads
    query_first = pl.multiple_of(lax.axis_index("seq") * count, count)
    live_tokens = lengths[lax.axis_index("section")]
    own_tokens[...] = tokens[pl.ds(query_first, count), :]
    hidden = tokens[0:seq_tokens, :].astype(f32)
    scale = lax.rsqrt(jnp.mean(hidden * hidden, axis=-1, keepdims=True) + epsilon)
    normed[...] = (hidden * scale * as_row(gain)).astype(bf16)
    keys[...] = mm(normed[...], key_weight[...], cols_cols).astype(bf16)
    values[...] = mm(normed[...], value_weight[...], cols_cols).astype(bf16)
    queries[...] = mm(
        normed[pl.ds(query_first, count), :], query_weight[...], cols_cols
    ).astype(bf16)
    span = seq_tokens + count
    hot = bucket_hot(rel_bias.shape[1], span, query_first, count)
    by_offset = mm(rel_bias[...].astype(f32), hot)
    live = 2 * iota((1, seq_tokens), 1) < live_tokens
    mixed = jnp.zeros((count, width), f32)
    for head in range(heads):
        mask = head_mask(width, head_dim, head)
        row = jnp.broadcast_to(by_offset[head : head + 1, :], (count, span))
        bias = pltpu.roll(row, span - (count - 1), 1, stride=1, stride_axis=0)[:, :seq_tokens]
        own = jnp.where(mask, queries[...], jnp.zeros((), bf16))
        scores = mm(own, keys[...], cols_cols) + bias
        scores = jnp.where(live, scores, masked_score)
        raised = jnp.exp(scores - jnp.max(scores, axis=-1, keepdims=True))
        part = (raised * (1.0 / jnp.sum(raised, axis=-1, keepdims=True))).astype(bf16)
        probs[head] = part
        mixed = jnp.where(mask, mm(part, values[...]), mixed)
    attended[...] = mixed.astype(bf16)


def gelu(value):
    inner = np.float32(np.sqrt(2 / np.pi)) * (value + 0.044715 * (value * value * value))
    return 0.5 * value * (1.0 + jnp.tanh(inner))


def gelu_both(value):
    root = np.float32(np.sqrt(2 / np.pi))
    square = value * value
    tanh = jnp.tanh(root * value * (1.0 + 0.044715 * square))
    half = 0.5 * (1.0 + tanh)
    slope = half + 0.5 * value * (1.0 - tanh * tanh) * root * (1.0 + 3 * 0.044715 * square)
    return (value * half, slope)


def feed_kernel(ways, *refs):
    attended = refs[:ways]
    out_weight = refs[ways : 2 * ways]
    tokens, gain, gate_weight, up_weight, down_weight, out_grad = refs[2 * ways : 2 * ways + 6]
    middle, normed, inner, grad_gate, grad_up = refs[2 * ways + 6 : 2 * ways + 11]
    pieces = refs[2 * ways + 11 : 3 * ways + 11]
    whole_part = refs[3 * ways + 11]
    count = middle.shape[0]
    branch = sum(mm(a[...], w[...]) for a, w in zip(attended, out_weight))
    total = tokens[...].astype(f32) + branch
    middle[...] = total
    scale = lax.rsqrt(jnp.mean(total * total, axis=-1, keepdims=True) + epsilon)
    normed[...] = (total * scale * as_row(gain)).astype(bf16)
    gate = mm(normed[...], gate_weight[...])
    upward = mm(normed[...], up_weight[...])
    grad_inner = mm(out_grad[lax.axis_index("section")], down_weight[...], cols_cols)
    active, slope = gelu_both(gate)
    inner[...] = (active * upward).astype(bf16)
    grad_gate[...] = (grad_inner * upward * slope).astype(bf16)
    grad_up[...] = (grad_inner * active).astype(bf16)
    whole_part[...] = mm(grad_gate[...], gate_weight[...], cols_cols) + mm(
        grad_up[...], up_weight[...], cols_cols
    )
    deal(whole_part, pieces)


def deal(source, pieces):
    piece = pieces[0].shape[0]
    for k, out in enumerate(pieces):
        at = pl.multiple_of((lax.axis_index("tensor") ^ k) * piece, piece)
        out[...] = source[pl.ds(at, piece), :].astype(bf16)


def collect(pieces, target):
    piece = pieces[0].shape[0]
    for k, item in enumerate(pieces):
        at = pl.multiple_of((lax.axis_index("tensor") ^ k) * piece, piece)
        target[pl.ds(at, piece), :] = item[...].astype(target.dtype)


def feed_grad_kernel(chunks, inner, normed, grad_gate, grad_up, out_grad, down_weight, *refs):
    sums, encoded = (refs[: 2 * chunks], refs[2 * chunks])
    stack = refs[2 * chunks + 1]
    first = 0
    for left, right in (
        (normed, grad_gate[...]),
        (normed, grad_up[...]),
        (inner, out_grad[lax.axis_index("section")]),
    ):
        product = mm(left[...], right, rows_rows)
        rows, columns = product.shape
        for at in range(0, columns, 256):
            stack[first : first + rows, :] = product[:, at : at + 256].astype(bf16)
            first += rows
    section = lax.axis_index("section")
    half = first // (2 * chunks)
    for chunk in range(chunks):
        for side, out in enumerate(sums[2 * chunk : 2 * chunk + 2]):
            at = (2 * chunk + (section ^ side)) * half
            out[...] = stack[pl.ds(pl.multiple_of(at, half), half), :]
    encoded[...] = mm(inner[...], down_weight[...]).astype(bf16)


def middle_kernel(ways, *refs):
    pieces = refs[:ways]
    middle, out_grad, gain, grad_branch, grad_middle, grad_gain = refs[ways:]
    piece = pieces[0].shape[0]
    at = pl.multiple_of(lax.axis_index("tensor") * piece, piece)
    grad_normed = sum(item[...].astype(f32) for item in pieces)
    own = middle[pl.ds(at, piece), :]
    scale = lax.rsqrt(jnp.mean(own * own, axis=-1, keepdims=True) + epsilon)
    grad_gain[...] = jnp.sum(grad_normed * own * scale, axis=0, keepdims=True)
    through = grad_normed * as_row(gain)
    total = (
        out_grad[lax.axis_index("section"), pl.ds(at, piece), :].astype(f32)
        + scale * through
        - own * (scale * scale * scale) * jnp.mean(through * own, axis=-1, keepdims=True)
    )
    grad_middle[...] = total
    grad_branch[...] = total.astype(bf16)


def attend_back_kernel(heads, ways, *refs):
    branches = refs[:ways]
    attended, probs, queries, keys, values, normed, out_weight = refs[ways : ways + 7]
    keep, send, rel_grad, grad_queries, grad_keys, grad_values = refs[ways + 7 : ways + 13]
    branch, stack = refs[ways + 13 :]
    count, width = queries.shape
    seq_tokens = keys.shape[0]
    head_dim = width // heads
    collect(branches, branch)
    query_first = pl.multiple_of(lax.axis_index("seq") * count, count)
    grad_attended = mm(branch[...], out_weight[...], cols_cols).astype(bf16)
    stack[3 * width :, :] = mm(attended[...], branch[...], rows_rows).astype(bf16)
    span = seq_tokens + count
    flip = (iota((count, count), 0) + iota((count, count), 1) == count - 1).astype(bf16)
    zero = jnp.zeros((), bf16)
    by_offset = []
    query_sum = jnp.zeros((count, width), f32)
    key_sum = jnp.zeros((seq_tokens, width), f32)
    value_sum = jnp.zeros((seq_tokens, width), f32)
    for head in range(heads):
        mask = head_mask(width, head_dim, head)
        own = jnp.where(mask, grad_attended, zero)
        grad_probs = mm(own, values[...], cols_cols)
        part = probs[head].astype(f32)
        inside = jnp.sum(part * grad_probs, axis=-1, keepdims=True)
        grad_scores = (part * (grad_probs - inside)).astype(bf16)
        flipped = jnp.concatenate(
            [mm(flip, grad_scores), jnp.zeros((count, count), f32)], axis=1
        )
        by_offset.append(
            jnp.sum(pltpu.roll(flipped, 0, 1, stride=1, stride_axis=0), axis=0, keepdims=True)
        )
        query_sum = jnp.where(mask, mm(grad_scores, keys[...]), query_sum)
        key_sum = key_sum + mm(
            grad_scores, jnp.where(mask, queries[...], zero), rows_rows
        )
        value_sum = value_sum + mm(probs[head], own, rows_rows)
    by_offset = jnp.concatenate(by_offset + [jnp.zeros((8 - heads, span), f32)], axis=0)
    hot = bucket_hot(128, span, query_first, count)
    rel_grad[...] = exact(by_offset, hot, cols_cols)
    query_sum = query_sum.astype(bf16)
    stack[0:width, :] = mm(
        query_sum, normed[pl.ds(query_first, count), :], rows_rows
    ).astype(bf16)
    grad_queries[...] = jnp.zeros(grad_queries.shape, bf16)
    grad_queries[pl.ds(query_first, count), :] = query_sum
    rest = grad_keys.shape[0] - seq_tokens
    for at, (total, place) in enumerate(((key_sum, grad_keys), (value_sum, grad_values))):
        total = total.astype(bf16)
        place[0:seq_tokens, :] = total
        place[seq_tokens:, :] = jnp.zeros((rest, width), bf16)
        stack[(at + 1) * width : (at + 2) * width, :] = mm(
            total, normed[...], rows_rows
        ).astype(bf16)
    half = keep.shape[0]
    section = lax.axis_index("section")
    keep[...] = stack[pl.ds(pl.multiple_of(section * half, half), half), :]
    send[...] = stack[pl.ds(pl.multiple_of((1 - section) * half, half), half), :]


def normed_back_kernel(
    steps,
    seq_tokens,
    ways,
    grad_queries,
    grad_keys,
    grad_values,
    tokens,
    query_weight,
    key_weight,
    value_weight,
    gain,
    grad_middle,
    grad_tokens,
    grad_gain,
    whole_part,
):
    token_rows, width = tokens.shape
    step = pl.program_id(0) if steps > 1 else 0
    whole_part[...] = (
        mm(grad_queries[...], query_weight[...])
        + mm(grad_keys[...], key_weight[...])
        + mm(grad_values[...], value_weight[...])
    )
    scale_row = as_row(gain)
    block = 32

    def one(part, total):
        own = pl.ds(pl.multiple_of(part * block, block), block)
        place = token_rows * step + part * block + iota((block, 1), 0)
        hidden = jnp.where(place < seq_tokens, tokens[own, :].astype(f32), 0.0)
        grad_normed = whole_part[own, :]
        scale = lax.rsqrt(jnp.mean(hidden * hidden, axis=-1, keepdims=True) + epsilon)
        against = grad_normed * hidden
        total = total + jnp.sum((against * scale).reshape(block // 8, 8, width), axis=0)
        inner = jnp.mean(against * scale_row, axis=-1, keepdims=True)
        result = scale * (grad_normed * scale_row) - hidden * (scale * scale * scale * inner)
        for at in range(width // 128):
            grad_tokens[at, own, :] = result[:, at * 128 : (at + 1) * 128]
        return total

    total = jnp.zeros((8, width), f32)
    total = lax.fori_loop(0, token_rows // block, one, total, unroll=11)
    total = jnp.sum(total, axis=0, keepdims=True)
    if steps > 1:
        total = total + jnp.where(step == 0, 0.0, grad_gain[0:1, :])
    grad_gain[0:1, :] = total
    piece = grad_middle.shape[0]
    own_first = (lax.axis_index("seq") * ways + lax.axis_index("tensor")) * piece
    own_first = own_first - token_rows * step
    for part in range(piece // block):
        begin = own_first + part * block

        @pl.when((begin >= 0) & (begin < token_rows))
        def _():
            place = pl.ds(pl.multiple_of(begin, block), block)
            rows = grad_middle[part * block : (part + 1) * block, :]
            for at in range(width // 128):
                grad_tokens[at, place, :] += rows[:, at * 128 : (at + 1) * 128]


def middle_back_kernel(heads, ways, seq_tokens, *refs):
    first, second = (refs[: ways + 7], refs[ways + 7 : ways + 13])
    keep, send, rel_grad, grad_tokens, grad_gain = refs[ways + 13 : ways + 18]
    branch, stack, grad_queries, grad_keys, grad_values, whole_part = refs[ways + 18 :]
    grads = (grad_queries, grad_keys, grad_values)
    attend_back_kernel(heads, ways, *first, keep, send, rel_grad, *grads, branch, stack)
    normed_back_kernel(
        1, seq_tokens, ways, *grads, *second, grad_tokens, grad_gain, whole_part
    )


def gbst_back_kernel(
    total_bytes,
    steps,
    grad_tokens,
    grad_gain_first,
    grad_gain_second,
    rel_grad,
    coefficients,
    size_weights,
    ids,
    pool,
    spread,
    total,
    embedding,
    conv_weight,
    conv_bias,
    score_weight,
    keep,
    send,
    hot,
    by_byte,
    by_score,
    small,
    packed,
    table,
    phased,
    against,
    found,
    mixing,
    weights,
):
    rows = ids.shape[0]
    vocab, width = embedding.shape
    step = pl.program_id(0) if steps > 1 else 0
    first = step * rows
    score = as_row(score_weight)
    bias = as_row(conv_bias)

    def at_step(wanted):
        return pl.when(step == wanted) if steps > 1 else lambda run: run()

    @at_step(0)
    def _():
        by_score[...] = jnp.zeros(by_score.shape, f32)
        small[...] = jnp.zeros(small.shape, f32)
        fill_table(embedding, conv_weight, table)

    row_total = split_mm(coefficients[...], total)
    lane = iota((rows, 128), 1)
    on_bias = []
    bias_grad = jnp.zeros((1, width), f32)
    for j in range(pairs):
        grad_rows = jnp.concatenate(
            [grad_tokens[at, pl.ds(j, rows, stride=pairs), :] for at in range(width // 128)],
            axis=1,
        )
        narrow = grad_rows.astype(bf16)
        phased[j * rows : (j + 1) * rows, :] = narrow
        bias_grad = bias_grad + jnp.sum(row_total[:, j : j + 1] * grad_rows, axis=0, keepdims=True)
        on_bias.append(jnp.sum(grad_rows * bias, axis=1, keepdims=True))
    against[...] = mm(phased[...], table[...], cols_cols)
    fill_hot(ids, hot, vocab)
    weights[...] = coefficients[...].astype(bf16)
    fill_mixing(hot, weights, mixing, vocab)
    product = mm(mixing[...].reshape(pairs * rows, taps * vocab), phased[...], rows_rows)
    if steps > 1:
        by_byte[...] = product + jnp.where(step == 0, 0.0, by_byte[...])
    else:
        by_byte[...] = product

    def pick(part, carry):
        own = pl.ds(pl.multiple_of(part * 16, 16), 16)
        spot = iota((16, 128), 1)
        result = jnp.zeros((16, 128), f32)
        for j in range(pairs):
            for r in reached(j):
                begin = pl.ds(pl.multiple_of(j * rows + part * 16, 16), 16)
                picked = sum(
                    hot[r + tap, own, :].astype(f32)
                    * against[begin, tap * vocab : (tap + 1) * vocab]
                    for tap in range(taps)
                )
                result = jnp.where(
                    spot == period * j + r, jnp.sum(picked, axis=1, keepdims=True), result
                )
        found[own, :] = result
        return carry

    lax.fori_loop(0, rows // 16, pick, 0, unroll=True)
    grad_coefficients = found[...]
    for j in range(pairs):
        grad_coefficients = grad_coefficients + jnp.where(lane // period == j, on_bias[j], 0.0)
    grad_coefficients = jnp.where(
        coefficient_inside(rows, first, total_bytes), grad_coefficients, 0.0
    )
    grad_sizes = lanes(split_mm(grad_coefficients, spread, cols_cols), 4)
    grad_sizes = [item * (0.5 / (size + 1)) for size, item in enumerate(grad_sizes)]
    mean_grad = sum(size_weights[size] * grad_sizes[size] for size in range(4))
    by_size = [size_weights[size] * (grad_sizes[size] - mean_grad) for size in range(4)]
    pooled = [item * (1.0 / (size + 2)) for size, item in enumerate(by_size[1:])]
    grad_scores = by_size[0] + split_mm(jnp.concatenate(pooled, axis=1), pool, cols_cols)
    grad_scores = jnp.where(position_inside(rows, first, total_bytes), grad_scores, 0.0)
    score_sum = jnp.sum(jnp.sum(grad_scores, axis=1, keepdims=True), axis=0, keepdims=True)
    small[1:2, :] += bias_grad + score_sum * score
    small[2:3, :] += score_sum * bias
    shifted = []
    for r in range(columns):
        item = pltpu.roll(grad_scores, 128 - r, 1) if r else grad_scores
        shifted.append(jnp.where(lane < taps, item, 0.0).astype(bf16))
    shifted = jnp.concatenate(shifted, axis=0)
    by_score[...] += mm(hot[...].reshape(columns * rows, vocab), shifted, rows_rows)

    @at_step(steps - 1)
    def _():
        emb = embedding[...].astype(f32)
        conv = conv_weight[...].astype(f32)
        grad_embedding = jnp.zeros((vocab, width), f32)
        grad_score = small[2:3, :]
        bytes_score = mm(by_score[...].astype(bf16), embedding[...], rows_rows)
        conv_rows = []
        for tap in range(taps):
            at = taps - 1 - tap
            here = by_byte[tap * vocab : (tap + 1) * vocab, :] + by_score[:, at : at + 1] * score
            grad_embedding = grad_embedding + conv[tap : tap + 1] * here
            conv_rows.append(jnp.sum(emb * here, axis=0, keepdims=True))
            grad_score = grad_score + conv[tap : tap + 1] * bytes_score[at : at + 1, :]
        rest = packed.shape[0] - vocab
        tail = conv_rows + [small[1:2, :], grad_score]
        tail += [grad_gain_first[0:1, :], grad_gain_second[0:1, :]]
        copies = jnp.concatenate([rel_grad[...]] * (width // 128), axis=1)
        own = iota(copies.shape, 1) // 128 == lax.axis_index("tensor")
        tail.append(jnp.where(own, copies, 0.0))
        used = sum(item.shape[0] for item in tail)
        tail = jnp.concatenate(tail + [jnp.zeros((rest - used, width), f32)], axis=0)
        packed[0:vocab, :] = grad_embedding.astype(bf16)
        packed[vocab:, :] = tail.astype(bf16)
        section = lax.axis_index("section")
        half = keep.shape[0]
        for side, out in enumerate((keep, send)):
            out[...] = packed[pl.ds(pl.multiple_of((section ^ side) * half, half), half), :]


def deal_kernel(keep, other, *refs):
    pieces, whole_part = (refs[:-1], refs[-1])
    whole_part[...] = keep[...].astype(f32) + other[...].astype(f32)
    deal(whole_part, pieces)


def copied_out(value):
    return [value] + [exchange(value, "tensor", k) for k in range(1, lax.axis_size("tensor"))]


def spread_out(pieces):
    return [pieces[0]] + [exchange(pieces[k], "tensor", k) for k in range(1, len(pieces))]


def seq_masks():
    return [1 << bit for bit in range(lax.axis_size("seq").bit_length() - 1)]


def merged(items):
    return sum(item.astype(f32) for item in items).astype(bf16)


def half_of(item, bit):
    half = item.shape[0] // 2
    return jnp.where(bit, item[half:], item[:half])


def even(rows):
    return rows % 32 == 0


def sum_over(items, axis, mask, halved):
    if not even(items[0].shape[0]):
        part = merged(items)
        return [part, exchange(part, axis, mask)]
    bit = (lax.axis_index(axis) & mask) != 0
    sent = merged([half_of(item, jnp.logical_not(bit)) for item in items])
    halved.append(mask)
    return [half_of(item, bit) for item in items] + [exchange(sent, axis, mask)]


class Staged:
    def __init__(self, keep, send):
        self.items = [keep, exchange(send, "section", 1)]
        self.masks = seq_masks()
        self.halved = []
        self.sent = None

    def add(self):
        mask = self.masks[0]
        rows = self.items[0].shape[0]
        if even(rows):
            bit = (lax.axis_index("seq") & mask) != 0
            self.sent = merged([half_of(item, jnp.logical_not(bit)) for item in self.items])
            self.items = [half_of(item, bit) for item in self.items]
            self.halved.append(mask)
        else:
            self.sent = merged(self.items)
            self.items = [self.sent]

    def swap(self, extra=None):
        rows = self.sent.shape[0]
        sent = self.sent if extra is None else jnp.concatenate([self.sent, extra], axis=0)
        sent = exchange(sent, "seq", self.masks.pop(0))
        self.items = self.items + [sent[:rows]]
        return sent[rows:]

    def before(self, value):
        self.sent, value = lax.optimization_barrier((self.sent, value))
        return value

    def received_before(self, value):
        self.items[-1], value = lax.optimization_barrier((self.items[-1], value))
        return value

    def finish(self):
        while self.masks:
            self.add()
            self.swap()
        return merged(self.items)


class Encoded:
    def __init__(self, rows):
        self.masks = [1 << bit for bit in range(lax.axis_size("tensor").bit_length() - 1)]
        self.items = [rows]
        self.left = list(self.masks)

    def swap(self):
        mask = self.left.pop(0)
        bit = (lax.axis_index("tensor") & mask) != 0
        blocks = 2 * len(self.left) if self.left else 1
        split = [
            item.reshape(blocks, 2, item.shape[0] // (2 * blocks), item.shape[1])
            for item in self.items
        ]
        shape = (self.items[0].shape[0] // 2, self.items[0].shape[1])
        keep = [jnp.where(bit, item[:, 1], item[:, 0]).reshape(shape) for item in split]
        sent = [jnp.where(bit, item[:, 0], item[:, 1]).reshape(shape) for item in split]
        self.items = keep + [exchange(merged(sent), "tensor", mask)]

    def gather(self):
        mask = self.masks.pop(0)
        self.pieces = [*self.pieces, exchange(jnp.concatenate(self.pieces), "tensor", mask)]


class Gather:
    def __init__(self, total, halved):
        self.pieces = {0: total}
        self.ahead = {}
        self.halved = halved
        self.masks = list(reversed(halved))
        self.arrays, self.holds = ([], [])
        self.done = []

    def swap(self, extra=None):
        mask = self.masks.pop(0)
        arrived = None
        for at in list(self.pieces):
            if at ^ mask in self.ahead:
                self.pieces[at ^ mask] = self.ahead[at ^ mask]
                continue
            sent = self.pieces[at]
            if extra is not None and arrived is None:
                sent = jnp.concatenate([sent, extra], axis=0)
            sent = exchange(sent, "seq", mask)
            if extra is not None and arrived is None:
                rows = self.pieces[at].shape[0]
                arrived, sent = (sent[rows:], sent[:rows])
            self.pieces[at ^ mask] = sent
        return arrived

    def early(self):
        for mask in self.masks:
            self.ahead[mask] = exchange(self.pieces[0], "seq", mask)

    def finish(self):
        while self.masks:
            self.swap()

    def across(self):
        names = [at for at in self.pieces if at not in self.done]
        self.done += names
        array = jnp.concatenate([self.pieces[at] for at in names], axis=0)
        self.arrays += [array, exchange(array, "section", 1)]
        self.holds += [(0, names), (1, names)]
        return self.arrays[-1]


def place_of(halved, at, rows, index):
    first = 0
    size = rows
    for mask in halved:
        size = size // 2
        first = first + jnp.where(((index ^ at) & mask) != 0, size, 0)
    return first


def unstack(arrays, halved, holds, stack):
    section, seq = (lax.axis_index("section"), lax.axis_index("seq"))
    half = stack.shape[0] // 2
    for array, (side, names) in zip(arrays, holds):
        rows = array.shape[0] // len(names)
        for i, name in enumerate(names):
            first = place_of(halved, name, half, seq) + (section ^ side) * half
            part = array[i * rows : (i + 1) * rows, :].astype(f32)
            stack[pl.ds(pl.multiple_of(first, 8), rows), :] = part


def weights_kernel(halved, holds, *refs):
    count = len(holds)
    outs, stack = (refs[count:-1], refs[-1])
    unstack(refs[:count], halved, holds, stack)
    rows = outs[0].shape[0]
    for i, out in enumerate(outs):
        out[...] = stack[i * rows : (i + 1) * rows, :]


def feed_weights_kernel(halved, holds, *refs):
    count = len(holds)
    outs, stack = (refs[count:-1], refs[-1])
    unstack(refs[:count], halved, holds, stack)
    first = 0
    for out in outs:
        rows, columns = out.shape
        for at in range(0, columns, 256):
            out[:, at : at + 256] = stack[first : first + rows, :]
            first += rows


def packed_kernel(ways, heads, *refs):
    pieces, others = (refs[:ways], refs[ways])
    embedding, conv, bias, score, first, second, rel, stack = refs[ways + 1 :]
    rows = pieces[0].shape[0]
    vocab, width = embedding.shape
    section, tensor = (lax.axis_index("section"), lax.axis_index("tensor"))
    for k, item in enumerate(pieces):
        other = others[k * rows : (k + 1) * rows, :]
        for side, rows_k in enumerate((item[...], other)):
            at = ((section ^ side) * ways + (tensor ^ k)) * rows
            stack[pl.ds(pl.multiple_of(at, rows), rows), :] = rows_k.astype(f32)
    embedding[...] = stack[0:vocab, :]
    conv[...] = stack[vocab : vocab + taps, :]
    for i, out in enumerate((bias, score, first, second)):
        out[...] = stack[vocab + taps + i : vocab + taps + i + 1, :].reshape(width)
    at = vocab + taps + 4
    own = stack[at : at + heads, pl.ds(pl.multiple_of(tensor * 128, 128), 128)]
    rel[...] = own[:, : rel.shape[1]]


def encoded_kernel(*refs):
    pieces, middle, out = (refs[:-2], refs[-2], refs[-1])
    piece = out.shape[0]
    at = pl.multiple_of(lax.axis_index("tensor") * piece, piece)
    total = sum(item[...].astype(f32) for item in pieces)
    out[...] = (middle[pl.ds(at, piece), :] + total).astype(bf16)


def assemble_kernel(*refs):
    pieces, out = (refs[:-1], refs[-1])
    rows = pieces[0].shape[0]
    at = 0
    for item in pieces:
        for part in range(item.shape[0] // rows):
            first = pl.multiple_of((lax.axis_index("tensor") ^ at) * rows, rows)
            out[pl.ds(first, rows), :] = item[part * rows : (part + 1) * rows, :]
            at += 1


def exchange(value, axis, mask):
    size = lax.axis_size(axis)
    return lax.ppermute(value, axis, [(i, i ^ mask) for i in range(size)])


def shards(
    byte_ids,
    byte_lengths,
    embedding,
    conv_weight,
    conv_bias,
    score_weight,
    norm_first,
    query_weight,
    key_weight,
    value_weight,
    out_weight,
    rel_bias,
    norm_second,
    gate_weight,
    up_weight,
    down_weight,
    out_grad,
):
    group = byte_ids.shape[1]
    ways = lax.axis_size("tensor")
    total_bytes = group * lax.axis_size("seq")
    count = group // 2
    seq_tokens = total_bytes // 2
    heads = rel_bias.shape[1]
    width = query_weight.shape[1]
    vocab, model = embedding.shape
    units = gate_weight.shape[1]
    piece = count // ways
    query_weight, key_weight, value_weight, rel_bias = (
        item.T for item in (query_weight, key_weight, value_weight, rel_bias)
    )
    steps = -(-total_bytes // (period * chunk_rows))
    rows = steps * chunk_rows
    token_rows = rows * pairs
    chunk_tokens = chunk_rows * pairs

    near = seq_tokens <= 1024
    held = pltpu.VMEM if near else like
    far = pltpu.HBM if near else like
    place = functools.partial(call, near=near)
    table, score_table, bias_score = place(
        prepare_kernel,
        [held((taps * vocab, model), bf16), held((vocab, 128), bf16), held((8, 128), f32)],
        embedding,
        conv_weight,
        score_weight,
        conv_bias,
        specs=[distant] * 4,
        cost=2,
    )

    all_ids = [byte_ids] + [
        exchange(byte_ids, "seq", k) for k in range(1, lax.axis_size("seq"))
    ]
    score_table, out_weight = lax.optimization_barrier((score_table, out_weight))
    out_weights = copied_out(out_weight)

    pool, spread, total = (jnp.asarray(item, bf16) for item in pool_tables())
    def chunked(item, dims):
        if steps == 1:
            return distant
        at = next(i for i, (a, b) in enumerate(zip(item.shape, dims)) if a != b)
        return pl.BlockSpec(dims, lambda i: tuple(i if d == at else 0 for d in range(len(dims))))

    def chunks(item):
        dims = tuple(
            chunk_rows if d == rows else chunk_tokens if d == token_rows else d
            for d in item.shape
        )
        return chunked(item, dims)

    grid = None if steps == 1 else (steps,)
    gbst_out = [
        held((token_rows, model), bf16),
        far((token_rows, model), bf16),
        far((rows, 128), f32),
        far((4, rows, 128), f32),
        far((rows, 128), f32),
    ]
    near_tokens, tokens, coefficients, size_weights, ids = place(
        functools.partial(gbst_kernel, total_bytes, steps, len(all_ids)),
        gbst_out,
        byte_lengths,
        *all_ids,
        table,
        score_table,
        pool,
        spread,
        total,
        conv_bias,
        bias_score,
        specs=[scalars, distant]
        + [local] * (len(all_ids) + 1)
        + [distant] * 4
        + [local],
        out_specs=[chunks(item) for item in gbst_out],
        scratch=[
            pltpu.VMEM((pairs, chunk_rows, taps * vocab), bf16),
            pltpu.VMEM((columns, chunk_rows, vocab), bf16),
            pltpu.VMEM((model // 128, chunk_tokens, 128), f32),
            pltpu.VMEM((8 * -(-(total_bytes // 128 + 4) // 8), 128), f32),
            pltpu.VMEM((chunk_rows, 128), bf16),
        ],
        grid=grid,
        cost=6,
    )

    normed, queries, keys, values, probs, attended, own_tokens = place(
        functools.partial(attend_kernel, heads),
        [
            far((seq_tokens, model), bf16),
            far((count, width), bf16),
            far((seq_tokens, width), bf16),
            far((seq_tokens, width), bf16),
            far((heads, count, seq_tokens), bf16),
            held((count, width), bf16),
            held((count, model), bf16),
        ],
        byte_lengths,
        near_tokens,
        norm_first,
        query_weight,
        key_weight,
        value_weight,
        rel_bias,
        specs=[scalars, local] + [whole] * 5,
        cost=4,
    )
    attended, *out_weights = lax.optimization_barrier((attended, *out_weights))
    all_attended = copied_out(attended)

    middle, normed_second, inner, grad_gate, grad_up, *normed_parts = place(
        functools.partial(feed_kernel, ways),
        [
            held((count, model), f32),
            held((count, model), bf16),
            held((count, units), bf16),
            held((count, units), bf16),
            held((count, units), bf16),
        ]
        + [held((piece, model), bf16)] * ways,
        *all_attended,
        *out_weights,
        own_tokens,
        norm_second,
        gate_weight,
        up_weight,
        down_weight,
        out_grad,
        specs=[local] * ways + [distant] * ways + [local, distant] + [whole] * 4,
        cost=3,
        scratch=[pltpu.VMEM((count, model), f32)],
    )
    normed_parts = spread_out(normed_parts)
    feed_rows = 3 * model * units // 256
    half = feed_rows // (2 * feed_chunks)
    feed_parts = place(
        functools.partial(feed_grad_kernel, feed_chunks),
        [held((half, 256), bf16)] * (2 * feed_chunks) + [far((count, model), bf16)],
        inner,
        normed_second,
        grad_gate,
        grad_up,
        out_grad,
        down_weight,
        specs=[local] * 4 + [whole] * 2,
        cost=2,
        scratch=[pltpu.VMEM((feed_rows, 256), bf16)],
    )
    feed_parts, encoded = (feed_parts[: 2 * feed_chunks], feed_parts[2 * feed_chunks])
    feed_sums = [Staged(*feed_parts[2 * i : 2 * i + 2]) for i in range(feed_chunks)]

    feed = feed_sums[0]
    feed.add()
    normed_parts[0] = feed.before(normed_parts[0])
    feed.swap()
    grad_branch, grad_middle, grad_gain_second = place(
        functools.partial(middle_kernel, ways),
        [held((piece, model), bf16), far((piece, model), f32), far((1, model), f32)],
        *normed_parts,
        middle,
        out_grad,
        norm_second,
        specs=[local] * (ways + 1) + [whole, distant],
    )
    branches = copied_out(grad_branch)
    branches[0] = feed.received_before(branches[0])
    feed.add()
    branches[0] = feed.before(branches[0])
    feed.swap()
    stack_rows = 4 * width
    first = (*branches, attended, probs, queries, keys, values, normed, out_weight)
    second = (tokens, query_weight, key_weight, value_weight, norm_first, grad_middle)
    weights_out = [held((stack_rows // 2, model), bf16)] * 2 + [far((8, 128), f32)]
    grads_out = [far((token_rows, width), bf16)] * 3
    grad_tokens_out = [held((model // 128, token_rows, 128), f32), held((8, model), f32)]
    per_tile = pl.BlockSpec((model // 128, chunk_tokens, 128), lambda i: (0, i, 0))
    scratch = [pltpu.VMEM((count, model), bf16), pltpu.VMEM((stack_rows, model), bf16)]
    whole_part = pltpu.VMEM((chunk_tokens, model), f32)
    first_specs = [local] * ways + [distant] * 7
    if steps == 1:
        weight_keep, weight_send, grad_rel, grad_tokens, grad_gain_first = place(
            functools.partial(middle_back_kernel, heads, ways, seq_tokens),
            weights_out + grad_tokens_out,
            *first,
            *second,
            specs=first_specs + [distant] * 6,
            scratch=scratch + [pltpu.VMEM((token_rows, width), bf16)] * 3 + [whole_part],
            limit=30,
            cost=10,
        )
    else:
        weight_keep, weight_send, grad_rel, *grads = place(
            functools.partial(attend_back_kernel, heads, ways),
            weights_out + grads_out,
            *first,
            specs=first_specs,
            scratch=scratch,
        )
        grad_tokens, grad_gain_first = place(
            functools.partial(normed_back_kernel, steps, seq_tokens, ways),
            grad_tokens_out,
            *grads,
            *second,
            specs=[chunks(item) for item in (*grads, tokens)] + [distant] * 5,
            out_specs=[per_tile, whole],
            scratch=[whole_part],
            grid=grid,
        )
    grad_tokens, weight_send, feed.items, encoded = lax.optimization_barrier(
        (grad_tokens, weight_send, feed.items, encoded)
    )
    branch = Encoded(encoded)
    feed_gather = Gather(feed.finish(), feed.halved)
    feed_gather.pieces[0], grad_tokens = lax.optimization_barrier(
        (feed_gather.pieces[0], grad_tokens)
    )
    feed_gather.swap()
    weight_sum = Staged(weight_keep, weight_send)
    weight_sum.add()
    grad_tokens = weight_sum.before(grad_tokens)
    weight_sum.swap()
    branch.swap()
    packed_rows = 32 * ways * -(-(vocab + taps + 12) // (32 * ways))
    quarter = packed_rows // (2 * ways)
    keep, send = place(
        functools.partial(gbst_back_kernel, total_bytes, steps),
        [held((packed_rows // 2, model), bf16)] * 2,
        grad_tokens,
        grad_gain_first,
        grad_gain_second,
        grad_rel,
        coefficients,
        size_weights,
        ids,
        pool,
        spread,
        total,
        embedding,
        conv_weight,
        conv_bias,
        score_weight,
        specs=[local if steps == 1 else per_tile, local if steps == 1 else whole]
        + [distant] * 2
        + [chunks(item) for item in (coefficients, size_weights, ids)]
        + [distant] * 7,
        scratch=[
            pltpu.VMEM((columns, chunk_rows, vocab), bf16),
            pltpu.VMEM((taps * vocab, model), f32),
            pltpu.VMEM((vocab, 128), f32),
            pltpu.VMEM((8, model), f32),
            pltpu.VMEM((packed_rows, model), bf16),
            pltpu.VMEM((taps * vocab, model), bf16),
            pltpu.VMEM((chunk_tokens, model), bf16),
            pltpu.VMEM((chunk_tokens, taps * vocab), f32),
            pltpu.VMEM((chunk_rows, 128), f32),
            pltpu.VMEM((pairs, chunk_rows, taps * vocab), bf16),
            pltpu.VMEM((chunk_rows, 128), bf16),
        ],
        grid=grid,
        limit=30,
        cost=12,
    )
    together = lax.optimization_barrier
    keep, send, feed_gather.pieces, weight_sum.items, branch.items = together(
        (keep, send, feed_gather.pieces, weight_sum.items, branch.items)
    )
    other = exchange(send, "section", 1)
    branch.swap()
    feed_gather.early()
    parts = place(
        deal_kernel,
        [held((quarter, model), bf16)] * ways,
        keep,
        other,
        specs=[local] * 2,
        scratch=[pltpu.VMEM((packed_rows // 2, model), f32)],
    )
    part = merged(spread_out(parts))
    weight_sum.add()
    part, branch.items, weight_sum.sent, weight_sum.items = together(
        (part, branch.items, weight_sum.sent, weight_sum.items)
    )
    masks = seq_masks()
    items = [part, exchange(part, "seq", masks[0])]
    weight_sum.swap()
    (own_encoded,) = place(
        encoded_kernel,
        [held((piece, model), bf16)],
        *branch.items,
        middle,
        specs=[local] * (len(branch.items) + 1),
    )
    branch.pieces = [own_encoded]
    branch.gather()
    items, branch.pieces, feed_gather.pieces, feed_gather.ahead = together(
        (items, branch.pieces, feed_gather.pieces, feed_gather.ahead)
    )
    for mask in masks[1:]:
        part = merged(items)
        items = [part, exchange(part, "seq", mask)]
    feed_gather.finish()
    while branch.masks:
        branch.gather()
    items, weight_sum.items, feed_gather.pieces, branch.pieces = together(
        (items, weight_sum.items, feed_gather.pieces, branch.pieces)
    )
    weight_gather = Gather(weight_sum.finish(), weight_sum.halved)
    weight_gather.swap()
    weight_gather.early()
    part = merged(items)
    gathered = copied_out(part)
    feed_gather.across()
    weight_gather.pieces = together((weight_gather.pieces, gathered))[0]
    gathered = [*gathered, exchange(jnp.concatenate(gathered, axis=0), "section", 1)]
    (output,) = place(
        assemble_kernel,
        [like((count, model), bf16)],
        *branch.pieces,
        specs=[local] * len(branch.pieces),
    )
    feed_grads = place(
        functools.partial(feed_weights_kernel, feed_gather.halved, feed_gather.holds),
        [like((model, units), f32), like((model, units), f32), like((units, model), f32)],
        *feed_gather.arrays,
        specs=[local] * len(feed_gather.arrays),
        scratch=[pltpu.VMEM((feed_rows, 256), f32)],
    )
    weight_gather.finish()
    weight_gather.pieces, feed_grads, output = together(
        (weight_gather.pieces, feed_grads, output)
    )
    weight_gather.across()
    grads = place(
        functools.partial(packed_kernel, ways, heads),
        [like((vocab, model), f32), like((taps, model), f32)]
        + [like((model,), f32)] * 4
        + [like((heads, rel_bias.shape[1]), f32)],
        *gathered,
        specs=[local] * len(gathered),
        scratch=[pltpu.VMEM((packed_rows, model), f32)],
    )

    weight_gather.arrays, grads, output, feed_grads = together(
        (weight_gather.arrays, grads, output, feed_grads)
    )
    weight_grads = place(
        functools.partial(weights_kernel, weight_gather.halved, weight_gather.holds),
        [like((width, model), f32)] * 4,
        *weight_gather.arrays,
        specs=[local] * len(weight_gather.arrays),
        scratch=[pltpu.VMEM((stack_rows, model), f32)],
    )
    grad_embedding, grad_conv, grad_bias, grad_score, grad_first, grad_second, grad_rel = grads
    return (
        output[None],
        grad_embedding,
        grad_conv,
        grad_bias,
        grad_score,
        grad_first,
        *(item.T for item in weight_grads[:3]),
        weight_grads[3],
        grad_rel.T,
        grad_second,
        *feed_grads,
    )


def solution(mesh):
    return jax.shard_map(
        shards,
        mesh=mesh,
        in_specs=(
            P(None, "seq"),
            P(),
            P(),
            P(),
            P(),
            P(),
            P(),
            P(None, "tensor"),
            P(None, "tensor"),
            P(None, "tensor"),
            P("tensor", None),
            P(None, "tensor"),
            P(),
            P(None, "tensor"),
            P(None, "tensor"),
            P("tensor", None),
            P(None, "seq", None),
        ),
        out_specs=(
            P("section", "seq", None),
            P(),
            P(),
            P(),
            P(),
            P(),
            P(None, "tensor"),
            P(None, "tensor"),
            P(None, "tensor"),
            P("tensor", None),
            P(None, "tensor"),
            P(),
            P(None, "tensor"),
            P(None, "tensor"),
            P("tensor", None),
        ),
        check_vma=False,
    )
```

```python
import functools

import jax
import jax.numpy as jnp
import numpy as np
from jax import lax
from jax.experimental import pallas as pl
from jax.experimental.pallas import tpu as pltpu
from jax.sharding import PartitionSpec as P

epsilon = 1e-06
masked_score = -1e30
far_thresholds = (12, 16, 23, 32, 46, 64, 91)
period = 12
pairs = period // 2
taps = 5
columns = period + taps - 1
chunk_rows = 176
feed_chunks = 1
f32 = jnp.float32
bf16 = jnp.bfloat16
whole = pl.BlockSpec(memory_space=pltpu.VMEM)
local = pl.BlockSpec(memory_space=pltpu.VMEM)
distant = pl.BlockSpec(memory_space=pltpu.VMEM)
scalars = pl.BlockSpec(memory_space=pltpu.SMEM)


def pool_tables():
    pool = np.zeros((128, 384), np.float32)
    spread = np.zeros((512, 128), np.float32)
    total = np.zeros((128, 128), np.float32)
    for size in range(1, 5):
        for g in range(period):
            for r in range(period):
                if r // size == g // size:
                    if size > 1:
                        pool[4 + r, 128 * (size - 2) + 4 + g] = 1.0
                    spread[128 * (size - 1) + 4 + g, period * (g // 2) + r] = 1.0
    for j in range(pairs):
        total[period * j : period * (j + 1), j] = 1.0
    return (pool, spread, total)


def split_mm(a, b, dims=((1,), (0,))):
    high = a.astype(bf16)
    low = (a - high.astype(f32)).astype(bf16)
    return mm(high, b[...], dims) + mm(low, b[...], dims)


def lanes(value, count):
    return [value[:, 128 * i : 128 * (i + 1)] for i in range(count)]


def reached(j):
    found = set()
    for g in (2 * j, 2 * j + 1):
        for size in range(1, 5):
            first = size * (g // size)
            found.update(range(first, first + size))
    return sorted(found)


def exact(a, b, dims=((1,), (0,))):
    return lax.dot_general(
        a, b, (dims, ((), ())), precision=lax.Precision.HIGHEST, preferred_element_type=f32
    )


def mm(a, b, dims=((1,), (0,))):
    return lax.dot_general(a, b, (dims, ((), ())), preferred_element_type=f32)


rows_rows = ((0,), (0,))
cols_cols = ((1,), (1,))


def call(kernel, out, *args, specs=None, scratch=(), grid=None, out_specs=None, near=False, limit=16, cost=1):
    extra = {} if grid is None else {"grid": grid}
    specs = [whole] * len(args) if specs is None else specs
    if near:
        spaces = {id(local): pltpu.VMEM, id(distant): pltpu.HBM}
        args = [
            pltpu.with_memory_space_constraint(arg, spaces[id(spec)]) if id(spec) in spaces else arg
            for arg, spec in zip(args, specs)
        ]
    return pl.pallas_call(
        kernel,
        out_shape=out,
        in_specs=specs,
        out_specs=jax.tree.map(lambda _: whole, out) if out_specs is None else out_specs,
        scratch_shapes=list(scratch),
        cost_estimate=pl.CostEstimate(
            flops=int(cost * 1e9), bytes_accessed=int(cost * 3e6), transcendentals=0
        ),
        compiler_params=pltpu.CompilerParams(
            vmem_limit_bytes=(limit if near else 56) * 2**20
        ),
        **extra,
    )(*args)


def like(shape, kind):
    return jax.ShapeDtypeStruct(shape, kind)


def iota(shape, dim):
    return lax.broadcasted_iota(jnp.int32, shape, dim)


def bucket_of(relative):
    distance = jnp.abs(relative)
    far_bucket = 8 + sum(
        ((distance >= threshold).astype(jnp.int32) for threshold in far_thresholds)
    )
    return jnp.where(distance < 8, distance, far_bucket) + 16 * (relative > 0).astype(jnp.int32)


def bucket_hot(buckets, width, query_first, queries):
    offsets = iota((buckets, width), 1) - (queries - 1) - query_first
    return (bucket_of(offsets) == iota((buckets, width), 0)).astype(f32)


def one_hot(ids, vocab):
    return jnp.where(ids == iota((ids.shape[0], vocab), 1), 1.0, 0.0).astype(bf16)


def head_mask(width, head_dim, head):
    return iota((1, width), 1) // head_dim == head


def as_row(vector):
    return vector[...].astype(f32).reshape(1, vector.shape[0])


def fill_table(embedding, conv_weight, table):
    vocab = embedding.shape[0]
    emb = embedding[...].astype(f32)
    for tap in range(taps):
        row = conv_weight[tap : tap + 1, :].astype(f32)
        table[tap * vocab : (tap + 1) * vocab, :] = (emb * row).astype(bf16)


def prepare_kernel(embedding, conv_weight, score_weight, conv_bias, table, score_table, bias_score):
    emb = embedding[...].astype(f32)
    conv = conv_weight[...].astype(f32)
    score = as_row(score_weight)
    fill_table(embedding, conv_weight, table)
    scored = jnp.concatenate(
        [conv[tap : tap + 1] * score for tap in reversed(range(taps))]
        + [jnp.zeros((128 - taps, conv.shape[1]), f32)],
        axis=0,
    )
    by_byte = exact(emb, scored, cols_cols)
    high = by_byte.astype(bf16).astype(f32)
    middle = (by_byte - high).astype(bf16).astype(f32)
    low = by_byte - high - middle
    score_table[...] = (high + pltpu.roll(middle, 32, 1) + pltpu.roll(low, 64, 1)).astype(bf16)
    bias_score[...] = jnp.broadcast_to(
        jnp.sum(as_row(conv_bias) * score, axis=1, keepdims=True), bias_score.shape
    )


def position_inside(rows, first, total_bytes):
    lane = iota((rows, 128), 1)
    place = period * (first + iota((rows, 128), 0)) + lane - 4
    return (lane >= 4) & (lane < 4 + period) & (place < total_bytes)


def coefficient_inside(rows, first, total_bytes):
    lane = iota((rows, 128), 1)
    place = period * (first + iota((rows, 128), 0)) + lax.rem(lane, period)
    return (lane < period * pairs) & (place < total_bytes)


def laid_out(found_ids, lengths, line, first, rows):
    section, seq = (lax.axis_index("section"), lax.axis_index("seq"))
    count = found_ids[0].shape[1] // 128
    line[...] = jnp.full(line.shape, -1.0, f32)
    for k, item in enumerate(found_ids):
        for at in range(count):
            both = item[:, at * 128 : (at + 1) * 128]
            row = jnp.where(section == 1, both[1:2], both[0:1])
            line[pl.ds((seq ^ k) * count + at + 1, 1), :] = row.astype(f32)
    place = 128 * (iota(line.shape, 0) - 1) + iota(line.shape, 1)
    values = jnp.where(place < lengths[section], line[...], -1.0).astype(bf16)
    shape = (rows, line.shape[0])
    flipped = first + rows - 1 - iota(shape, 0)
    here = (period * flipped + 126) // 128
    found = [
        mm((here + step == iota(shape, 1)).astype(bf16), values) for step in range(2)
    ]
    start = lax.rem(2 - period * (first + rows - 1) + 128 * period * (rows + first), 128)
    for _ in range(period // 4):
        found = [pltpu.roll(item, 0, 1, stride=4, stride_axis=0) for item in found]
    found = [pltpu.roll(item, start, 1) for item in found]
    shape = (rows, 128)
    lane = iota(shape, 1)
    begin = lax.rem(period * (first + rows - 1 - iota(shape, 0)) + 126, 128)
    merged_rows = jnp.where(lane + begin < 128, found[0], found[1]).astype(bf16)
    flip = (iota((rows, rows), 0) + iota((rows, rows), 1) == rows - 1).astype(bf16)
    return mm(flip, merged_rows)


def fill_hot(ids, hot, vocab):
    rows = ids.shape[0]
    value = iota((rows, vocab), 1).astype(f32)
    for r in range(columns):
        found = jnp.where(ids[:, r : r + 1] == value, 1.0, 0.0).astype(bf16)
        hot[r] = found


def fill_mixing(hot, narrow, mixing, vocab):
    rows = narrow.shape[0]

    def mix(step, carry):
        own = pl.ds(pl.multiple_of(step * 16, 16), 16)
        weight = narrow[own, :]
        for j in range(pairs):
            acc = [None] * taps
            for r in reached(j):
                at = period * j + r
                column = jnp.broadcast_to(weight[:, at : at + 1], (16, vocab))
                for tap in range(taps):
                    term = hot[r + tap, own, :] * column
                    acc[tap] = term if acc[tap] is None else acc[tap] + term
            for tap in range(taps):
                mixing[j, own, tap * vocab : (tap + 1) * vocab] = acc[tap]
        return carry

    lax.fori_loop(0, rows // 16, mix, 0, unroll=True)


def gbst_kernel(total_bytes, steps, parts, lengths, *refs):
    found_ids = refs[:parts]
    table, score_table, pool, spread, total, conv_bias, bias_score = refs[parts : parts + 7]
    tokens, kept, coefficients, size_weights, ids = refs[parts + 7 : parts + 12]
    mixing, hot, natural, line, narrow = refs[parts + 12 :]
    rows = ids.shape[0]
    vocab = score_table.shape[0]
    width = table.shape[1]
    first = pl.program_id(0) * rows if steps > 1 else 0
    ids[...] = laid_out(found_ids, lengths, line, first, rows)
    fill_hot(ids, hot, vocab)
    parts = mm(hot[...].reshape(columns * rows, vocab), score_table[...])
    scores = parts[:rows]
    for r in range(1, columns):
        scores = scores + pltpu.roll(parts[r * rows : (r + 1) * rows], r, 1)
    scores = scores + pltpu.roll(scores, 96, 1) + pltpu.roll(scores, 64, 1)
    scores = jnp.where(
        position_inside(rows, first, total_bytes), scores + bias_score[0:1, :], 0.0
    )
    pooled = lanes(split_mm(scores, pool), 3)
    by_size = [scores] + [item * (1.0 / (size + 2)) for size, item in enumerate(pooled)]
    largest = functools.reduce(jnp.maximum, by_size)
    weights = [jnp.exp(item - largest) for item in by_size]
    scale = 1.0 / sum(weights)
    weights = [weight * scale for weight in weights]
    for size in range(4):
        size_weights[size] = weights[size]
    weights = [weight * (0.5 / (size + 1)) for size, weight in enumerate(weights)]
    spread_sum = split_mm(jnp.concatenate(weights, axis=1), spread)
    spread_sum = jnp.where(coefficient_inside(rows, first, total_bytes), spread_sum, 0.0)
    coefficients[...] = spread_sum
    narrow[...] = spread_sum.astype(bf16)
    row_total = split_mm(spread_sum, total)

    fill_mixing(hot, narrow, mixing, vocab)
    bias = as_row(conv_bias)
    by_phase = mm(mixing[...].reshape(pairs * rows, taps * vocab), table[...])
    for j in range(pairs):
        rows_j = by_phase[j * rows : (j + 1) * rows] + row_total[:, j : j + 1] * bias
        for at in range(width // 128):
            natural[at, pl.ds(j, rows, stride=pairs), :] = rows_j[:, at * 128 : (at + 1) * 128]
    for at in range(width // 128):
        tokens[:, at * 128 : (at + 1) * 128] = natural[at].astype(bf16)
    kept[...] = tokens[...]


def attend_kernel(
    heads,
    lengths,
    tokens,
    gain,
    query_weight,
    key_weight,
    value_weight,
    rel_bias,
    normed,
    queries,
    keys,
    values,
    probs,
    attended,
    own_tokens,
):
    seq_tokens = normed.shape[0]
    count, width = queries.shape
    head_dim = width // heads
    query_first = pl.multiple_of(lax.axis_index("seq") * count, count)
    live_tokens = lengths[lax.axis_index("section")]
    own_tokens[...] = tokens[pl.ds(query_first, count), :]
    hidden = tokens[0:seq_tokens, :].astype(f32)
    scale = lax.rsqrt(jnp.mean(hidden * hidden, axis=-1, keepdims=True) + epsilon)
    normed[...] = (hidden * scale * as_row(gain)).astype(bf16)
    keys[...] = mm(normed[...], key_weight[...], cols_cols).astype(bf16)
    values[...] = mm(normed[...], value_weight[...], cols_cols).astype(bf16)
    queries[...] = mm(
        normed[pl.ds(query_first, count), :], query_weight[...], cols_cols
    ).astype(bf16)
    span = seq_tokens + count
    hot = bucket_hot(rel_bias.shape[1], span, query_first, count)
    by_offset = mm(rel_bias[...].astype(f32), hot)
    live = 2 * iota((1, seq_tokens), 1) < live_tokens
    mixed = jnp.zeros((count, width), f32)
    for head in range(heads):
        mask = head_mask(width, head_dim, head)
        row = jnp.broadcast_to(by_offset[head : head + 1, :], (count, span))
        bias = pltpu.roll(row, span - (count - 1), 1, stride=1, stride_axis=0)[:, :seq_tokens]
        own = jnp.where(mask, queries[...], jnp.zeros((), bf16))
        scores = mm(own, keys[...], cols_cols) + bias
        scores = jnp.where(live, scores, masked_score)
        raised = jnp.exp(scores - jnp.max(scores, axis=-1, keepdims=True))
        part = (raised * (1.0 / jnp.sum(raised, axis=-1, keepdims=True))).astype(bf16)
        probs[head] = part
        mixed = jnp.where(mask, mm(part, values[...]), mixed)
    attended[...] = mixed.astype(bf16)


def gelu(value):
    inner = np.float32(np.sqrt(2 / np.pi)) * (value + 0.044715 * (value * value * value))
    return 0.5 * value * (1.0 + jnp.tanh(inner))


def gelu_both(value):
    root = np.float32(np.sqrt(2 / np.pi))
    square = value * value
    tanh = jnp.tanh(root * value * (1.0 + 0.044715 * square))
    half = 0.5 * (1.0 + tanh)
    slope = half + 0.5 * value * (1.0 - tanh * tanh) * root * (1.0 + 3 * 0.044715 * square)
    return (value * half, slope)


def feed_kernel(ways, *refs):
    attended = refs[:ways]
    out_weight = refs[ways : 2 * ways]
    tokens, gain, gate_weight, up_weight, down_weight, out_grad = refs[2 * ways : 2 * ways + 6]
    middle, normed, inner, grad_gate, grad_up = refs[2 * ways + 6 : 2 * ways + 11]
    pieces = refs[2 * ways + 11 : 3 * ways + 11]
    whole_part = refs[3 * ways + 11]
    count = middle.shape[0]
    branch = sum(mm(a[...], w[...]) for a, w in zip(attended, out_weight))
    total = tokens[...].astype(f32) + branch
    middle[...] = total
    scale = lax.rsqrt(jnp.mean(total * total, axis=-1, keepdims=True) + epsilon)
    normed[...] = (total * scale * as_row(gain)).astype(bf16)
    gate = mm(normed[...], gate_weight[...])
    upward = mm(normed[...], up_weight[...])
    grad_inner = mm(out_grad[lax.axis_index("section")], down_weight[...], cols_cols)
    active, slope = gelu_both(gate)
    inner[...] = (active * upward).astype(bf16)
    grad_gate[...] = (grad_inner * upward * slope).astype(bf16)
    grad_up[...] = (grad_inner * active).astype(bf16)
    whole_part[...] = mm(grad_gate[...], gate_weight[...], cols_cols) + mm(
        grad_up[...], up_weight[...], cols_cols
    )
    deal(whole_part, pieces)


def deal(source, pieces):
    piece = pieces[0].shape[0]
    for k, out in enumerate(pieces):
        at = pl.multiple_of((lax.axis_index("tensor") ^ k) * piece, piece)
        out[...] = source[pl.ds(at, piece), :].astype(bf16)


def collect(pieces, target):
    piece = pieces[0].shape[0]
    for k, item in enumerate(pieces):
        at = pl.multiple_of((lax.axis_index("tensor") ^ k) * piece, piece)
        target[pl.ds(at, piece), :] = item[...].astype(target.dtype)


def feed_grad_kernel(chunks, inner, normed, grad_gate, grad_up, out_grad, down_weight, *refs):
    sums, encoded = (refs[: 2 * chunks], refs[2 * chunks])
    stack = refs[2 * chunks + 1]
    first = 0
    for left, right in (
        (normed, grad_gate[...]),
        (normed, grad_up[...]),
        (inner, out_grad[lax.axis_index("section")]),
    ):
        product = mm(left[...], right, rows_rows)
        rows, columns = product.shape
        for at in range(0, columns, 256):
            stack[first : first + rows, :] = product[:, at : at + 256].astype(bf16)
            first += rows
    section = lax.axis_index("section")
    half = first // (2 * chunks)
    for chunk in range(chunks):
        for side, out in enumerate(sums[2 * chunk : 2 * chunk + 2]):
            at = (2 * chunk + (section ^ side)) * half
            out[...] = stack[pl.ds(pl.multiple_of(at, half), half), :]
    encoded[...] = mm(inner[...], down_weight[...]).astype(bf16)


def middle_kernel(ways, *refs):
    pieces = refs[:ways]
    middle, out_grad, gain, grad_branch, grad_middle, grad_gain = refs[ways:]
    piece = pieces[0].shape[0]
    at = pl.multiple_of(lax.axis_index("tensor") * piece, piece)
    grad_normed = sum(item[...].astype(f32) for item in pieces)
    own = middle[pl.ds(at, piece), :]
    scale = lax.rsqrt(jnp.mean(own * own, axis=-1, keepdims=True) + epsilon)
    grad_gain[...] = jnp.sum(grad_normed * own * scale, axis=0, keepdims=True)
    through = grad_normed * as_row(gain)
    total = (
        out_grad[lax.axis_index("section"), pl.ds(at, piece), :].astype(f32)
        + scale * through
        - own * (scale * scale * scale) * jnp.mean(through * own, axis=-1, keepdims=True)
    )
    grad_middle[...] = total
    grad_branch[...] = total.astype(bf16)


def attend_back_kernel(heads, ways, *refs):
    branches = refs[:ways]
    attended, probs, queries, keys, values, normed, out_weight = refs[ways : ways + 7]
    keep, send, rel_grad, grad_queries, grad_keys, grad_values = refs[ways + 7 : ways + 13]
    branch, stack = refs[ways + 13 :]
    count, width = queries.shape
    seq_tokens = keys.shape[0]
    head_dim = width // heads
    collect(branches, branch)
    query_first = pl.multiple_of(lax.axis_index("seq") * count, count)
    grad_attended = mm(branch[...], out_weight[...], cols_cols).astype(bf16)
    stack[3 * width :, :] = mm(attended[...], branch[...], rows_rows).astype(bf16)
    span = seq_tokens + count
    flip = (iota((count, count), 0) + iota((count, count), 1) == count - 1).astype(bf16)
    zero = jnp.zeros((), bf16)
    by_offset = []
    query_sum = jnp.zeros((count, width), f32)
    key_sum = jnp.zeros((seq_tokens, width), f32)
    value_sum = jnp.zeros((seq_tokens, width), f32)
    for head in range(heads):
        mask = head_mask(width, head_dim, head)
        own = jnp.where(mask, grad_attended, zero)
        grad_probs = mm(own, values[...], cols_cols)
        part = probs[head].astype(f32)
        inside = jnp.sum(part * grad_probs, axis=-1, keepdims=True)
        grad_scores = (part * (grad_probs - inside)).astype(bf16)
        flipped = jnp.concatenate(
            [mm(flip, grad_scores), jnp.zeros((count, count), f32)], axis=1
        )
        by_offset.append(
            jnp.sum(pltpu.roll(flipped, 0, 1, stride=1, stride_axis=0), axis=0, keepdims=True)
        )
        query_sum = jnp.where(mask, mm(grad_scores, keys[...]), query_sum)
        key_sum = key_sum + mm(
            grad_scores, jnp.where(mask, queries[...], zero), rows_rows
        )
        value_sum = value_sum + mm(probs[head], own, rows_rows)
    by_offset = jnp.concatenate(by_offset + [jnp.zeros((8 - heads, span), f32)], axis=0)
    hot = bucket_hot(128, span, query_first, count)
    rel_grad[...] = exact(by_offset, hot, cols_cols)
    query_sum = query_sum.astype(bf16)
    stack[0:width, :] = mm(
        query_sum, normed[pl.ds(query_first, count), :], rows_rows
    ).astype(bf16)
    grad_queries[...] = jnp.zeros(grad_queries.shape, bf16)
    grad_queries[pl.ds(query_first, count), :] = query_sum
    rest = grad_keys.shape[0] - seq_tokens
    for at, (total, place) in enumerate(((key_sum, grad_keys), (value_sum, grad_values))):
        total = total.astype(bf16)
        place[0:seq_tokens, :] = total
        place[seq_tokens:, :] = jnp.zeros((rest, width), bf16)
        stack[(at + 1) * width : (at + 2) * width, :] = mm(
            total, normed[...], rows_rows
        ).astype(bf16)
    half = keep.shape[0]
    section = lax.axis_index("section")
    keep[...] = stack[pl.ds(pl.multiple_of(section * half, half), half), :]
    send[...] = stack[pl.ds(pl.multiple_of((1 - section) * half, half), half), :]


def normed_back_kernel(
    steps,
    seq_tokens,
    ways,
    grad_queries,
    grad_keys,
    grad_values,
    tokens,
    query_weight,
    key_weight,
    value_weight,
    gain,
    grad_middle,
    grad_tokens,
    grad_gain,
    whole_part,
):
    token_rows, width = tokens.shape
    step = pl.program_id(0) if steps > 1 else 0
    whole_part[...] = (
        mm(grad_queries[...], query_weight[...])
        + mm(grad_keys[...], key_weight[...])
        + mm(grad_values[...], value_weight[...])
    )
    scale_row = as_row(gain)
    block = 32

    def one(part, total):
        own = pl.ds(pl.multiple_of(part * block, block), block)
        place = token_rows * step + part * block + iota((block, 1), 0)
        hidden = jnp.where(place < seq_tokens, tokens[own, :].astype(f32), 0.0)
        grad_normed = whole_part[own, :]
        scale = lax.rsqrt(jnp.mean(hidden * hidden, axis=-1, keepdims=True) + epsilon)
        against = grad_normed * hidden
        total = total + jnp.sum((against * scale).reshape(block // 8, 8, width), axis=0)
        inner = jnp.mean(against * scale_row, axis=-1, keepdims=True)
        result = scale * (grad_normed * scale_row) - hidden * (scale * scale * scale * inner)
        for at in range(width // 128):
            grad_tokens[at, own, :] = result[:, at * 128 : (at + 1) * 128]
        return total

    total = jnp.zeros((8, width), f32)
    total = lax.fori_loop(0, token_rows // block, one, total, unroll=11)
    total = jnp.sum(total, axis=0, keepdims=True)
    if steps > 1:
        total = total + jnp.where(step == 0, 0.0, grad_gain[0:1, :])
    grad_gain[0:1, :] = total
    piece = grad_middle.shape[0]
    own_first = (lax.axis_index("seq") * ways + lax.axis_index("tensor")) * piece
    own_first = own_first - token_rows * step
    for part in range(piece // block):
        begin = own_first + part * block

        @pl.when((begin >= 0) & (begin < token_rows))
        def _():
            place = pl.ds(pl.multiple_of(begin, block), block)
            rows = grad_middle[part * block : (part + 1) * block, :]
            for at in range(width // 128):
                grad_tokens[at, place, :] += rows[:, at * 128 : (at + 1) * 128]


def middle_back_kernel(heads, ways, seq_tokens, *refs):
    first, second = (refs[: ways + 7], refs[ways + 7 : ways + 13])
    keep, send, rel_grad, grad_tokens, grad_gain = refs[ways + 13 : ways + 18]
    branch, stack, grad_queries, grad_keys, grad_values, whole_part = refs[ways + 18 :]
    grads = (grad_queries, grad_keys, grad_values)
    attend_back_kernel(heads, ways, *first, keep, send, rel_grad, *grads, branch, stack)
    normed_back_kernel(
        1, seq_tokens, ways, *grads, *second, grad_tokens, grad_gain, whole_part
    )


def gbst_back_kernel(
    total_bytes,
    steps,
    grad_tokens,
    grad_gain_first,
    grad_gain_second,
    rel_grad,
    coefficients,
    size_weights,
    ids,
    pool,
    spread,
    total,
    embedding,
    conv_weight,
    conv_bias,
    score_weight,
    keep,
    send,
    hot,
    by_byte,
    by_score,
    small,
    packed,
    table,
    phased,
    against,
    found,
    mixing,
    weights,
):
    rows = ids.shape[0]
    vocab, width = embedding.shape
    step = pl.program_id(0) if steps > 1 else 0
    first = step * rows
    score = as_row(score_weight)
    bias = as_row(conv_bias)

    def at_step(wanted):
        return pl.when(step == wanted) if steps > 1 else lambda run: run()

    @at_step(0)
    def _():
        by_score[...] = jnp.zeros(by_score.shape, f32)
        small[...] = jnp.zeros(small.shape, f32)
        fill_table(embedding, conv_weight, table)

    row_total = split_mm(coefficients[...], total)
    lane = iota((rows, 128), 1)
    on_bias = []
    bias_grad = jnp.zeros((1, width), f32)
    for j in range(pairs):
        grad_rows = jnp.concatenate(
            [grad_tokens[at, pl.ds(j, rows, stride=pairs), :] for at in range(width // 128)],
            axis=1,
        )
        narrow = grad_rows.astype(bf16)
        phased[j * rows : (j + 1) * rows, :] = narrow
        bias_grad = bias_grad + jnp.sum(row_total[:, j : j + 1] * grad_rows, axis=0, keepdims=True)
        on_bias.append(jnp.sum(grad_rows * bias, axis=1, keepdims=True))
    against[...] = mm(phased[...], table[...], cols_cols)
    fill_hot(ids, hot, vocab)
    weights[...] = coefficients[...].astype(bf16)
    fill_mixing(hot, weights, mixing, vocab)
    product = mm(mixing[...].reshape(pairs * rows, taps * vocab), phased[...], rows_rows)
    if steps > 1:
        by_byte[...] = product + jnp.where(step == 0, 0.0, by_byte[...])
    else:
        by_byte[...] = product

    def pick(part, carry):
        own = pl.ds(pl.multiple_of(part * 16, 16), 16)
        spot = iota((16, 128), 1)
        result = jnp.zeros((16, 128), f32)
        for j in range(pairs):
            for r in reached(j):
                begin = pl.ds(pl.multiple_of(j * rows + part * 16, 16), 16)
                picked = sum(
                    hot[r + tap, own, :].astype(f32)
                    * against[begin, tap * vocab : (tap + 1) * vocab]
                    for tap in range(taps)
                )
                result = jnp.where(
                    spot == period * j + r, jnp.sum(picked, axis=1, keepdims=True), result
                )
        found[own, :] = result
        return carry

    lax.fori_loop(0, rows // 16, pick, 0, unroll=True)
    grad_coefficients = found[...]
    for j in range(pairs):
        grad_coefficients = grad_coefficients + jnp.where(lane // period == j, on_bias[j], 0.0)
    grad_coefficients = jnp.where(
        coefficient_inside(rows, first, total_bytes), grad_coefficients, 0.0
    )
    grad_sizes = lanes(split_mm(grad_coefficients, spread, cols_cols), 4)
    grad_sizes = [item * (0.5 / (size + 1)) for size, item in enumerate(grad_sizes)]
    mean_grad = sum(size_weights[size] * grad_sizes[size] for size in range(4))
    by_size = [size_weights[size] * (grad_sizes[size] - mean_grad) for size in range(4)]
    pooled = [item * (1.0 / (size + 2)) for size, item in enumerate(by_size[1:])]
    grad_scores = by_size[0] + split_mm(jnp.concatenate(pooled, axis=1), pool, cols_cols)
    grad_scores = jnp.where(position_inside(rows, first, total_bytes), grad_scores, 0.0)
    score_sum = jnp.sum(jnp.sum(grad_scores, axis=1, keepdims=True), axis=0, keepdims=True)
    small[1:2, :] += bias_grad + score_sum * score
    small[2:3, :] += score_sum * bias
    shifted = []
    for r in range(columns):
        item = pltpu.roll(grad_scores, 128 - r, 1) if r else grad_scores
        shifted.append(jnp.where(lane < taps, item, 0.0).astype(bf16))
    shifted = jnp.concatenate(shifted, axis=0)
    by_score[...] += mm(hot[...].reshape(columns * rows, vocab), shifted, rows_rows)

    @at_step(steps - 1)
    def _():
        emb = embedding[...].astype(f32)
        conv = conv_weight[...].astype(f32)
        grad_embedding = jnp.zeros((vocab, width), f32)
        grad_score = small[2:3, :]
        bytes_score = mm(by_score[...].astype(bf16), embedding[...], rows_rows)
        conv_rows = []
        for tap in range(taps):
            at = taps - 1 - tap
            here = by_byte[tap * vocab : (tap + 1) * vocab, :] + by_score[:, at : at + 1] * score
            grad_embedding = grad_embedding + conv[tap : tap + 1] * here
            conv_rows.append(jnp.sum(emb * here, axis=0, keepdims=True))
            grad_score = grad_score + conv[tap : tap + 1] * bytes_score[at : at + 1, :]
        rest = packed.shape[0] - vocab
        tail = conv_rows + [small[1:2, :], grad_score]
        tail += [grad_gain_first[0:1, :], grad_gain_second[0:1, :]]
        copies = jnp.concatenate([rel_grad[...]] * (width // 128), axis=1)
        own = iota(copies.shape, 1) // 128 == lax.axis_index("tensor")
        tail.append(jnp.where(own, copies, 0.0))
        used = sum(item.shape[0] for item in tail)
        tail = jnp.concatenate(tail + [jnp.zeros((rest - used, width), f32)], axis=0)
        packed[0:vocab, :] = grad_embedding.astype(bf16)
        packed[vocab:, :] = tail.astype(bf16)
        section = lax.axis_index("section")
        half = keep.shape[0]
        for side, out in enumerate((keep, send)):
            out[...] = packed[pl.ds(pl.multiple_of((section ^ side) * half, half), half), :]


def deal_kernel(keep, other, *refs):
    pieces, whole_part = (refs[:-1], refs[-1])
    whole_part[...] = keep[...].astype(f32) + other[...].astype(f32)
    deal(whole_part, pieces)


def copied_out(value):
    return [value] + [exchange(value, "tensor", k) for k in range(1, lax.axis_size("tensor"))]


def spread_out(pieces):
    return [pieces[0]] + [exchange(pieces[k], "tensor", k) for k in range(1, len(pieces))]


def seq_masks():
    return [1 << bit for bit in range(lax.axis_size("seq").bit_length() - 1)]


def merged(items):
    return sum(item.astype(f32) for item in items).astype(bf16)


def half_of(item, bit):
    half = item.shape[0] // 2
    return jnp.where(bit, item[half:], item[:half])


def even(rows):
    return rows % 32 == 0


def sum_over(items, axis, mask, halved):
    if not even(items[0].shape[0]):
        part = merged(items)
        return [part, exchange(part, axis, mask)]
    bit = (lax.axis_index(axis) & mask) != 0
    sent = merged([half_of(item, jnp.logical_not(bit)) for item in items])
    halved.append(mask)
    return [half_of(item, bit) for item in items] + [exchange(sent, axis, mask)]


class Staged:
    def __init__(self, keep, send):
        self.items = [keep, exchange(send, "section", 1)]
        self.masks = seq_masks()
        self.halved = []
        self.sent = None

    def add(self):
        mask = self.masks[0]
        rows = self.items[0].shape[0]
        if even(rows):
            bit = (lax.axis_index("seq") & mask) != 0
            self.sent = merged([half_of(item, jnp.logical_not(bit)) for item in self.items])
            self.items = [half_of(item, bit) for item in self.items]
            self.halved.append(mask)
        else:
            self.sent = merged(self.items)
            self.items = [self.sent]

    def swap(self, extra=None):
        rows = self.sent.shape[0]
        sent = self.sent if extra is None else jnp.concatenate([self.sent, extra], axis=0)
        sent = exchange(sent, "seq", self.masks.pop(0))
        self.items = self.items + [sent[:rows]]
        return sent[rows:]

    def before(self, value):
        self.sent, value = lax.optimization_barrier((self.sent, value))
        return value

    def received_before(self, value):
        self.items[-1], value = lax.optimization_barrier((self.items[-1], value))
        return value

    def finish(self):
        while self.masks:
            self.add()
            self.swap()
        return merged(self.items)


class Encoded:
    def __init__(self, rows):
        self.masks = [1 << bit for bit in range(lax.axis_size("tensor").bit_length() - 1)]
        self.items = [rows]
        self.left = list(self.masks)

    def swap(self):
        mask = self.left.pop(0)
        bit = (lax.axis_index("tensor") & mask) != 0
        blocks = 2 * len(self.left) if self.left else 1
        split = [
            item.reshape(blocks, 2, item.shape[0] // (2 * blocks), item.shape[1])
            for item in self.items
        ]
        shape = (self.items[0].shape[0] // 2, self.items[0].shape[1])
        keep = [jnp.where(bit, item[:, 1], item[:, 0]).reshape(shape) for item in split]
        sent = [jnp.where(bit, item[:, 0], item[:, 1]).reshape(shape) for item in split]
        self.items = keep + [exchange(merged(sent), "tensor", mask)]

    def gather(self):
        mask = self.masks.pop(0)
        self.pieces = [*self.pieces, exchange(jnp.concatenate(self.pieces), "tensor", mask)]


class Gather:
    def __init__(self, total, halved):
        self.pieces = {0: total}
        self.ahead = {}
        self.halved = halved
        self.masks = list(reversed(halved))
        self.arrays, self.holds = ([], [])
        self.done = []

    def swap(self, extra=None):
        mask = self.masks.pop(0)
        arrived = None
        for at in list(self.pieces):
            if at ^ mask in self.ahead:
                self.pieces[at ^ mask] = self.ahead[at ^ mask]
                continue
            sent = self.pieces[at]
            if extra is not None and arrived is None:
                sent = jnp.concatenate([sent, extra], axis=0)
            sent = exchange(sent, "seq", mask)
            if extra is not None and arrived is None:
                rows = self.pieces[at].shape[0]
                arrived, sent = (sent[rows:], sent[:rows])
            self.pieces[at ^ mask] = sent
        return arrived

    def early(self):
        for mask in self.masks:
            self.ahead[mask] = exchange(self.pieces[0], "seq", mask)

    def finish(self):
        while self.masks:
            self.swap()

    def across(self):
        names = [at for at in self.pieces if at not in self.done]
        self.done += names
        array = jnp.concatenate([self.pieces[at] for at in names], axis=0)
        self.arrays += [array, exchange(array, "section", 1)]
        self.holds += [(0, names), (1, names)]
        return self.arrays[-1]


def place_of(halved, at, rows, index):
    first = 0
    size = rows
    for mask in halved:
        size = size // 2
        first = first + jnp.where(((index ^ at) & mask) != 0, size, 0)
    return first


def unstack(arrays, halved, holds, stack):
    section, seq = (lax.axis_index("section"), lax.axis_index("seq"))
    half = stack.shape[0] // 2
    for array, (side, names) in zip(arrays, holds):
        rows = array.shape[0] // len(names)
        for i, name in enumerate(names):
            first = place_of(halved, name, half, seq) + (section ^ side) * half
            part = array[i * rows : (i + 1) * rows, :].astype(f32)
            stack[pl.ds(pl.multiple_of(first, 8), rows), :] = part


def weights_kernel(halved, holds, *refs):
    count = len(holds)
    outs, stack = (refs[count:-1], refs[-1])
    unstack(refs[:count], halved, holds, stack)
    rows = outs[0].shape[0]
    for i, out in enumerate(outs):
        out[...] = stack[i * rows : (i + 1) * rows, :]


def feed_weights_kernel(halved, holds, *refs):
    count = len(holds)
    outs, stack = (refs[count:-1], refs[-1])
    unstack(refs[:count], halved, holds, stack)
    first = 0
    for out in outs:
        rows, columns = out.shape
        for at in range(0, columns, 256):
            out[:, at : at + 256] = stack[first : first + rows, :]
            first += rows


def packed_kernel(ways, heads, *refs):
    pieces, others = (refs[:ways], refs[ways])
    embedding, conv, bias, score, first, second, rel, stack = refs[ways + 1 :]
    rows = pieces[0].shape[0]
    vocab, width = embedding.shape
    section, tensor = (lax.axis_index("section"), lax.axis_index("tensor"))
    for k, item in enumerate(pieces):
        other = others[k * rows : (k + 1) * rows, :]
        for side, rows_k in enumerate((item[...], other)):
            at = ((section ^ side) * ways + (tensor ^ k)) * rows
            stack[pl.ds(pl.multiple_of(at, rows), rows), :] = rows_k.astype(f32)
    embedding[...] = stack[0:vocab, :]
    conv[...] = stack[vocab : vocab + taps, :]
    for i, out in enumerate((bias, score, first, second)):
        out[...] = stack[vocab + taps + i : vocab + taps + i + 1, :].reshape(width)
    at = vocab + taps + 4
    own = stack[at : at + heads, pl.ds(pl.multiple_of(tensor * 128, 128), 128)]
    rel[...] = own[:, : rel.shape[1]]


def encoded_kernel(*refs):
    pieces, middle, out = (refs[:-2], refs[-2], refs[-1])
    piece = out.shape[0]
    at = pl.multiple_of(lax.axis_index("tensor") * piece, piece)
    total = sum(item[...].astype(f32) for item in pieces)
    out[...] = (middle[pl.ds(at, piece), :] + total).astype(bf16)


def assemble_kernel(*refs):
    pieces, out = (refs[:-1], refs[-1])
    rows = pieces[0].shape[0]
    at = 0
    for item in pieces:
        for part in range(item.shape[0] // rows):
            first = pl.multiple_of((lax.axis_index("tensor") ^ at) * rows, rows)
            out[pl.ds(first, rows), :] = item[part * rows : (part + 1) * rows, :]
            at += 1


def exchange(value, axis, mask):
    size = lax.axis_size(axis)
    return lax.ppermute(value, axis, [(i, i ^ mask) for i in range(size)])


def shards(
    byte_ids,
    byte_lengths,
    embedding,
    conv_weight,
    conv_bias,
    score_weight,
    norm_first,
    query_weight,
    key_weight,
    value_weight,
    out_weight,
    rel_bias,
    norm_second,
    gate_weight,
    up_weight,
    down_weight,
    out_grad,
):
    group = byte_ids.shape[1]
    ways = lax.axis_size("tensor")
    total_bytes = group * lax.axis_size("seq")
    count = group // 2
    seq_tokens = total_bytes // 2
    heads = rel_bias.shape[1]
    width = query_weight.shape[1]
    vocab, model = embedding.shape
    units = gate_weight.shape[1]
    piece = count // ways
    query_weight, key_weight, value_weight, rel_bias = (
        item.T for item in (query_weight, key_weight, value_weight, rel_bias)
    )
    steps = -(-total_bytes // (period * chunk_rows))
    rows = steps * chunk_rows
    token_rows = rows * pairs
    chunk_tokens = chunk_rows * pairs

    near = seq_tokens <= 1024
    held = pltpu.VMEM if near else like
    far = pltpu.HBM if near else like
    place = functools.partial(call, near=near)
    table, score_table, bias_score = place(
        prepare_kernel,
        [held((taps * vocab, model), bf16), held((vocab, 128), bf16), held((8, 128), f32)],
        embedding,
        conv_weight,
        score_weight,
        conv_bias,
        specs=[distant] * 4,
        cost=2,
    )

    all_ids = [byte_ids] + [
        exchange(byte_ids, "seq", k) for k in range(1, lax.axis_size("seq"))
    ]
    score_table, out_weight = lax.optimization_barrier((score_table, out_weight))
    out_weights = copied_out(out_weight)

    pool, spread, total = (jnp.asarray(item, bf16) for item in pool_tables())
    def chunked(item, dims):
        if steps == 1:
            return distant
        at = next(i for i, (a, b) in enumerate(zip(item.shape, dims)) if a != b)
        return pl.BlockSpec(dims, lambda i: tuple(i if d == at else 0 for d in range(len(dims))))

    def chunks(item):
        dims = tuple(
            chunk_rows if d == rows else chunk_tokens if d == token_rows else d
            for d in item.shape
        )
        return chunked(item, dims)

    grid = None if steps == 1 else (steps,)
    gbst_out = [
        held((token_rows, model), bf16),
        far((token_rows, model), bf16),
        far((rows, 128), f32),
        far((4, rows, 128), f32),
        far((rows, 128), f32),
    ]
    near_tokens, tokens, coefficients, size_weights, ids = place(
        functools.partial(gbst_kernel, total_bytes, steps, len(all_ids)),
        gbst_out,
        byte_lengths,
        *all_ids,
        table,
        score_table,
        pool,
        spread,
        total,
        conv_bias,
        bias_score,
        specs=[scalars, distant]
        + [local] * (len(all_ids) + 1)
        + [distant] * 4
        + [local],
        out_specs=[chunks(item) for item in gbst_out],
        scratch=[
            pltpu.VMEM((pairs, chunk_rows, taps * vocab), bf16),
            pltpu.VMEM((columns, chunk_rows, vocab), bf16),
            pltpu.VMEM((model // 128, chunk_tokens, 128), f32),
            pltpu.VMEM((8 * -(-(total_bytes // 128 + 4) // 8), 128), f32),
            pltpu.VMEM((chunk_rows, 128), bf16),
        ],
        grid=grid,
        cost=6,
    )

    normed, queries, keys, values, probs, attended, own_tokens = place(
        functools.partial(attend_kernel, heads),
        [
            far((seq_tokens, model), bf16),
            far((count, width), bf16),
            far((seq_tokens, width), bf16),
            far((seq_tokens, width), bf16),
            far((heads, count, seq_tokens), bf16),
            held((count, width), bf16),
            held((count, model), bf16),
        ],
        byte_lengths,
        near_tokens,
        norm_first,
        query_weight,
        key_weight,
        value_weight,
        rel_bias,
        specs=[scalars, local] + [whole] * 5,
        cost=4,
    )
    attended, *out_weights = lax.optimization_barrier((attended, *out_weights))
    all_attended = copied_out(attended)

    middle, normed_second, inner, grad_gate, grad_up, *normed_parts = place(
        functools.partial(feed_kernel, ways),
        [
            held((count, model), f32),
            held((count, model), bf16),
            held((count, units), bf16),
            held((count, units), bf16),
            held((count, units), bf16),
        ]
        + [held((piece, model), bf16)] * ways,
        *all_attended,
        *out_weights,
        own_tokens,
        norm_second,
        gate_weight,
        up_weight,
        down_weight,
        out_grad,
        specs=[local] * ways + [distant] * ways + [local, distant] + [whole] * 4,
        cost=3,
        scratch=[pltpu.VMEM((count, model), f32)],
    )
    normed_parts = spread_out(normed_parts)
    feed_rows = 3 * model * units // 256
    half = feed_rows // (2 * feed_chunks)
    feed_parts = place(
        functools.partial(feed_grad_kernel, feed_chunks),
        [held((half, 256), bf16)] * (2 * feed_chunks) + [far((count, model), bf16)],
        inner,
        normed_second,
        grad_gate,
        grad_up,
        out_grad,
        down_weight,
        specs=[local] * 4 + [whole] * 2,
        cost=2,
        scratch=[pltpu.VMEM((feed_rows, 256), bf16)],
    )
    feed_parts, encoded = (feed_parts[: 2 * feed_chunks], feed_parts[2 * feed_chunks])
    feed_sums = [Staged(*feed_parts[2 * i : 2 * i + 2]) for i in range(feed_chunks)]

    feed = feed_sums[0]
    feed.add()
    normed_parts[0] = feed.before(normed_parts[0])
    feed.swap()
    grad_branch, grad_middle, grad_gain_second = place(
        functools.partial(middle_kernel, ways),
        [held((piece, model), bf16), far((piece, model), f32), far((1, model), f32)],
        *normed_parts,
        middle,
        out_grad,
        norm_second,
        specs=[local] * (ways + 1) + [whole, distant],
    )
    branches = copied_out(grad_branch)
    branches[0] = feed.received_before(branches[0])
    feed.add()
    branches[0] = feed.before(branches[0])
    feed.swap()
    stack_rows = 4 * width
    first = (*branches, attended, probs, queries, keys, values, normed, out_weight)
    second = (tokens, query_weight, key_weight, value_weight, norm_first, grad_middle)
    weights_out = [held((stack_rows // 2, model), bf16)] * 2 + [far((8, 128), f32)]
    grads_out = [far((token_rows, width), bf16)] * 3
    grad_tokens_out = [held((model // 128, token_rows, 128), f32), held((8, model), f32)]
    per_tile = pl.BlockSpec((model // 128, chunk_tokens, 128), lambda i: (0, i, 0))
    scratch = [pltpu.VMEM((count, model), bf16), pltpu.VMEM((stack_rows, model), bf16)]
    whole_part = pltpu.VMEM((chunk_tokens, model), f32)
    first_specs = [local] * ways + [distant] * 7
    if steps == 1:
        weight_keep, weight_send, grad_rel, grad_tokens, grad_gain_first = place(
            functools.partial(middle_back_kernel, heads, ways, seq_tokens),
            weights_out + grad_tokens_out,
            *first,
            *second,
            specs=first_specs + [whole] * 6,
            scratch=scratch + [pltpu.VMEM((token_rows, width), bf16)] * 3 + [whole_part],
            limit=30,
            cost=10,
        )
    else:
        weight_keep, weight_send, grad_rel, *grads = place(
            functools.partial(attend_back_kernel, heads, ways),
            weights_out + grads_out,
            *first,
            specs=first_specs,
            scratch=scratch,
        )
        grad_tokens, grad_gain_first = place(
            functools.partial(normed_back_kernel, steps, seq_tokens, ways),
            grad_tokens_out,
            *grads,
            *second,
            specs=[chunks(item) for item in (*grads, tokens)] + [distant] * 5,
            out_specs=[per_tile, whole],
            scratch=[whole_part],
            grid=grid,
        )
    grad_tokens, weight_send, feed.items, encoded = lax.optimization_barrier(
        (grad_tokens, weight_send, feed.items, encoded)
    )
    branch = Encoded(encoded)
    feed_gather = Gather(feed.finish(), feed.halved)
    feed_gather.pieces[0], grad_tokens = lax.optimization_barrier(
        (feed_gather.pieces[0], grad_tokens)
    )
    feed_gather.swap()
    weight_sum = Staged(weight_keep, weight_send)
    weight_sum.add()
    grad_tokens = weight_sum.before(grad_tokens)
    weight_sum.swap()
    branch.swap()
    packed_rows = 32 * ways * -(-(vocab + taps + 12) // (32 * ways))
    quarter = packed_rows // (2 * ways)
    keep, send = place(
        functools.partial(gbst_back_kernel, total_bytes, steps),
        [held((packed_rows // 2, model), bf16)] * 2,
        grad_tokens,
        grad_gain_first,
        grad_gain_second,
        grad_rel,
        coefficients,
        size_weights,
        ids,
        pool,
        spread,
        total,
        embedding,
        conv_weight,
        conv_bias,
        score_weight,
        specs=[local if steps == 1 else per_tile, local if steps == 1 else whole]
        + [distant] * 2
        + [chunks(item) for item in (coefficients, size_weights, ids)]
        + [distant] * 7,
        scratch=[
            pltpu.VMEM((columns, chunk_rows, vocab), bf16),
            pltpu.VMEM((taps * vocab, model), f32),
            pltpu.VMEM((vocab, 128), f32),
            pltpu.VMEM((8, model), f32),
            pltpu.VMEM((packed_rows, model), bf16),
            pltpu.VMEM((taps * vocab, model), bf16),
            pltpu.VMEM((chunk_tokens, model), bf16),
            pltpu.VMEM((chunk_tokens, taps * vocab), f32),
            pltpu.VMEM((chunk_rows, 128), f32),
            pltpu.VMEM((pairs, chunk_rows, taps * vocab), bf16),
            pltpu.VMEM((chunk_rows, 128), bf16),
        ],
        grid=grid,
        limit=30,
        cost=12,
    )
    together = lax.optimization_barrier
    keep, send, feed_gather.pieces, weight_sum.items, branch.items = together(
        (keep, send, feed_gather.pieces, weight_sum.items, branch.items)
    )
    other = exchange(send, "section", 1)
    branch.swap()
    feed_gather.early()
    parts = place(
        deal_kernel,
        [held((quarter, model), bf16)] * ways,
        keep,
        other,
        specs=[local] * 2,
        scratch=[pltpu.VMEM((packed_rows // 2, model), f32)],
    )
    part = merged(spread_out(parts))
    weight_sum.add()
    part, branch.items, weight_sum.sent, weight_sum.items = together(
        (part, branch.items, weight_sum.sent, weight_sum.items)
    )
    masks = seq_masks()
    items = [part, exchange(part, "seq", masks[0])]
    weight_sum.swap()
    (own_encoded,) = place(
        encoded_kernel,
        [held((piece, model), bf16)],
        *branch.items,
        middle,
        specs=[local] * (len(branch.items) + 1),
    )
    branch.pieces = [own_encoded]
    branch.gather()
    items, branch.pieces, feed_gather.pieces, feed_gather.ahead = together(
        (items, branch.pieces, feed_gather.pieces, feed_gather.ahead)
    )
    for mask in masks[1:]:
        part = merged(items)
        items = [part, exchange(part, "seq", mask)]
    feed_gather.finish()
    while branch.masks:
        branch.gather()
    items, weight_sum.items, feed_gather.pieces, branch.pieces = together(
        (items, weight_sum.items, feed_gather.pieces, branch.pieces)
    )
    weight_gather = Gather(weight_sum.finish(), weight_sum.halved)
    weight_gather.swap()
    weight_gather.early()
    part = merged(items)
    gathered = copied_out(part)
    feed_gather.across()
    weight_gather.pieces = together((weight_gather.pieces, gathered))[0]
    gathered = [*gathered, exchange(jnp.concatenate(gathered, axis=0), "section", 1)]
    (output,) = place(
        assemble_kernel,
        [like((count, model), bf16)],
        *branch.pieces,
        specs=[local] * len(branch.pieces),
    )
    feed_grads = place(
        functools.partial(feed_weights_kernel, feed_gather.halved, feed_gather.holds),
        [like((model, units), f32), like((model, units), f32), like((units, model), f32)],
        *feed_gather.arrays,
        specs=[local] * len(feed_gather.arrays),
        scratch=[pltpu.VMEM((feed_rows, 256), f32)],
    )
    weight_gather.finish()
    weight_gather.pieces, feed_grads, output = together(
        (weight_gather.pieces, feed_grads, output)
    )
    weight_gather.across()
    grads = place(
        functools.partial(packed_kernel, ways, heads),
        [like((vocab, model), f32), like((taps, model), f32)]
        + [like((model,), f32)] * 4
        + [like((heads, rel_bias.shape[1]), f32)],
        *gathered,
        specs=[local] * len(gathered),
        scratch=[pltpu.VMEM((packed_rows, model), f32)],
    )

    weight_gather.arrays, grads, output, feed_grads = together(
        (weight_gather.arrays, grads, output, feed_grads)
    )
    weight_grads = place(
        functools.partial(weights_kernel, weight_gather.halved, weight_gather.holds),
        [like((width, model), f32)] * 4,
        *weight_gather.arrays,
        specs=[local] * len(weight_gather.arrays),
        scratch=[pltpu.VMEM((stack_rows, model), f32)],
    )
    grad_embedding, grad_conv, grad_bias, grad_score, grad_first, grad_second, grad_rel = grads
    return (
        output[None],
        grad_embedding,
        grad_conv,
        grad_bias,
        grad_score,
        grad_first,
        *(item.T for item in weight_grads[:3]),
        weight_grads[3],
        grad_rel.T,
        grad_second,
        *feed_grads,
    )


def solution(mesh):
    return jax.shard_map(
        shards,
        mesh=mesh,
        in_specs=(
            P(None, "seq"),
            P(),
            P(),
            P(),
            P(),
            P(),
            P(),
            P(None, "tensor"),
            P(None, "tensor"),
            P(None, "tensor"),
            P("tensor", None),
            P(None, "tensor"),
            P(),
            P(None, "tensor"),
            P(None, "tensor"),
            P("tensor", None),
            P(None, "seq", None),
        ),
        out_specs=(
            P("section", "seq", None),
            P(),
            P(),
            P(),
            P(),
            P(),
            P(None, "tensor"),
            P(None, "tensor"),
            P(None, "tensor"),
            P("tensor", None),
            P(None, "tensor"),
            P(),
            P(None, "tensor"),
            P(None, "tensor"),
            P("tensor", None),
        ),
        check_vma=False,
    )
```
